32 devices in a mesh: dp: 32 (over z, y, x, core).
Axes of the slice: x: 2, y: 2, z: 4, core: 2. Of those that a mesh axis runs over, the one named last changes fastest.
Arguments:
- inputs: bfloat16 [130560, 256], P('dp'), may hold values from -6 to 6
- frames: int32 [128, 4], P('dp'), may hold values from 1 to 20, 60 in all within a row
- cotangent: float32 [130560, 256], P('dp'), may hold values from -28 to 28
- proj_in: float32 [256, 768], replicated, may hold values from -0.375 to 0.375
- proj_out: float32 [256, 256], replicated, may hold values from -2 to 2
- ffn_up: float32 [256, 1024], replicated, may hold values from -0.375 to 0.375
- ffn_down: float32 [1024, 256], replicated, may hold values from -0.1875 to 0.1875
- vectors: float32 [8, 256], replicated, may hold values from -1 to 2
- ffn_bias: float32 [1024], replicated, may hold values from -1.2 to 1.2
- first_in: float32 [196608], P('dp'), may hold values from -433.59705 to 433.59705
- second_in: float32 [196608], P('dp'), may hold values from 0 to 130560, as said below
- first_out: float32 [65536], P('dp'), may hold values from -433.59705 to 433.59705
- second_out: float32 [65536], P('dp'), may hold values from 0 to 130560, as said below
- first_up: float32 [262144], P('dp'), may hold values from -1011.72645 to 1011.72645
- second_up: float32 [262144], P('dp'), may hold values from 0 to 652800, as said below
- first_down: float32 [262144], P('dp'), may hold values from -1156.2588 to 1156.2588
- second_down: float32 [262144], P('dp'), may hold values from 0 to 913920, as said below
- first_vec: float32 [8, 256], replicated, may hold values from -1156.2588 to 1156.2588
- second_vec: float32 [8, 256], replicated, may hold values from 0 to 913920, as said below
- first_bias: float32 [1024], replicated, may hold values from -1011.72645 to 1011.72645
- second_bias: float32 [1024], replicated, may hold values from 0 to 652800, as said below
Outputs:
- block_out: bfloat16 [130560, 256], P('dp')
- grad_inputs: float32 [130560, 256], P('dp')
- grad_in: float32 [196608], P('dp')
- grad_out: float32 [65536], P('dp')
- grad_up: float32 [262144], P('dp')
- grad_down: float32 [262144], P('dp')
- grad_vec: float32 [8, 256], replicated
- grad_bias: float32 [1024], replicated
- momentum_in: float32 [196608], P('dp')
- variance_in: float32 [196608], P('dp')
- weight_in: float32 [256, 768], replicated
- copy_in: bfloat16 [256, 768], replicated
- momentum_out: float32 [65536], P('dp')
- variance_out: float32 [65536], P('dp')
- weight_out: float32 [256, 256], replicated
- copy_out: bfloat16 [256, 256], replicated
- momentum_up: float32 [262144], P('dp')
- variance_up: float32 [262144], P('dp')
- weight_up: float32 [256, 1024], replicated
- copy_up: bfloat16 [256, 1024], replicated
- momentum_down: float32 [262144], P('dp')
- variance_down: float32 [262144], P('dp')
- weight_down: float32 [1024, 256], replicated
- copy_down: bfloat16 [1024, 256], replicated
- momentum_vec: float32 [8, 256], replicated
- variance_vec: float32 [8, 256], replicated
- weight_vec: float32 [8, 256], replicated
- momentum_bias: float32 [1024], replicated
- variance_bias: float32 [1024], replicated
- weight_bias: float32 [1024], replicated
- norms: float32 [4, 2], replicated
The draws below stay inside these ranges and needn't reach their ends.
Inputs may be any that keep to these rules, and one draw needn't show every extreme that they name: Row m gives in order the frames of the 4 sequences packed into micro-batch m, micro-batches in the order of the tokens; each row sums to 60 and its largest entry is 20. `second_in`: positive. `second_out`: positive. `second_up`: positive. `second_down`: positive. `second_vec`: positive. `second_bias`: positive.
All inputs are finite; a program needn't handle non-finite values.
Results may differ from the reference program's by a relative error of at most 0.007.
The reference program's roundings to bfloat16 on the way count: a program that leaves them out, or rounds other values in their place, can miss the bound.
Values sent between devices are 32-bit elements; how exact they have to be, the bound alone decides.
A program may use at most 192 MiB of HBM per device.

```python
import math
import jax
import jax.numpy as jnp
import numpy as np
from jax import lax

D = 256
HEADS = 4
HEAD_DIM = 64
FF = 1024
FRAME = 17
SEQ_FRAMES = 20
FRAMES_MB = 60
SEQS_MB = 4
MICRO = 4
STEP = 10
TOK_MB = 1020
TOKENS = 130560
N_DP = 32


def second_moment(key, count, scale, top):
    position = jnp.arange(count, dtype=jnp.float32) / (count - 1)
    jitter = jnp.exp(jax.random.uniform(key, (count,), jnp.float32, -0.6931472, 0.6931472))
    return scale * scale * (top - (top - 1.0) * position) * jitter


def grad_scale(factor):
    return factor * jnp.sqrt(jnp.float32(TOKENS))


def draw_cotangent(key, part):
    key = jax.random.fold_in(key, 1)
    base = jax.random.truncated_normal(key, -4.0, 4.0, (TOKENS, D), jnp.float32)
    rise = 2.0
    row = jnp.arange(TOKENS, dtype=jnp.float32)[:, None] / (TOKENS - 1)
    column = jnp.arange(D, dtype=jnp.float32)[None, :] / (D - 1)
    return base * (1.0 + rise * row) * (0.6 + 0.8 * column)


def draw_vectors(key, part):
    key = jax.random.fold_in(key, 2)
    key_gain, key_shift = jax.random.split(key)
    gains = jnp.exp(jax.random.uniform(key_gain, (8, D), jnp.float32, -0.6931472, 0.6931472))
    shifts = 0.3 * jax.random.truncated_normal(key_shift, -3.0, 3.0, (8, D), jnp.float32)
    rows = jnp.arange(8, dtype=jnp.int32)[:, None]
    return jnp.where((rows == 3) | (rows == 5), gains, shifts)


def draw_first_in(key, part):
    key = jax.random.fold_in(key, 11)
    noise = jax.random.truncated_normal(key, -4.0, 4.0, (3 * D * D,), jnp.float32)
    return noise * grad_scale(0.3)


def draw_second_in(key, part):
    key = jax.random.fold_in(key, 12)
    top = 4.0
    return second_moment(key, 3 * D * D, grad_scale(0.3), top)


def draw_first_out(key, part):
    key = jax.random.fold_in(key, 13)
    noise = jax.random.truncated_normal(key, -4.0, 4.0, (D * D,), jnp.float32)
    return noise * grad_scale(0.3)


def draw_second_out(key, part):
    key = jax.random.fold_in(key, 14)
    top = 4.0
    return second_moment(key, D * D, grad_scale(0.3), top)


def draw_first_up(key, part):
    key = jax.random.fold_in(key, 15)
    noise = jax.random.truncated_normal(key, -4.0, 4.0, (D * FF,), jnp.float32)
    return noise * grad_scale(0.7)


def draw_second_up(key, part):
    key = jax.random.fold_in(key, 16)
    top = 4.0
    return second_moment(key, D * FF, grad_scale(0.7), top)


def draw_first_down(key, part):
    key = jax.random.fold_in(key, 17)
    noise = jax.random.truncated_normal(key, -4.0, 4.0, (FF * D,), jnp.float32)
    return noise * grad_scale(0.8)


def draw_second_down(key, part):
    key = jax.random.fold_in(key, 18)
    top = 4.0
    return second_moment(key, FF * D, grad_scale(0.8), top)


def draw_first_vec(key, part):
    key = jax.random.fold_in(key, 19)
    noise = jax.random.truncated_normal(key, -4.0, 4.0, (8, D), jnp.float32)
    return noise * grad_scale(0.8)


def draw_second_vec(key, part):
    key = jax.random.fold_in(key, 20)
    top = 4.0
    return second_moment(key, 8 * D, grad_scale(0.8), top).reshape(8, D)


def draw_first_bias(key, part):
    key = jax.random.fold_in(key, 21)
    noise = jax.random.truncated_normal(key, -4.0, 4.0, (FF,), jnp.float32)
    return noise * grad_scale(0.7)


def draw_second_bias(key, part):
    key = jax.random.fold_in(key, 22)
    top = 4.0
    return second_moment(key, FF, grad_scale(0.7), top)


def steps_of(key, dims, pieces, least, top_value):
    level = 1.0
    for axis_at, shards_of in pieces:
        draws = jax.random.uniform(jax.random.fold_in(jax.random.fold_in(key, 6), axis_at), (shards_of,), jnp.float32, least / len(pieces), top_value / len(pieces))
        level = level * jnp.repeat(jnp.exp(draws), dims[axis_at] // shards_of).reshape((-1,) + (1,) * (len(dims) - 1 - axis_at))
    return level


def length_profile(amount, total, most, skew):
    weights = [(1 << 20) // math.isqrt(grade ** skew) + 1 for grade in range(2, amount + 1)]
    spare, given = total - most - (amount - 1), [1] * (amount - 1)
    while spare > 0:
        movable = [i for i in range(amount - 1) if given[i] < most]
        pool, remaining = sum([weights[i] for i in movable]), spare
        for i in movable:
            extra = min(most - given[i], max(1, remaining * weights[i] // pool), spare)
            given[i] = given[i] + extra
            spare = spare - extra
    return np.array([most] + given)


def uneven(stream_key, amount, total, reach, lean):
    if amount == 2:
        one = jax.random.randint(stream_key, (), max(1, total - reach), min(reach, total - 1) + 1)
        return jnp.stack([one, total - one])
    lengths = jnp.asarray(length_profile(amount, total, reach, lean), jnp.int32)
    couples = (amount - 1) // 2
    donor, receiver = lengths[1:1 + 2 * couples:2], lengths[2:2 + 2 * couples:2]
    room = jnp.minimum(donor - 1, reach - receiver)
    moved = jax.random.randint(jax.random.fold_in(stream_key, 1), (couples,), 0, 1 << 20) % (room + 1)
    lengths = lengths.at[1:1 + 2 * couples:2].set(donor - moved).at[2:2 + 2 * couples:2].set(receiver + moved)
    return lengths[jax.random.permutation(jax.random.fold_in(stream_key, 2), amount)]


def bell_draw(stream_key, dims, width, most, cuts=(), kind=jnp.bfloat16):
    loudness = steps_of(stream_key, dims, cuts, -0.22, 0.18) if cuts else 1.0
    array = jax.random.normal(stream_key, dims, jnp.float32) * width * loudness
    return jnp.minimum(jnp.maximum(array, -most), most).astype(kind)


def setup_inputs(seed: int = 0) -> dict:
    key_of = jax.random.split(jax.random.key(seed), 22)
    inputs = bell_draw(key_of[0], (TOKENS, D), 1.0, 6.0, ((0, 32),))
    frames = jax.vmap(lambda own: uneven(own, SEQS_MB, FRAMES_MB, SEQ_FRAMES, 0))(jax.random.split(key_of[1], (N_DP * MICRO))).reshape((N_DP * MICRO, SEQS_MB)).astype(jnp.int32)
    cotangent = draw_cotangent(jax.random.fold_in(key_of[21], 71), 0)
    proj_in = bell_draw(key_of[3], (D, 3 * D), D ** -0.5, 0.375, (), jnp.float32)
    proj_out = bell_draw(key_of[4], (D, D), (D // 32) ** -0.5, 2.0, (), jnp.float32)
    ffn_up = bell_draw(key_of[5], (D, FF), D ** -0.5, 0.375, (), jnp.float32)
    ffn_down = bell_draw(key_of[6], (FF, D), FF ** -0.5, 0.1875, (), jnp.float32)
    vectors = draw_vectors(jax.random.fold_in(key_of[21], 71), 0)
    ffn_bias = bell_draw(key_of[8], (FF,), 0.3, 1.2, (), jnp.float32)
    first_in = draw_first_in(jax.random.fold_in(key_of[21], 71), 0)
    second_in = draw_second_in(jax.random.fold_in(key_of[21], 71), 0)
    first_out = draw_first_out(jax.random.fold_in(key_of[21], 71), 0)
    second_out = draw_second_out(jax.random.fold_in(key_of[21], 71), 0)
    first_up = draw_first_up(jax.random.fold_in(key_of[21], 71), 0)
    second_up = draw_second_up(jax.random.fold_in(key_of[21], 71), 0)
    first_down = draw_first_down(jax.random.fold_in(key_of[21], 71), 0)
    second_down = draw_second_down(jax.random.fold_in(key_of[21], 71), 0)
    first_vec = draw_first_vec(jax.random.fold_in(key_of[21], 71), 0)
    second_vec = draw_second_vec(jax.random.fold_in(key_of[21], 71), 0)
    first_bias = draw_first_bias(jax.random.fold_in(key_of[21], 71), 0)
    second_bias = draw_second_bias(jax.random.fold_in(key_of[21], 71), 0)
    return dict(inputs=inputs, frames=frames, cotangent=cotangent, proj_in=proj_in, proj_out=proj_out, ffn_up=ffn_up, ffn_down=ffn_down, vectors=vectors, ffn_bias=ffn_bias, first_in=first_in, second_in=second_in, first_out=first_out, second_out=second_out, first_up=first_up, second_up=second_up, first_down=first_down, second_down=second_down, first_vec=first_vec, second_vec=second_vec, first_bias=first_bias, second_bias=second_bias)


@jax.custom_vjp
def low(v):
    return lax.optimization_barrier(v.astype(jnp.bfloat16)).astype(jnp.float32)

@jax.custom_vjp
def low_back(v):
    return v

def low_keep(v):
    return (low(v), None)

def low_pass(kept, grad):
    return (grad,)

def back_keep(v):
    return (v, None)

def back_low(kept, grad):
    return (low(grad),)
low.defvjp(low_keep, low_pass)
low_back.defvjp(back_keep, back_low)
EPS_NORM = 1e-05
EPS_ADAM = 1e-06
BETA = 0.5
DECAY = 0.01
RATE = 0.5
RATE_VEC = 0.2

def hi_dot(left, right):
    return jnp.dot(left, right, precision=lax.Precision.HIGHEST, preferred_element_type=jnp.float32)

def layer_norm(values, gain, shift):
    center = values - lax.optimization_barrier(jnp.mean(values, axis=-1, keepdims=True))
    spread = lax.optimization_barrier(jnp.mean(center * center, axis=-1, keepdims=True))
    return center * lax.rsqrt(spread + EPS_NORM) * gain + shift

def allowed(counts, length):
    ends = jnp.cumsum(counts.astype(jnp.int32))
    frame = jnp.arange(length, dtype=jnp.int32) // FRAME
    owner = lax.optimization_barrier(jnp.sum((frame[:, None] >= ends[None, :]).astype(jnp.int32), axis=1))
    return (owner[:, None] == owner[None, :]) & (frame[:, None] >= frame[None, :])

def forward(params, values, mask):
    proj_in, proj_out, ffn_up, ffn_down, vectors, ffn_bias = params
    length = values.shape[0]
    scale = 1.0 / math.sqrt(HEAD_DIM)
    h_one = low(layer_norm(values, vectors[3], vectors[4]))
    joined = hi_dot(h_one, low(proj_in))
    joined = joined + jnp.concatenate([vectors[0], jnp.zeros_like(vectors[0]), vectors[1]])
    joined = low(low_back(joined))
    query = joined[:, :D].reshape(length, HEADS, HEAD_DIM)
    keys = joined[:, D:2 * D].reshape(length, HEADS, HEAD_DIM)
    vals = joined[:, 2 * D:].reshape(length, HEADS, HEAD_DIM)
    score = jnp.einsum('qhd,khd->hqk', query, keys, precision=lax.Precision.HIGHEST) * scale
    score = low_back(score)
    score = jnp.where(mask[None], score, -1e+30)
    peak = lax.optimization_barrier(jnp.max(score, axis=-1, keepdims=True))
    weight = jnp.exp(score - peak)
    prob = weight / lax.optimization_barrier(jnp.sum(weight, axis=-1, keepdims=True))
    mixed = jnp.einsum('hqk,khd->qhd', low(prob), vals, precision=lax.Precision.HIGHEST).reshape(length, D)
    mixed = low(low_back(mixed))
    branch = low_back(hi_dot(mixed, low(proj_out)) + vectors[2])
    resid = values + branch
    h_two = low(layer_norm(resid, vectors[5], vectors[6]))
    pre = low_back(hi_dot(h_two, low(ffn_up)) + ffn_bias)
    hidden = low(jax.nn.gelu(pre, approximate=False))
    feed = low_back(hi_dot(hidden, low(ffn_down)) + vectors[7])
    return resid + feed

def lamb(weight, grad, first, second, fix):
    flat_g = grad.reshape(-1)
    flat_w = weight.reshape(-1)
    momentum = BETA * first + (1.0 - BETA) * flat_g
    variance = BETA * second + (1.0 - BETA) * flat_g * flat_g
    advance = momentum / fix / (jnp.sqrt(variance / fix) + EPS_ADAM) + DECAY * flat_w
    w_norm = jnp.sqrt(jnp.sum(flat_w * flat_w))
    u_norm = jnp.sqrt(jnp.sum(advance * advance))
    fresh = (flat_w - RATE * (w_norm / (u_norm + EPS_ADAM)) * advance).reshape(weight.shape)
    return (momentum, variance, fresh, fresh.astype(jnp.bfloat16), jnp.stack([w_norm, u_norm]))

def adam_plain(weight, grad, first, second, fix):
    momentum = BETA * first + (1.0 - BETA) * grad
    variance = BETA * second + (1.0 - BETA) * grad * grad
    fresh = weight - RATE_VEC * (momentum / fix) / (jnp.sqrt(variance / fix) + EPS_ADAM)
    return (momentum, variance, fresh)

def reference(inputs, frames, cotangent, proj_in, proj_out, ffn_up, ffn_down, vectors, ffn_bias, first_in, second_in, first_out, second_out, first_up, second_up, first_down, second_down, first_vec, second_vec, first_bias, second_bias):
    params = (proj_in, proj_out, ffn_up, ffn_down, vectors, ffn_bias)
    batch_in = inputs.astype(jnp.float32).reshape(-1, TOK_MB, D)
    batch_cot = cotangent.reshape(-1, TOK_MB, D)
    zeros = jax.tree.map(jnp.zeros_like, params)

    def one_block(total, item):
        values, cot, counts = item
        mask = allowed(counts, TOK_MB)
        result, pull = jax.vjp(lambda p, v: forward(p, v, mask), params, values)
        d_params, d_values = pull(cot)
        return (jax.tree.map(jnp.add, total, d_params), (result.astype(jnp.bfloat16), d_values))
    grads, (results, d_inputs) = lax.scan(one_block, zeros, (batch_in, batch_cot, frames))
    g_in, g_out, g_up, g_down, g_vec, g_bias = grads
    fix = 1.0 - BETA ** STEP
    m_in, v_in, w_in, c_in, n_in = lamb(proj_in, g_in, first_in, second_in, fix)
    m_out, v_out, w_out, c_out, n_out = lamb(proj_out, g_out, first_out, second_out, fix)
    m_up, v_up, w_up, c_up, n_up = lamb(ffn_up, g_up, first_up, second_up, fix)
    m_down, v_down, w_down, c_down, n_down = lamb(ffn_down, g_down, first_down, second_down, fix)
    m_vec, v_vec, w_vec = adam_plain(vectors, g_vec, first_vec, second_vec, fix)
    m_bias, v_bias, w_bias = adam_plain(ffn_bias, g_bias, first_bias, second_bias, fix)
    norms = jnp.stack([n_in, n_out, n_up, n_down])
    return (results.reshape(-1, D), d_inputs.reshape(-1, D), g_in.reshape(-1), g_out.reshape(-1), g_up.reshape(-1), g_down.reshape(-1), g_vec, g_bias, m_in, v_in, w_in, c_in, m_out, v_out, w_out, c_out, m_up, v_up, w_up, c_up, m_down, v_down, w_down, c_down, m_vec, v_vec, w_vec, m_bias, v_bias, w_bias, norms)
```

```python
import functools
import math

import jax
import jax.numpy as jnp
from jax import lax
from jax.experimental import pallas as pl
from jax.experimental.pallas import tpu as pltpu
from jax.sharding import PartitionSpec as P

HEADS = 4
FRAME = 17
STEP = 10

EPS_NORM = 1e-05
EPS_ADAM = 1e-06
BETA = 0.5
DECAY = 0.01
RATE = 0.5
RATE_VEC = 0.2

TILE = 256
QT = 128
SPAN = 384
LEAD = 16
REACH = 16
BIG = 1e30

f32 = jnp.float32
bf16 = jnp.bfloat16


def dot(a, b):
    return jnp.dot(a, b, preferred_element_type=f32)


def dot_nt(a, b):
    return lax.dot_general(a, b, (((1,), (1,)), ((), ())), preferred_element_type=f32)


def normalize(x):
    inv = 1.0 / x.shape[1]
    center = x - jnp.sum(x, axis=1, keepdims=True) * inv
    rstd = lax.rsqrt(jnp.sum(center * center, axis=1, keepdims=True) * inv + EPS_NORM)
    return center * rstd, rstd


def norm_back(dy, gain, n, rstd):
    inv = 1.0 / n.shape[1]
    e = dy * gain
    mean_e = jnp.sum(e, axis=1, keepdims=True) * inv
    mean_en = jnp.sum(e * n, axis=1, keepdims=True) * inv
    return rstd * (e - mean_e - n * mean_en)


def gelu_parts(x):
    den = 1.0 + jnp.abs(x) * (0.3275911 / math.sqrt(2.0))
    t = pl.reciprocal(den, approx=True)
    t = t * (2.0 - den * t)
    bell = jnp.exp(x * x * -0.5)
    poly = 0.5 * 1.061405429
    for c in (-1.453152027, 1.421413741, -0.284496736, 0.254829592):
        poly = poly * t + 0.5 * c
    tail = poly * t * bell
    cdf = jnp.where(x < 0.0, tail, 1.0 - tail)
    return x * cdf, cdf + x * (bell * (1.0 / math.sqrt(2.0 * math.pi)))


def fold8(x):
    return jnp.sum(x.reshape(x.shape[0] // 8, 8, x.shape[1]), axis=0)


def local_kernel(
    frames_ref, x_hbm, cot_hbm, pin_ref, pout_ref, pup_ref, pdown_ref, vec_ref, bias_ref,
    bo_hbm, gi_hbm, ga_ref, gup_ref, gdown_ref,
    xs, cs, bos, qs, ks, vs, dq, dk, dv, dms, lse, dka, dva, turned, win, wout, wup, wdown, gdt, sums, bsum, sems,
):
    rows, width = x_hbm.shape
    padded = xs.shape[0]
    steps = padded // TILE
    pairs = width // 128
    hidden_width = pup_ref.shape[1]
    micro, packed = frames_ref.shape

    x_in = pltpu.make_async_copy(x_hbm, xs.at[pl.ds(0, rows)], sems.at[0])
    c_in = pltpu.make_async_copy(cot_hbm, cs.at[pl.ds(0, rows)], sems.at[1])
    x_in.start()
    c_in.start()

    win[...] = pin_ref[...].astype(bf16)
    wout[...] = pout_ref[...].astype(bf16)
    wup[...] = pup_ref[...].astype(bf16)
    wdown[...] = pdown_ref[...].astype(bf16)
    gap = padded - rows
    if gap:
        xs[pl.ds(rows, gap)] = jnp.zeros((gap, width), bf16)
        cs[pl.ds(rows, gap)] = jnp.zeros((gap, width), f32)
        dq[pl.ds(rows, gap)] = jnp.zeros((gap, width), bf16)
    for ref in (qs, ks, vs, dms):
        ref[pl.ds(padded, SPAN)] = jnp.zeros((SPAN, width), bf16)
    for ref in (ga_ref, gup_ref, gdt, sums, bsum):
        ref[...] = jnp.zeros_like(ref)
    x_in.wait()

    def tile_at(i):
        return pl.ds(pl.multiple_of(i * TILE, TILE), TILE)

    gain_one, shift_one = vec_ref[3:4, :], vec_ref[4:5, :]
    gain_two, shift_two = vec_ref[5:6, :], vec_ref[6:7, :]

    def project(i, _):
        at = tile_at(i)
        n, _r = normalize(xs[at].astype(f32))
        h = (n * gain_one + shift_one).astype(bf16)
        q = dot(h, win[:, :width]) + vec_ref[0:1, :]
        qs[at] = q.astype(bf16) * jnp.array(0.125, bf16)
        ks[at] = dot(h, win[:, width : 2 * width]).astype(bf16)
        vs[at] = (dot(h, win[:, 2 * width :]) + vec_ref[1:2, :]).astype(bf16)
        return 0

    lax.fori_loop(0, steps, project, 0)

    first_head = lax.broadcasted_iota(jnp.int32, (1, 128), 1) < 64
    keep0 = first_head.astype(f32).astype(bf16)
    keep1 = 1.0 - keep0

    def depth(j):
        return min(QT * (j + 1) + REACH, SPAN)

    def filled(j):
        return min(-(-depth(j) // 128) * 128, SPAN)

    def limits(j, off, stop):
        t = QT * j + (lax.broadcasted_iota(jnp.int32, (1, 2 * QT), 1) & (QT - 1))
        frame = ((t - off) * 241) >> 12
        end = jnp.minimum(off + FRAME * (frame + 1), stop)
        return end, (t >= off) & (t < stop)

    def hide(score, j, off, end):
        m = score.shape[0]
        edge = QT * j
        row = lambda lo, hi: lo + lax.broadcasted_iota(jnp.int32, (hi - lo, 2 * QT), 0)
        if j == 0:
            s = row(0, m)
            return jnp.where((s >= off) & (s < end), score, -BIG)
        return jnp.concatenate(
            [
                jnp.where(row(0, LEAD) >= off, score[:LEAD], -BIG),
                score[LEAD:edge],
                jnp.where(row(edge, m) < end, score[edge:], -BIG),
            ],
            axis=0,
        )

    def heads_apart(block):
        return jnp.concatenate([block * keep0, block * keep1], axis=0)

    def fill(block, j):
        short = filled(j) - depth(j)
        if not short:
            return block
        return jnp.concatenate([block, jnp.zeros((short, block.shape[1]), block.dtype)], axis=0)

    def heads_back(out):
        both = jnp.concatenate([out[:64, :QT], out[64:, QT:]], axis=0)
        return both.T

    def put(ref, at_row, lanes, value, off):
        lead = pl.ds(pl.multiple_of(at_row, LEAD), LEAD)
        own = lax.broadcasted_iota(jnp.int32, (LEAD, 128), 0) >= off
        old = ref[lead, lanes].astype(f32)
        ref[lead, lanes] = jnp.where(own, value[:LEAD], old).astype(bf16)
        rest = value.shape[0] - LEAD
        ref[pl.ds(pl.multiple_of(at_row + LEAD, LEAD), rest), lanes] = value[LEAD:].astype(bf16)

    def window(i, start):
        length = frames_ref[i // packed, i % packed] * FRAME
        off = start & (LEAD - 1)
        return pl.multiple_of(start - off, LEAD), off, off + length, start + length

    def attend(i, start):
        base, off, stop, after = window(i, start)
        for p in range(pairs):
            turned[p] = vs[pl.ds(base, SPAN), 128 * p : 128 * (p + 1)].T

        def step(j):
            end, valid = limits(j, off, stop)
            m = depth(j)
            for p in range(pairs):
                lanes = slice(128 * p, 128 * (p + 1))
                query = heads_apart(qs[pl.ds(pl.multiple_of(base + QT * j, LEAD), QT), lanes])
                score = hide(dot_nt(ks[pl.ds(base, m), lanes], query), j, off, end)
                peak = jnp.max(score, axis=0, keepdims=True)
                weight = jnp.exp(score - peak)
                total = jnp.sum(weight, axis=0, keepdims=True)
                prob = (weight * jnp.where(valid, 1.0 / total, 0.0)).astype(bf16)
                row = pairs * j + p
                lse[i, row : row + 1, :] = jnp.where(valid, peak + jnp.log(total), BIG)
                out = dot(turned[p, :, : filled(j)], fill(prob, j))
                block = heads_back(out)
                if j == 0:
                    put(dq, base, lanes, block, off)
                else:
                    dq[pl.ds(pl.multiple_of(base + QT * j, LEAD), QT), lanes] = block.astype(bf16)

        step(0)
        for j in range(1, SPAN // QT):
            pl.when(stop > QT * j)(functools.partial(step, j))
        return after

    lax.fori_loop(0, micro * packed, attend, 0)

    c_in.wait()

    def feed_forward(i, _):
        at = tile_at(i)
        mixed = dq[at]
        resid = xs[at].astype(f32) + dot(mixed, wout[...]) + vec_ref[2:3, :]
        n, rstd = normalize(resid)
        h = (n * gain_two + shift_two).astype(bf16)
        cot = cs[at]
        low = cot.astype(bf16)
        h_t, low_t = h.T, low.T
        feed = jnp.zeros((TILE, width), f32)
        d_h = jnp.zeros((TILE, width), f32)
        for c in range(0, hidden_width, 256):
            cols = slice(c, c + 256)
            pre = dot(h, wup[:, cols]) + bias_ref[:, cols]
            act, slope = gelu_parts(pre)
            act = act.astype(bf16)
            feed += dot(act, wdown[cols, :])
            d_pre = (dot_nt(low, wdown[cols, :]) * slope).astype(bf16)
            d_h += dot_nt(d_pre, wup[:, cols])
            gdt[:, cols] += dot(low_t, act)
            gup_ref[:, cols] += dot(h_t, d_pre)
            bsum[:, cols] += fold8(d_pre.astype(f32))
        bos[at] = (resid + feed + vec_ref[7:8, :]).astype(bf16)
        d_resid = cot + norm_back(d_h, gain_two, n, rstd)
        cs[at] = d_resid
        branch = d_resid.astype(bf16)
        sums[2] += fold8(branch.astype(f32))
        sums[5] += fold8(d_h * n)
        sums[6] += fold8(d_h)
        sums[7] += fold8(low.astype(f32))
        ga_ref[:, 3 * width : 4 * width] += dot(mixed.T, branch)
        dms[at] = dot_nt(branch, wout[...]).astype(bf16)
        return 0

    lax.fori_loop(0, steps, feed_forward, 0)
    bo_out = pltpu.make_async_copy(bos.at[pl.ds(0, rows)], bo_hbm, sems.at[2])
    bo_out.start()

    def attend_back(i, start):
        base, off, stop, after = window(i, start)
        for p in range(pairs):
            turned[p] = ks[pl.ds(base, SPAN), 128 * p : 128 * (p + 1)].T
        dka[...] = jnp.zeros_like(dka)
        dva[...] = jnp.zeros_like(dva)

        def step(j):
            end, _valid = limits(j, off, stop)
            m = depth(j)
            for p in range(pairs):
                lanes = slice(128 * p, 128 * (p + 1))
                here = pl.ds(pl.multiple_of(base + QT * j, LEAD), QT)
                query = heads_apart(qs[here, lanes])
                d_out = heads_apart(dms[here, lanes])
                row = pairs * j + p
                score = hide(dot_nt(ks[pl.ds(base, m), lanes], query), j, off, end)
                prob = jnp.exp(score - lse[i, row : row + 1, :])
                d_prob = dot_nt(vs[pl.ds(base, m), lanes], d_out)
                delta = jnp.sum(prob * d_prob, axis=0, keepdims=True)
                d_score = (prob * (d_prob - delta)).astype(bf16)
                dva[:m, lanes] += dot(prob.astype(bf16), d_out)
                dka[:m, lanes] += dot(d_score, query)
                out = dot(turned[p, :, : filled(j)], fill(d_score, j))
                block = heads_back(out) * 0.125
                if j == 0:
                    put(dq, base, lanes, block, off)
                else:
                    dq[here, lanes] = block.astype(bf16)

        step(0)
        for j in range(1, SPAN // QT):
            pl.when(stop > QT * j)(functools.partial(step, j))
        for p in range(pairs):
            lanes = slice(128 * p, 128 * (p + 1))
            put(dk, base, lanes, dka[:, lanes], off)
            put(dv, base, lanes, dva[:, lanes], off)
        return after

    lax.fori_loop(0, micro * packed, attend_back, 0)
    if gap:
        for ref in (dq, dk, dv):
            ref[pl.ds(rows, gap)] = jnp.zeros((gap, width), bf16)

    def project_back(i, _):
        at = tile_at(i)
        n, rstd = normalize(xs[at].astype(f32))
        h_t = (n * gain_one + shift_one).astype(bf16).T
        d_h = jnp.zeros((TILE, width), f32)
        for b, ref in enumerate((dq, dk, dv)):
            cols = slice(b * width, (b + 1) * width)
            block = ref[at]
            d_h += dot_nt(block, win[:, cols])
            ga_ref[:, cols] += dot(h_t, block)
            if b != 1:
                sums[b // 2] += fold8(block.astype(f32))
        sums[3] += fold8(d_h * n)
        sums[4] += fold8(d_h)
        cs[at] = cs[at] + norm_back(d_h, gain_one, n, rstd)
        return 0

    lax.fori_loop(0, steps, project_back, 0)
    gi_out = pltpu.make_async_copy(cs.at[pl.ds(0, rows)], gi_hbm, sems.at[3])
    gi_out.start()
    for c in range(0, hidden_width, 256):
        gdown_ref[c : c + 256, :] = gdt[:, c : c + 256].T
    vec = jnp.sum(sums[...], axis=1)
    tail = 4 * width
    for b in range(width // 128):
        ga_ref[8 * b : 8 * b + 8, tail : tail + 128] = vec[:, 128 * b : 128 * (b + 1)]
    bias = jnp.sum(bsum[...], axis=0, keepdims=True)
    for b in range(hidden_width // 128):
        row = 8 * (width // 128) + b
        ga_ref[row : row + 1, tail : tail + 128] = bias[:, 128 * b : 128 * (b + 1)]
    bo_out.wait()
    gi_out.wait()


def local_grads(inputs, frames, cotangent, proj_in, proj_out, ffn_up, ffn_down, vectors, ffn_bias):
    rows, width = inputs.shape
    hidden_width = ffn_up.shape[1]
    padded = -(-rows // TILE) * TILE
    wide = padded + SPAN
    pairs = width // 128
    vmem = pl.BlockSpec(memory_space=pltpu.VMEM)
    hbm = pl.BlockSpec(memory_space=pl.ANY)
    return pl.pallas_call(
        local_kernel,
        out_shape=(
            jax.ShapeDtypeStruct((rows, width), bf16),
            jax.ShapeDtypeStruct((rows, width), f32),
            jax.ShapeDtypeStruct((width, 4 * width + 128), f32),
            jax.ShapeDtypeStruct((width, hidden_width), f32),
            jax.ShapeDtypeStruct((hidden_width, width), f32),
        ),
        in_specs=[pl.BlockSpec(memory_space=pltpu.SMEM), hbm, hbm] + [vmem] * 6,
        out_specs=(hbm, hbm, vmem, vmem, vmem),
        scratch_shapes=[
            pltpu.VMEM((padded, width), bf16),
            pltpu.VMEM((padded, width), f32),
            pltpu.VMEM((padded, width), bf16),
            *[pltpu.VMEM((wide, width), bf16)] * 7,
            pltpu.VMEM((frames.size, 8, 2 * QT), f32),
            pltpu.VMEM((SPAN, width), f32),
            pltpu.VMEM((SPAN, width), f32),
            pltpu.VMEM((pairs, 128, SPAN), bf16),
            pltpu.VMEM((width, 3 * width), bf16),
            pltpu.VMEM((width, width), bf16),
            pltpu.VMEM((width, hidden_width), bf16),
            pltpu.VMEM((hidden_width, width), bf16),
            pltpu.VMEM((width, hidden_width), f32),
            pltpu.VMEM((8, 8, width), f32),
            pltpu.VMEM((8, hidden_width), f32),
            pltpu.SemaphoreType.DMA((4,)),
        ],
        compiler_params=pltpu.CompilerParams(vmem_limit_bytes=60 * 1024 * 1024),
        name="local_grads",
    )(frames, inputs, cotangent, proj_in, proj_out, ffn_up, ffn_down, vectors, ffn_bias.reshape(1, hidden_width))


def own_share(array, length, place):
    return lax.dynamic_slice_in_dim(array.reshape(-1), place * length, length)


def shard_steps(shares, firsts, seconds, weights, place, fix):
    results = []
    for share, first, second, weight in zip(shares, firsts, seconds, weights):
        momentum = BETA * first + (1.0 - BETA) * share
        variance = BETA * second + (1.0 - BETA) * share * share
        w_share = own_share(weight, first.shape[0], place)
        advance = momentum / fix / (jnp.sqrt(variance / fix) + EPS_ADAM) + DECAY * w_share
        results.append((momentum, variance, advance, w_share))
    return results


def adam_plain(weight, grad, first, second, fix):
    momentum = BETA * first + (1.0 - BETA) * grad
    variance = BETA * second + (1.0 - BETA) * grad * grad
    fresh = weight - RATE_VEC * (momentum / fix) / (jnp.sqrt(variance / fix) + EPS_ADAM)
    return (momentum, variance, fresh)


def on_device(
    inputs,
    frames,
    cotangent,
    proj_in,
    proj_out,
    ffn_up,
    ffn_down,
    vectors,
    ffn_bias,
    first_in,
    second_in,
    first_out,
    second_out,
    first_up,
    second_up,
    first_down,
    second_down,
    first_vec,
    second_vec,
    first_bias,
    second_bias,
):
    bf = jnp.bfloat16
    width = inputs.shape[1]
    block_out, grad_inputs, g_a, g_up, g_down = local_grads(
        inputs, frames, cotangent, proj_in, proj_out, ffn_up, ffn_down, vectors, ffn_bias
    )
    g_in = g_a[:, : 3 * width]
    g_out = g_a[:, 3 * width : 4 * width]
    extra = g_a[:24, 4 * width :]
    g_vec = jnp.concatenate([extra[:8], extra[8:16]], axis=1)
    g_bias = extra[16:24].reshape(-1)
    fix = 1.0 - BETA**STEP
    place = lax.axis_index("dp")
    weights = (proj_in, proj_out, ffn_up, ffn_down)
    firsts = (first_in, first_out, first_up, first_down)
    seconds = (second_in, second_out, second_up, second_down)
    g_in, g_out, g_up, g_down, g_vec, g_bias = lax.psum(
        (g_in, g_out, g_up, g_down, g_vec, g_bias), "dp"
    )
    shares = [
        own_share(full, first.shape[0], place)
        for full, first in zip((g_in, g_out, g_up, g_down), firsts)
    ]
    updated = shard_steps(shares, firsts, seconds, weights, place, fix)
    squares = jnp.stack([jnp.sum(entry[2] * entry[2]) for entry in updated])
    squares = lax.psum(squares, "dp")
    w_norms = jnp.stack([jnp.sqrt(jnp.sum(weight * weight)) for weight in weights])
    u_norms = jnp.sqrt(squares)
    fresh_shares = tuple(
        (
            entry[3] - RATE * (w_norms[index] / (u_norms[index] + EPS_ADAM)) * entry[2]
            for index, entry in enumerate(updated)
        )
    )
    gathered = lax.all_gather(fresh_shares, "dp", axis=0, tiled=True)
    fresh = [full.reshape(weight.shape) for full, weight in zip(gathered, weights)]
    m_vec, v_vec, w_vec = adam_plain(vectors, g_vec, first_vec, second_vec, fix)
    m_bias, v_bias, w_bias = adam_plain(ffn_bias, g_bias, first_bias, second_bias, fix)
    norms = jnp.stack([w_norms, u_norms], axis=1)
    return (
        block_out,
        grad_inputs,
        shares[0],
        shares[1],
        shares[2],
        shares[3],
        g_vec,
        g_bias,
        updated[0][0],
        updated[0][1],
        fresh[0],
        fresh[0].astype(bf),
        updated[1][0],
        updated[1][1],
        fresh[1],
        fresh[1].astype(bf),
        updated[2][0],
        updated[2][1],
        fresh[2],
        fresh[2].astype(bf),
        updated[3][0],
        updated[3][1],
        fresh[3],
        fresh[3].astype(bf),
        m_vec,
        v_vec,
        w_vec,
        m_bias,
        v_bias,
        w_bias,
        norms,
    )


def solution(mesh):
    placed = (
        P("dp", None),
        P("dp", None),
        P("dp", None),
        P(),
        P(),
        P(),
        P(),
        P(),
        P(),
        P("dp"),
        P("dp"),
        P("dp"),
        P("dp"),
        P("dp"),
        P("dp"),
        P("dp"),
        P("dp"),
        P(),
        P(),
        P(),
        P(),
    )
    return jax.shard_map(
        on_device,
        mesh=mesh,
        in_specs=placed,
        out_specs=(
            P("dp", None),
            P("dp", None),
            P("dp"),
            P("dp"),
            P("dp"),
            P("dp"),
            P(),
            P(),
            P("dp"),
            P("dp"),
            P(),
            P(),
            P("dp"),
            P("dp"),
            P(),
            P(),
            P("dp"),
            P("dp"),
            P(),
            P(),
            P("dp"),
            P("dp"),
            P(),
            P(),
            P(),
            P(),
            P(),
            P(),
            P(),
            P(),
            P(),
        ),
        check_vma=False,
    )
```

```python
import functools
import math

import jax
import jax.numpy as jnp
from jax import lax
from jax.experimental import pallas as pl
from jax.experimental.pallas import tpu as pltpu
from jax.sharding import PartitionSpec as P

HEADS = 4
FRAME = 17
STEP = 10

EPS_NORM = 1e-05
EPS_ADAM = 1e-06
BETA = 0.5
DECAY = 0.01
RATE = 0.5
RATE_VEC = 0.2

TILE = 256
QT = 128
SPAN = 384
LEAD = 16
REACH = 16
BIG = 1e30

f32 = jnp.float32
bf16 = jnp.bfloat16


def dot(a, b):
    return jnp.dot(a, b, preferred_element_type=f32)


def dot_nt(a, b):
    return lax.dot_general(a, b, (((1,), (1,)), ((), ())), preferred_element_type=f32)


def normalize(x):
    inv = 1.0 / x.shape[1]
    center = x - jnp.sum(x, axis=1, keepdims=True) * inv
    rstd = lax.rsqrt(jnp.sum(center * center, axis=1, keepdims=True) * inv + EPS_NORM)
    return center * rstd, rstd


def norm_back(dy, gain, n, rstd):
    inv = 1.0 / n.shape[1]
    e = dy * gain
    mean_e = jnp.sum(e, axis=1, keepdims=True) * inv
    mean_en = jnp.sum(e * n, axis=1, keepdims=True) * inv
    return rstd * (e - mean_e - n * mean_en)


def gelu_parts(x):
    den = 1.0 + jnp.abs(x) * (0.3275911 / math.sqrt(2.0))
    t = pl.reciprocal(den, approx=True)
    t = t * (2.0 - den * t)
    bell = jnp.exp(x * x * -0.5)
    poly = 0.5 * 1.061405429
    for c in (-1.453152027, 1.421413741, -0.284496736, 0.254829592):
        poly = poly * t + 0.5 * c
    tail = poly * t * bell
    cdf = jnp.where(x < 0.0, tail, 1.0 - tail)
    return x * cdf, cdf + x * (bell * (1.0 / math.sqrt(2.0 * math.pi)))


def fold8(x):
    return jnp.sum(x.reshape(x.shape[0] // 8, 8, x.shape[1]), axis=0)


def local_kernel(
    frames_ref, x_hbm, cot_hbm, pin_ref, pout_ref, pup_ref, pdown_ref, vec_ref, bias_ref,
    bo_hbm, gi_hbm, ga_ref, gup_ref, gdown_ref,
    xs, cs, bos, qs, ks, vs, dq, dk, dv, dms, lse, dka, dva, turned, win, wout, wup, wdown, gdt, sums, bsum, sems,
):
    rows, width = x_hbm.shape
    padded = xs.shape[0]
    steps = padded // TILE
    pairs = width // 128
    hidden_width = pup_ref.shape[1]
    micro, packed = frames_ref.shape

    x_in = pltpu.make_async_copy(x_hbm, xs.at[pl.ds(0, rows)], sems.at[0])
    c_in = pltpu.make_async_copy(cot_hbm, cs.at[pl.ds(0, rows)], sems.at[1])
    x_in.start()
    c_in.start()

    win[...] = pin_ref[...].astype(bf16)
    wout[...] = pout_ref[...].astype(bf16)
    wup[...] = pup_ref[...].astype(bf16)
    wdown[...] = pdown_ref[...].astype(bf16)
    gap = padded - rows
    if gap:
        xs[pl.ds(rows, gap)] = jnp.zeros((gap, width), bf16)
        cs[pl.ds(rows, gap)] = jnp.zeros((gap, width), f32)
        dq[pl.ds(rows, gap)] = jnp.zeros((gap, width), bf16)
    for ref in (qs, ks, vs, dms):
        ref[pl.ds(padded, SPAN)] = jnp.zeros((SPAN, width), bf16)
    for ref in (ga_ref, gup_ref, gdt, sums, bsum):
        ref[...] = jnp.zeros_like(ref)
    x_in.wait()

    def tile_at(i):
        return pl.ds(pl.multiple_of(i * TILE, TILE), TILE)

    gain_one, shift_one = vec_ref[3:4, :], vec_ref[4:5, :]
    gain_two, shift_two = vec_ref[5:6, :], vec_ref[6:7, :]

    def project(i, _):
        at = tile_at(i)
        n, _r = normalize(xs[at].astype(f32))
        h = (n * gain_one + shift_one).astype(bf16)
        q = dot(h, win[:, :width]) + vec_ref[0:1, :]
        qs[at] = q.astype(bf16) * jnp.array(0.125, bf16)
        ks[at] = dot(h, win[:, width : 2 * width]).astype(bf16)
        vs[at] = (dot(h, win[:, 2 * width :]) + vec_ref[1:2, :]).astype(bf16)
        return 0

    lax.fori_loop(0, steps, project, 0)

    first_head = lax.broadcasted_iota(jnp.int32, (1, 128), 1) < 64
    keep0 = first_head.astype(f32).astype(bf16)
    keep1 = 1.0 - keep0

    def depth(j):
        return min(QT * (j + 1) + REACH, SPAN)

    def filled(j):
        return min(-(-depth(j) // 128) * 128, SPAN)

    def limits(j, off, stop):
        t = QT * j + (lax.broadcasted_iota(jnp.int32, (1, 2 * QT), 1) & (QT - 1))
        frame = ((t - off) * 241) >> 12
        end = jnp.minimum(off + FRAME * (frame + 1), stop)
        return end, (t >= off) & (t < stop)

    def hide(score, j, off, end):
        m = score.shape[0]
        edge = QT * j
        row = lambda lo, hi: lo + lax.broadcasted_iota(jnp.int32, (hi - lo, 2 * QT), 0)
        if j == 0:
            s = row(0, m)
            return jnp.where((s >= off) & (s < end), score, -BIG)
        return jnp.concatenate(
            [
                jnp.where(row(0, LEAD) >= off, score[:LEAD], -BIG),
                score[LEAD:edge],
                jnp.where(row(edge, m) < end, score[edge:], -BIG),
            ],
            axis=0,
        )

    def heads_apart(block):
        return jnp.concatenate([block * keep0, block * keep1], axis=0)

    def fill(block, j):
        short = filled(j) - depth(j)
        if not short:
            return block
        return jnp.concatenate([block, jnp.zeros((short, block.shape[1]), block.dtype)], axis=0)

    def heads_back(out):
        both = jnp.concatenate([out[:64, :QT], out[64:, QT:]], axis=0)
        return both.T

    def put(ref, at_row, lanes, value, off):
        lead = pl.ds(pl.multiple_of(at_row, LEAD), LEAD)
        own = lax.broadcasted_iota(jnp.int32, (LEAD, 128), 0) >= off
        old = ref[lead, lanes].astype(f32)
        ref[lead, lanes] = jnp.where(own, value[:LEAD], old).astype(bf16)
        rest = value.shape[0] - LEAD
        ref[pl.ds(pl.multiple_of(at_row + LEAD, LEAD), rest), lanes] = value[LEAD:].astype(bf16)

    def window(i, start):
        length = frames_ref[i // packed, i % packed] * FRAME
        off = start & (LEAD - 1)
        return pl.multiple_of(start - off, LEAD), off, off + length, start + length

    def attend(i, start):
        base, off, stop, after = window(i, start)
        for p in range(pairs):
            turned[p] = vs[pl.ds(base, SPAN), 128 * p : 128 * (p + 1)].T

        def step(j):
            end, valid = limits(j, off, stop)
            m = depth(j)
            for p in range(pairs):
                lanes = slice(128 * p, 128 * (p + 1))
                query = heads_apart(qs[pl.ds(pl.multiple_of(base + QT * j, LEAD), QT), lanes])
                score = hide(dot_nt(ks[pl.ds(base, m), lanes], query), j, off, end)
                peak = jnp.max(score, axis=0, keepdims=True)
                weight = jnp.exp(score - peak)
                total = jnp.sum(weight, axis=0, keepdims=True)
                prob = (weight * jnp.where(valid, 1.0 / total, 0.0)).astype(bf16)
                row = pairs * j + p
                lse[i, row : row + 1, :] = jnp.where(valid, peak + jnp.log(total), BIG)
                out = dot(turned[p, :, : filled(j)], fill(prob, j))
                block = heads_back(out)
                if j == 0:
                    put(dq, base, lanes, block, off)
                else:
                    dq[pl.ds(pl.multiple_of(base + QT * j, LEAD), QT), lanes] = block.astype(bf16)

        step(0)
        for j in range(1, SPAN // QT):
            pl.when(stop > QT * j)(functools.partial(step, j))
        return after

    lax.fori_loop(0, micro * packed, attend, 0)

    c_in.wait()

    def feed_forward(i, _):
        at = tile_at(i)
        mixed = dq[at]
        resid = xs[at].astype(f32) + dot(mixed, wout[...]) + vec_ref[2:3, :]
        n, rstd = normalize(resid)
        h = (n * gain_two + shift_two).astype(bf16)
        cot = cs[at]
        low = cot.astype(bf16)
        h_t, low_t = h.T, low.T
        feed = jnp.zeros((TILE, width), f32)
        d_h = jnp.zeros((TILE, width), f32)
        for c in range(0, hidden_width, 256):
            cols = slice(c, c + 256)
            pre = dot(h, wup[:, cols]) + bias_ref[:, cols]
            act, slope = gelu_parts(pre)
            act = act.astype(bf16)
            feed += dot(act, wdown[cols, :])
            d_pre = (dot_nt(low, wdown[cols, :]) * slope).astype(bf16)
            d_h += dot_nt(d_pre, wup[:, cols])
            gdt[:, cols] += dot(low_t, act)
            gup_ref[:, cols] += dot(h_t, d_pre)
            bsum[:, cols] += fold8(d_pre.astype(f32))
        bos[at] = (resid + feed + vec_ref[7:8, :]).astype(bf16)
        d_resid = cot + norm_back(d_h, gain_two, n, rstd)
        cs[at] = d_resid
        branch = d_resid.astype(bf16)
        sums[2] += fold8(branch.astype(f32))
        sums[5] += fold8(d_h * n)
        sums[6] += fold8(d_h)
        sums[7] += fold8(low.astype(f32))
        ga_ref[:, 3 * width : 4 * width] += dot(mixed.T, branch)
        dms[at] = dot_nt(branch, wout[...]).astype(bf16)
        return 0

    lax.fori_loop(0, steps, feed_forward, 0)
    bo_out = pltpu.make_async_copy(bos.at[pl.ds(0, rows)], bo_hbm, sems.at[2])
    bo_out.start()

    def attend_back(i, start):
        base, off, stop, after = window(i, start)
        for p in range(pairs):
            turned[p] = ks[pl.ds(base, SPAN), 128 * p : 128 * (p + 1)].T
        dka[...] = jnp.zeros_like(dka)
        dva[...] = jnp.zeros_like(dva)

        def step(j):
            end, _valid = limits(j, off, stop)
            m = depth(j)
            for p in range(pairs):
                lanes = slice(128 * p, 128 * (p + 1))
                here = pl.ds(pl.multiple_of(base + QT * j, LEAD), QT)
                query = heads_apart(qs[here, lanes])
                d_out = heads_apart(dms[here, lanes])
                row = pairs * j + p
                score = hide(dot_nt(ks[pl.ds(base, m), lanes], query), j, off, end)
                prob = jnp.exp(score - lse[i, row : row + 1, :])
                d_prob = dot_nt(vs[pl.ds(base, m), lanes], d_out)
                delta = jnp.sum(prob * d_prob, axis=0, keepdims=True)
                d_score = (prob * (d_prob - delta)).astype(bf16)
                dva[:m, lanes] += dot(prob.astype(bf16), d_out)
                dka[:m, lanes] += dot(d_score, query)
                out = dot(turned[p, :, : filled(j)], fill(d_score, j))
                block = heads_back(out) * 0.125
                if j == 0:
                    put(dq, base, lanes, block, off)
                else:
                    dq[here, lanes] = block.astype(bf16)

        step(0)
        for j in range(1, SPAN // QT):
            pl.when(stop > QT * j)(functools.partial(step, j))
        for p in range(pairs):
            lanes = slice(128 * p, 128 * (p + 1))
            put(dk, base, lanes, dka[:, lanes], off)
            put(dv, base, lanes, dva[:, lanes], off)
        return after

    lax.fori_loop(0, micro * packed, attend_back, 0)
    if gap:
        for ref in (dq, dk, dv):
            ref[pl.ds(rows, gap)] = jnp.zeros((gap, width), bf16)

    def project_back(i, _):
        at = tile_at(i)
        n, rstd = normalize(xs[at].astype(f32))
        h_t = (n * gain_one + shift_one).astype(bf16).T
        d_h = jnp.zeros((TILE, width), f32)
        for b, ref in enumerate((dq, dk, dv)):
            cols = slice(b * width, (b + 1) * width)
            block = ref[at]
            d_h += dot_nt(block, win[:, cols])
            ga_ref[:, cols] += dot(h_t, block)
            if b != 1:
                sums[b // 2] += fold8(block.astype(f32))
        sums[3] += fold8(d_h * n)
        sums[4] += fold8(d_h)
        cs[at] = cs[at] + norm_back(d_h, gain_one, n, rstd)
        return 0

    lax.fori_loop(0, steps, project_back, 0)
    gi_out = pltpu.make_async_copy(cs.at[pl.ds(0, rows)], gi_hbm, sems.at[3])
    gi_out.start()
    for c in range(0, hidden_width, 256):
        gdown_ref[c : c + 256, :] = gdt[:, c : c + 256].T
    vec = jnp.sum(sums[...], axis=1)
    tail = 4 * width
    for b in range(width // 128):
        ga_ref[8 * b : 8 * b + 8, tail : tail + 128] = vec[:, 128 * b : 128 * (b + 1)]
    bias = jnp.sum(bsum[...], axis=0, keepdims=True)
    for b in range(hidden_width // 128):
        row = 8 * (width // 128) + b
        ga_ref[row : row + 1, tail : tail + 128] = bias[:, 128 * b : 128 * (b + 1)]
    bo_out.wait()
    gi_out.wait()


def local_grads(inputs, frames, cotangent, proj_in, proj_out, ffn_up, ffn_down, vectors, ffn_bias):
    rows, width = inputs.shape
    hidden_width = ffn_up.shape[1]
    padded = -(-rows // TILE) * TILE
    wide = padded + SPAN
    pairs = width // 128
    vmem = pl.BlockSpec(memory_space=pltpu.VMEM)
    hbm = pl.BlockSpec(memory_space=pl.ANY)
    return pl.pallas_call(
        local_kernel,
        out_shape=(
            jax.ShapeDtypeStruct((rows, width), bf16),
            jax.ShapeDtypeStruct((rows, width), f32),
            jax.ShapeDtypeStruct((width, 4 * width + 128), f32),
            jax.ShapeDtypeStruct((width, hidden_width), f32),
            jax.ShapeDtypeStruct((hidden_width, width), f32),
        ),
        in_specs=[pl.BlockSpec(memory_space=pltpu.SMEM), hbm, hbm] + [vmem] * 6,
        out_specs=(hbm, hbm, vmem, vmem, vmem),
        scratch_shapes=[
            pltpu.VMEM((padded, width), bf16),
            pltpu.VMEM((padded, width), f32),
            pltpu.VMEM((padded, width), bf16),
            *[pltpu.VMEM((wide, width), bf16)] * 7,
            pltpu.VMEM((frames.size, 8, 2 * QT), f32),
            pltpu.VMEM((SPAN, width), f32),
            pltpu.VMEM((SPAN, width), f32),
            pltpu.VMEM((pairs, 128, SPAN), bf16),
            pltpu.VMEM((width, 3 * width), bf16),
            pltpu.VMEM((width, width), bf16),
            pltpu.VMEM((width, hidden_width), bf16),
            pltpu.VMEM((hidden_width, width), bf16),
            pltpu.VMEM((width, hidden_width), f32),
            pltpu.VMEM((8, 8, width), f32),
            pltpu.VMEM((8, hidden_width), f32),
            pltpu.SemaphoreType.DMA((4,)),
        ],
        compiler_params=pltpu.CompilerParams(vmem_limit_bytes=60 * 1024 * 1024),
        name="local_grads",
    )(frames, inputs, cotangent, proj_in, proj_out, ffn_up, ffn_down, vectors, ffn_bias.reshape(1, hidden_width))


def over_all(x):
    return jnp.sum(jnp.sum(x, axis=0, keepdims=True), axis=1, keepdims=True)


def momenta(first, second, grad):
    return BETA * first + (1.0 - BETA) * grad, BETA * second + (1.0 - BETA) * grad * grad


def direction(momentum, variance):
    fix = 1.0 - BETA**STEP
    return momentum / fix / (jnp.sqrt(variance / fix) + EPS_ADAM)


def places(order):
    top = len(order) - 1

    def chunk_of(pos):
        return sum((pos // (1 << (top - k))) % 2 * (1 << b) for k, b in enumerate(order))

    def place_of(chunk):
        return sum((chunk // (1 << b)) % 2 * (1 << (top - k)) for k, b in enumerate(order))

    return chunk_of, place_of


def matrix_lanes(shapes):
    return ((0, 0), (0, shapes[0][-1]), (1, 0), (2, 0))


def flat_rows(rows, blocks, b):
    return pl.ds(b, rows, stride=blocks) if blocks > 1 else pl.ds(0, rows)


def exchange_kernel(n, orders, stages, *refs):
    sources, owns, firsts, seconds = refs[:3], refs[3:7], refs[7:11], refs[11:15]
    full, shares = refs[15:18], refs[18:21]
    parcels, landed, send_sems, recv_sems = refs[21:24], refs[24:27], refs[27], refs[28]
    me = lax.axis_index("dp")

    def bit(k):
        return (me // (1 << k)) % 2

    def partner(k):
        return me + (1 - 2 * bit(k)) * (1 << k)

    barrier = pltpu.get_barrier_semaphore()
    for k in range(stages):
        pl.semaphore_signal(barrier, inc=1, device_id=(partner(k),), device_id_type=pl.DeviceIdType.MESH)
    pl.semaphore_wait(barrier, stages)

    def region(k):
        return n - (n >> k)

    def remote(p, slot, src, dst, k):
        return pltpu.make_async_remote_copy(
            src_ref=src,
            dst_ref=dst,
            send_sem=send_sems.at[p, slot],
            recv_sem=recv_sems.at[p, slot],
            device_id=(partner(k),),
            device_id_type=pl.DeviceIdType.MESH,
        )

    sent = []
    halving = {}

    def halve(p, k):
        m = n >> (k + 1)
        order = orders[p]
        if k == 0:
            away = (1 - bit(order[0])) * m

            def pack(i, _):
                parcels[p][i] = sources[p][places(order)[0](away + i)]
                return 0

            lax.fori_loop(0, m, pack, 0)
            src = parcels[p]
        else:
            src = landed[p].at[pl.ds(region(k - 1) + (1 - bit(order[k])) * m, m)]
        copy = remote(p, k, src, landed[p].at[pl.ds(region(k), m)], order[k])
        copy.start()
        halving[p, k] = copy
        sent.append(copy)

    def add(p, k):
        m = n >> (k + 1)
        order = orders[p]
        mine = bit(order[k]) * m
        halving[p, k].wait_recv()

        def one(i, _):
            if k == 0:
                kept = sources[p][places(order)[0](mine + i)]
            else:
                kept = landed[p][region(k - 1) + mine + i]
            at = region(k) + i
            landed[p][at] = landed[p][at] + kept
            return 0

        lax.fori_loop(0, m, one, 0)

    parts = range(len(orders))
    for p in parts:
        halve(p, 0)
    for k in range(1, stages):
        for p in parts:
            add(p, k - 1)
            halve(p, k)

    homes = [places(order)[1](me) for order in orders]
    matrices = matrix_lanes([own.shape for own in owns])
    gathering = {}

    def gather(p, k):
        size = 1 << (stages - 1 - k)
        at = pl.ds(homes[p] // size * size, size)
        copy = remote(p, stages + k, full[p].at[at], full[p].at[at], orders[p][k])
        copy.start()
        gathering[p, k] = copy
        sent.append(copy)

    for p in parts:
        add(p, stages - 1)
        last = region(stages - 1)
        for i, (part, lane) in enumerate(matrices):
            if part != p:
                continue
            rows = sources[p].shape[1]
            blocks = owns[i].shape[2] // 128
            for b in range(blocks):
                flat = flat_rows(rows, blocks, b)
                lanes = slice(128 * b, 128 * (b + 1))
                here = slice(lane + 128 * b, lane + 128 * (b + 1))
                momentum, variance = momenta(firsts[i][flat, :], seconds[i][flat, :], landed[p][last, :, here])
                full[p][homes[p], :, here] = direction(momentum, variance) + DECAY * owns[i][me, :, lanes]
        if p == 0:
            tail = slice(full[0].shape[2] - 128, full[0].shape[2])
            full[0][homes[0], :, tail] = landed[0][last, :, tail]
        shares[p][...] = landed[p][last]
        gather(p, stages - 1)
    for k in range(stages - 2, -1, -1):
        for p in parts:
            gathering[p, k + 1].wait_recv()
            gather(p, k)
    for p in parts:
        gathering[p, 0].wait_recv()

    for copy in sent:
        copy.wait_send()


def renew_kernel(n, orders, *refs):
    full, shares = refs[:3], refs[3:6]
    weights, firsts, seconds = refs[6:10], refs[10:14], refs[14:18]
    vec, bias, fvec, svec, fbias, sbias = refs[18:24]
    g_out, m_out, v_out = refs[24:28], refs[28:32], refs[32:36]
    w_new, w_low = refs[36:40], refs[40:44]
    gvec, gbias, mvec, vvec, wvec, mbias, vbias, wbias, norms = refs[44:53]
    rows24 = refs[53]
    for i, (part, lane) in enumerate(matrix_lanes([w.shape for w in weights])):
        _, rows, columns = weights[i].shape
        here = slice(lane, lane + columns)
        place_of = places(orders[part])[1]
        blocks = columns // 128
        for b in range(blocks):
            flat = flat_rows(rows, blocks, b)
            g = shares[part][:, lane + 128 * b : lane + 128 * (b + 1)]
            g_out[i][flat, :] = g
            m_out[i][flat, :], v_out[i][flat, :] = momenta(firsts[i][flat, :], seconds[i][flat, :], g)
        step = full[part][:, :, here]
        u_norm = jnp.sqrt(over_all(jnp.sum(step * step, axis=0)))
        old = weights[i][...]
        w_norm = jnp.sqrt(over_all(jnp.sum(old * old, axis=0)))
        norms[i : i + 1, 0:1] = w_norm
        norms[i : i + 1, 1:2] = u_norm
        ratio = RATE * (w_norm / (u_norm + EPS_ADAM))

        def renew(chunk, _, i=i, part=part, here=here, place_of=place_of, ratio=ratio):
            w_new[i][chunk] = weights[i][chunk] - ratio * full[part][place_of(chunk), :, here]
            return 0

        lax.fori_loop(0, n, renew, 0)
        if rows % 8 == 0:
            w_low[i][...] = w_new[i][...].reshape(n * rows, columns).astype(bf16)
        else:
            w_low[i][...] = jnp.zeros_like(w_low[i])

    rows = full[0].shape[1]
    tail = full[0].shape[2] - 128
    for chunk in range(rows24.shape[0] // rows):
        rows24[chunk * rows : (chunk + 1) * rows, :] = full[0][places(orders[0])[1](chunk), :, tail:]

    def plain(weight, grad, first, second):
        momentum, variance = momenta(first, second, grad)
        return momentum, variance, weight - RATE_VEC * direction(momentum, variance)

    grad = jnp.concatenate([rows24[0:8, :], rows24[8:16, :]], axis=1)
    gvec[...] = grad
    mvec[...], vvec[...], wvec[...] = plain(vec[...], grad, fvec[...], svec[...])
    grad = rows24[16:24, :]
    gbias[...] = grad
    mbias[...], vbias[...], wbias[...] = plain(bias[...], grad, fbias[...], sbias[...])


def exchange(n, grads, weights, vectors, ffn_bias, firsts, seconds, others):
    stages = n.bit_length() - 1
    far = list(range(1, stages))
    turns = [far[s:] + far[:s] for s in (len(far) * p // 3 for p in range(3))]
    orders = tuple((0, *turn) for turn in turns)
    cut = lambda a: a.reshape(n, a.shape[0] // n, a.shape[1])
    sources, blocks = list(map(cut, grads)), list(map(cut, weights))
    flat = lambda a: a.reshape(-1, 128)
    vmem = pl.BlockSpec(memory_space=pltpu.VMEM)
    like = lambda a, dtype=f32: jax.ShapeDtypeStruct(a.shape, dtype)
    firsts, seconds = list(map(flat, firsts)), list(map(flat, seconds))
    operands = [*sources, *blocks, *firsts, *seconds]
    shapes = [*map(like, sources), *[jax.ShapeDtypeStruct(s.shape[1:], f32) for s in sources]]
    reduced = pl.pallas_call(
        functools.partial(exchange_kernel, n, orders, stages),
        out_shape=shapes,
        in_specs=[vmem] * len(operands),
        out_specs=[vmem] * len(shapes),
        scratch_shapes=[
            *[pltpu.VMEM((n // 2, *s.shape[1:]), f32) for s in sources],
            *[pltpu.VMEM(s.shape, f32) for s in sources],
            pltpu.SemaphoreType.DMA((3, 2 * stages)),
            pltpu.SemaphoreType.DMA((3, 2 * stages)),
        ],
        compiler_params=pltpu.CompilerParams(
            collective_id=0, has_side_effects=True, vmem_limit_bytes=32 * 1024 * 1024
        ),
        name="exchange",
    )(*operands)
    line_bias = flat(ffn_bias)
    operands = [
        *reduced, *blocks, *firsts, *seconds, vectors, line_bias, others[0], others[1], flat(others[2]), flat(others[3]),
    ]
    moments = list(map(like, firsts))
    shapes = [
        *moments, *moments, *moments, *map(like, blocks), *[like(w, bf16) for w in weights],
        like(vectors), like(line_bias), *[like(vectors)] * 3, *[like(line_bias)] * 3, jax.ShapeDtypeStruct((4, 2), f32),
    ]
    results = pl.pallas_call(
        functools.partial(renew_kernel, n, orders),
        out_shape=shapes,
        in_specs=[vmem] * len(operands),
        out_specs=[vmem] * len(shapes),
        scratch_shapes=[pltpu.VMEM((24, 128), f32)],
        compiler_params=pltpu.CompilerParams(vmem_limit_bytes=32 * 1024 * 1024),
        name="renew",
    )(*operands)
    g, m, v = ([a.reshape(-1) for a in results[4 * i : 4 * i + 4]] for i in range(3))
    w = [new.reshape(old.shape) for new, old in zip(results[12:16], weights)]
    low = [new.astype(bf16) if block.shape[1] % 8 else own for new, own, block in zip(w, results[16:20], blocks)]
    gvec, gbias, mvec, vvec, wvec, mbias, vbias, wbias, norms = results[20:]
    line = lambda a: a.reshape(-1)
    steps = [entry for i in range(4) for entry in (m[i], v[i], w[i], low[i])]
    return (*g, gvec, line(gbias), *steps, mvec, vvec, wvec, line(mbias), line(vbias), line(wbias), norms)


def on_device(n, inputs, frames, cotangent, *rest):
    proj_in, proj_out, ffn_up, ffn_down, vectors, ffn_bias = rest[:6]
    moments, others = rest[6:14], rest[14:]
    block_out, grad_inputs, *grads = local_grads(
        inputs, frames, cotangent, proj_in, proj_out, ffn_up, ffn_down, vectors, ffn_bias
    )
    weights = (proj_in, proj_out, ffn_up, ffn_down)
    return (
        block_out,
        grad_inputs,
        *exchange(n, grads, weights, vectors, ffn_bias, moments[0::2], moments[1::2], others),
    )


def solution(mesh):
    split, rows, copied = P("dp"), P("dp", None), P()
    step = (split, split, copied, copied)
    return jax.shard_map(
        functools.partial(on_device, mesh.shape["dp"]),
        mesh=mesh,
        in_specs=(rows, rows, rows, *[copied] * 6, *[split] * 8, *[copied] * 4),
        out_specs=(rows, rows, *[split] * 4, copied, copied, *step * 4, *[copied] * 7),
        check_vma=False,
    )
```

```python
import functools
import math

import jax
import jax.numpy as jnp
from jax import lax
from jax.experimental import pallas as pl
from jax.experimental.pallas import tpu as pltpu
from jax.sharding import PartitionSpec as P

HEADS = 4
FRAME = 17
STEP = 10

EPS_NORM = 1e-05
EPS_ADAM = 1e-06
BETA = 0.5
DECAY = 0.01
RATE = 0.5
RATE_VEC = 0.2

TILE = 256
GROUP = 2
PROJECTED = 4
SLOTS = 2
LAG, LAG_BACK, LAG_FEED, LAG_PROJECT = 3, 2, 2, 1
QT = 128
SPAN = 384
LEAD = 16
REACH = 16
BIG = 1e30

f32 = jnp.float32
bf16 = jnp.bfloat16


def dot(a, b):
    return jnp.dot(a, b, preferred_element_type=f32)


def dot_nt(a, b):
    return lax.dot_general(a, b, (((1,), (1,)), ((), ())), preferred_element_type=f32)


def normalize(x):
    inv = 1.0 / x.shape[1]
    center = x - jnp.sum(x, axis=1, keepdims=True) * inv
    rstd = lax.rsqrt(jnp.sum(center * center, axis=1, keepdims=True) * inv + EPS_NORM)
    return center * rstd, rstd


def norm_back(dy, gain, n, rstd):
    inv = 1.0 / n.shape[1]
    e = dy * gain
    mean_e = jnp.sum(e, axis=1, keepdims=True) * inv
    mean_en = jnp.sum(e * n, axis=1, keepdims=True) * inv
    return rstd * (e - mean_e - n * mean_en)


def gelu_parts(x):
    t = pltpu.reciprocal(1.0 + jnp.abs(x) * (0.3275911 / math.sqrt(2.0)), approx=True)
    y = x * math.sqrt(0.5 / math.log(2.0))
    bell = jnp.exp2(-0.5 * math.log2(2.0 * math.pi) - y * y)
    unit = 0.5 * math.sqrt(2.0 * math.pi)
    poly = unit * 1.061405429
    for c in (-1.453152027, 1.421413741, -0.284496736, 0.254829592):
        poly = poly * t + unit * c
    tail = poly * t * bell
    cdf = jnp.where(x < 0.0, tail, 1.0 - tail)
    return x * cdf, cdf + x * bell


def stagger(work, stages, lag):
    held = {}
    for u in range(len(work) + lag * (len(stages) - 1)):
        for k, stage in enumerate(stages):
            at = u - k * lag
            if 0 <= at < len(work):
                held[at] = stage(work[at], held.get(at))


def fold8(x):
    return jnp.sum(x.reshape(x.shape[0] // 8, 8, x.shape[1]), axis=0)


def local_kernel(
    frames_hbm, x_hbm, cot_hbm, pin_hbm, pout_hbm, pup_hbm, pdown_hbm, vec_hbm, bias_hbm,
    bo_hbm, gi_hbm, ga_ref, gup_hbm, gdown_hbm,
    frames_ref, pin_ref, pout_ref, pup_ref, pdown_ref, vec_ref, bias_ref, xs, cs, bos, qs, ks, vs, dq, dk, dv, dms, lse, dka, dva, counts, members, starts, win, wout, wup, wdown, gup_ref, gdown_ref, gdt, sums, bsum, sems, x_sems, gi_sems,
):
    rows, width = x_hbm.shape
    padded = xs.shape[0]
    steps = padded // TILE
    pairs = width // 128
    hidden_width = pup_hbm.shape[1]
    micro, packed = frames_hbm.shape

    piece = TILE * PROJECTED
    final = padded // piece - 1

    def by_piece(i, act, hbm, local, sems_, out=False):
        def at(start, size):
            ends = hbm.at[pl.ds(start, size)], local.at[pl.ds(start, size)]
            act(pltpu.make_async_copy(*(ends[::-1] if out else ends), sems_.at[i]))

        pl.when(i < final)(lambda: at(pl.multiple_of(i * piece, piece), piece))
        pl.when(i == final)(lambda: at(final * piece, rows - final * piece))

    begin, finish = lambda copy: copy.start(), lambda copy: copy.wait()
    loads = [
        pltpu.make_async_copy(src, dst, sems.at[k])
        for k, (src, dst) in enumerate(
            (
                (vec_hbm, vec_ref),
                (pin_hbm, pin_ref),
                (frames_hbm, frames_ref),
                (bias_hbm, bias_ref),
                (pout_hbm, pout_ref),
                (pup_hbm, pup_ref),
                (pdown_hbm, pdown_ref),
                (cot_hbm, cs.at[pl.ds(0, rows)]),
            )
        )
    ]
    for copy in loads[:2]:
        copy.start()
    for i in range(final + 1):
        by_piece(i, begin, x_hbm, xs, x_sems)
    for copy in loads[2:]:
        copy.start()

    gap = padded - rows
    if gap:
        xs[pl.ds(rows, gap)] = jnp.zeros((gap, width), bf16)
        cs[pl.ds(rows, gap)] = jnp.zeros((gap, width), f32)
        dq[pl.ds(rows, gap)] = jnp.zeros((gap, width), bf16)
    for ref in (qs, ks, vs, dms):
        ref[pl.ds(padded, SPAN)] = jnp.zeros((SPAN, width), bf16)
    for ref in (ga_ref, gup_ref, gdt, sums, bsum):
        ref[...] = jnp.zeros_like(ref)
    for copy in loads[:2]:
        copy.wait()
    win[...] = pin_ref[...].astype(bf16)

    gain_one, shift_one = vec_ref[3:4, :], vec_ref[4:5, :]
    gain_two, shift_two = vec_ref[5:6, :], vec_ref[6:7, :]

    def spot(i, g, group=GROUP):
        return pl.ds(pl.multiple_of((i * group + g) * TILE, TILE), TILE)

    def project(i, _):
        by_piece(i, finish, x_hbm, xs, x_sems)

        def even(g, _):
            n, _rstd = normalize(xs[spot(i, g, PROJECTED)].astype(f32))
            return (n * gain_one + shift_one).astype(bf16)

        def spread(g, h):
            return [dot(h, win[:, b * width : (b + 1) * width]) for b in range(3)]

        def keep(g, held):
            q, k, v = held
            at = spot(i, g, PROJECTED)
            qs[at] = (q + vec_ref[0:1, :]).astype(bf16) * jnp.array(0.125, bf16)
            ks[at] = k.astype(bf16)
            vs[at] = (v + vec_ref[1:2, :]).astype(bf16)

        stagger(list(range(PROJECTED)), (even, spread, keep), LAG_PROJECT)
        return 0

    lax.fori_loop(0, steps // PROJECTED, project, 0)

    for copy in loads[2:]:
        copy.wait()
    wout[...] = pout_ref[...].astype(bf16)
    wup[...] = pup_ref[...].astype(bf16)
    wdown[...] = pdown_ref[...].astype(bf16)

    first_head = lax.broadcasted_iota(jnp.int32, (1, 128), 1) < 64
    keep0 = first_head.astype(f32).astype(bf16)
    keep1 = 1.0 - keep0

    def depth(j):
        return min(QT * (j + 1) + REACH, SPAN)

    def filled(j):
        return min(-(-depth(j) // 128) * 128, SPAN)

    def limits(j, off, stop):
        t = QT * j + (lax.broadcasted_iota(jnp.int32, (1, 2 * QT), 1) & (QT - 1))
        frame = ((t - off) * 241) >> 12
        end = jnp.minimum(off + FRAME * (frame + 1), stop)
        return end, (t >= off) & (t < stop)

    def hide(score, j, off, end):
        m = score.shape[0]
        edge = QT * j
        row = lambda lo, hi: lo + lax.broadcasted_iota(jnp.int32, (hi - lo, 2 * QT), 0)
        if j == 0:
            s = row(0, m)
            return jnp.where((s >= off) & (s < end), score, -BIG)
        return jnp.concatenate(
            [
                jnp.where(row(0, LEAD) >= off, score[:LEAD], -BIG),
                score[LEAD:edge],
                jnp.where(row(edge, m) < end, score[edge:], -BIG),
            ],
            axis=0,
        )

    def heads_apart(block):
        return jnp.concatenate([block * keep0, block * keep1], axis=0)

    def fill(block, j):
        short = filled(j) - depth(j)
        if not short:
            return block
        return jnp.concatenate([block, jnp.zeros((short, block.shape[1]), block.dtype)], axis=0)

    def heads_back(out):
        both = jnp.concatenate([out[:64, :QT], out[64:, QT:]], axis=0)
        return both.T

    def put(ref, base, lanes, block, j, off, stop):
        at = pl.ds(pl.multiple_of(base + QT * j, LEAD), QT)
        own = lax.broadcasted_iota(jnp.int32, (QT, 128), 0)
        keep = own < stop - QT * j
        if j == 0:
            keep &= own >= off
        ref[at, lanes] = jnp.where(keep, block, ref[at, lanes].astype(f32)).astype(bf16)

    classes = SPAN // QT
    for c in range(classes):
        counts[c] = 0

    def sort(i, start):
        length = frames_ref[i // packed, i % packed] * FRAME
        tiles = ((start & (LEAD - 1)) + length + QT - 1) // QT - 1
        seat = counts[tiles]
        members[tiles, seat] = i
        counts[tiles] = seat + 1
        starts[i] = start
        return start + length

    lax.fori_loop(0, micro * packed, sort, 0)
    for c in range(classes - 1):
        odd = counts[c] & 1

        @pl.when(odd == 1)
        def _(c=c):
            members[c + 1, counts[c + 1]] = members[c, counts[c] - 1]
            counts[c + 1] = counts[c + 1] + 1

    def window(n, tiles):
        i = members[tiles - 1, n]
        start = starts[i]
        off = start & (LEAD - 1)
        stop = off + frames_ref[i // packed, i % packed] * FRAME
        return i, pl.multiple_of(start - off, LEAD), off, stop

    def units(tiles, n):
        windows = [window(SLOTS * n + slot, tiles) for slot in range(SLOTS)]
        for j in reversed(range(tiles)):
            for p in range(pairs):
                for slot in range(SLOTS):
                    yield slot, p, slice(128 * p, 128 * (p + 1)), j, windows[slot]

    def attend(tiles, n, _):
        todo, v_t = [], {}

        def compare(unit, _):
            _slot, _p, lanes, j, (_i, base, _off, _stop) = unit
            query = heads_apart(qs[pl.ds(pl.multiple_of(base + QT * j, LEAD), QT), lanes])
            return dot_nt(ks[pl.ds(base, depth(j)), lanes], query)

        def soften(unit, raw):
            slot, p, lanes, j, (i, base, off, stop) = unit
            end, valid = limits(j, off, stop)
            score = hide(raw, j, off, end)
            peak = jnp.max(score, axis=0, keepdims=True)
            weight = jnp.exp(score - peak)
            total = jnp.sum(weight, axis=0, keepdims=True)
            row = pairs * j + p
            lse[i, row : row + 1, :] = jnp.where(valid, peak + jnp.log(total), BIG)
            prob = (weight * jnp.where(valid, 1.0 / total, 0.0)).astype(bf16)
            if (slot, p) not in v_t:
                v_t[slot, p] = vs[pl.ds(base, filled(tiles - 1)), lanes].T
            return dot(v_t[slot, p][:, : filled(j)], fill(prob, j))

        def turn(unit, out):
            _slot, _p, lanes, j, (_i, base, off, stop) = unit
            todo.append((dq, base, lanes, heads_back(out), j, off, stop))

        stagger(list(units(tiles, n)), (compare, soften, turn), LAG)
        for entry in todo:
            put(*entry)
        return 0

    for tiles in range(1, classes + 1):
        lax.fori_loop(0, counts[tiles - 1] // SLOTS, functools.partial(attend, tiles), 0)

    ones = jnp.ones((16, TILE * GROUP), bf16)

    def join(blocks, axis):
        return jnp.concatenate(blocks, axis=axis)

    def feed_forward(i, _):
        state = []
        for g in range(GROUP):
            at = spot(i, g)
            mixed = dq[at]
            resid = xs[at].astype(f32) + dot(mixed, wout[...]) + vec_ref[2:3, :]
            n, rstd = normalize(resid)
            h = (n * gain_two + shift_two).astype(bf16)
            state.append((at, mixed, resid, n, rstd, h, cs[at].astype(bf16)))
        h_t = jnp.concatenate([join([e[5].T for e in state], 1), ones], axis=0)
        low_t = join([e[6].T for e in state], 1)
        feeds, d_hs, acts, d_pres = [None] * GROUP, [None] * GROUP, {}, {}

        def expand(unit, _):
            c, g = unit
            cols = slice(c, c + 256)
            return dot(state[g][5], wup[:, cols]), dot_nt(state[g][6], wdown[cols, :])

        def bend(unit, held):
            c, g = unit
            pre, d_act = held
            act, slope = gelu_parts(pre + bias_ref[:, c : c + 256])
            act = act.astype(bf16)
            d_pre = (d_act * slope).astype(bf16)
            acts[c, g], d_pres[c, g] = act, d_pre
            return act, d_pre

        def shrink(unit, held):
            c, g = unit
            act, d_pre = held
            cols = slice(c, c + 256)
            feed, d_h = dot(act, wdown[cols, :]), dot_nt(d_pre, wup[:, cols])
            feeds[g] = feed if feeds[g] is None else feeds[g] + feed
            d_hs[g] = d_h if d_hs[g] is None else d_hs[g] + d_h
            if g == GROUP - 1:
                act = join([acts.get((c, k)) for k in range(GROUP)], 0)
                d_pre = join([d_pres.get((c, k)) for k in range(GROUP)], 0)
                gdt[:, cols] += dot(low_t, act)
                both = dot(h_t, d_pre)
                gup_ref[:, cols] += both[:width]
                bsum[:, cols] += both[width : width + 8]

        stagger([(c, g) for c in range(0, hidden_width, 256) for g in range(GROUP)], (expand, bend, shrink), LAG_FEED)
        branches = []
        for g in range(GROUP):
            at, _mixed, resid, n, rstd, _h, _low = state[g]
            feed, d_h = feeds[g], d_hs[g]
            bos[at] = (resid + feed + vec_ref[7:8, :]).astype(bf16)
            d_resid = cs[at] + norm_back(d_h, gain_two, n, rstd)
            cs[at] = d_resid
            branch = d_resid.astype(bf16)
            branches.append(branch)
            sums[5] += fold8(d_h * n)
            sums[6] += fold8(d_h)
            dms[at] = dot_nt(branch, wout[...]).astype(bf16)
        mixed_t = jnp.concatenate([join([e[1].T for e in state], 1), ones], axis=0)
        both = dot(mixed_t, join(branches, 0))
        ga_ref[:, 3 * width : 4 * width] += both[:width]
        sums[2] += both[width : width + 8] * 0.125
        sums[7] += dot(ones, join([e[6] for e in state], 0))[:8] * 0.125
        return 0

    lax.fori_loop(0, steps // GROUP, feed_forward, 0)
    bo_out = pltpu.make_async_copy(bos.at[pl.ds(0, rows)], bo_hbm, sems.at[8])
    bo_out.start()
    for c in range(0, hidden_width, 256):
        gdown_ref[c : c + 256, :] = gdt[:, c : c + 256].T
    grads_out = [
        pltpu.make_async_copy(gup_ref, gup_hbm, sems.at[9]),
        pltpu.make_async_copy(gdown_ref, gdown_hbm, sems.at[10]),
    ]
    for copy in grads_out:
        copy.start()

    def attend_back(tiles, n, _):
        todo, k_t = [], {}

        def compare(unit, _):
            _slot, _p, lanes, j, (_i, base, _off, _stop) = unit
            here = pl.ds(pl.multiple_of(base + QT * j, LEAD), QT)
            query, d_out = heads_apart(qs[here, lanes]), heads_apart(dms[here, lanes])
            m = depth(j)
            return query, d_out, dot_nt(ks[pl.ds(base, m), lanes], query), dot_nt(vs[pl.ds(base, m), lanes], d_out)

        def soften(unit, held):
            slot, p, lanes, j, (i, base, off, stop) = unit
            query, d_out, raw, d_prob = held
            end, _valid = limits(j, off, stop)
            row = pairs * j + p
            prob = jnp.exp(hide(raw, j, off, end) - lse[i, row : row + 1, :])
            delta = jnp.sum(prob * d_prob, axis=0, keepdims=True)
            d_score = (prob * (d_prob - delta)).astype(bf16)
            if (slot, p) not in k_t:
                k_t[slot, p] = ks[pl.ds(base, filled(tiles - 1)), lanes].T
            out = dot(k_t[slot, p][:, : filled(j)], fill(d_score, j))
            return dot(prob.astype(bf16), d_out), dot(d_score, query), out

        def collect(unit, held):
            slot, _p, lanes, j, (_i, base, off, stop) = unit
            d_val, d_key, out = held
            m = depth(j)
            first = j == tiles - 1
            dva[slot, :m, lanes] = d_val if first else dva[slot, :m, lanes] + d_val
            dka[slot, :m, lanes] = d_key if first else dka[slot, :m, lanes] + d_key
            todo.append((dq, base, lanes, heads_back(out) * 0.125, j, off, stop))

        stagger(list(units(tiles, n)), (compare, soften, collect), LAG_BACK)
        for entry in todo:
            put(*entry)
        for slot, p, lanes, j, (i, base, off, stop) in units(tiles, n):
            at = slice(QT * j, QT * (j + 1))
            put(dv, base, lanes, dva[slot, at, lanes], j, off, stop)
            put(dk, base, lanes, dka[slot, at, lanes], j, off, stop)
        return 0

    for tiles in range(1, classes + 1):
        lax.fori_loop(0, counts[tiles - 1] // SLOTS, functools.partial(attend_back, tiles), 0)
    if gap:
        for ref in (dq, dk, dv):
            ref[pl.ds(rows, gap)] = jnp.zeros((gap, width), bf16)

    def project_back(i, _):
        turned, blocks = {}, {}

        def even(g, _):
            n, rstd = normalize(xs[spot(i, g, PROJECTED)].astype(f32))
            turned[g] = (n * gain_one + shift_one).astype(bf16).T
            return n, rstd

        def spread(g, held):
            d_h = None
            for b, ref in enumerate((dq, dk, dv)):
                block = ref[spot(i, g, PROJECTED)]
                blocks[b, g] = block
                part = dot_nt(block, win[:, b * width : (b + 1) * width])
                d_h = part if d_h is None else d_h + part
            return *held, d_h

        def keep(g, held):
            n, rstd, d_h = held
            sums[3] += fold8(d_h * n)
            sums[4] += fold8(d_h)
            at = spot(i, g, PROJECTED)
            cs[at] = cs[at] + norm_back(d_h, gain_one, n, rstd)
            if g == PROJECTED - 1:
                h_t = jnp.concatenate([join([turned[k] for k in range(PROJECTED)], 1), jnp.ones((16, TILE * PROJECTED), bf16)], axis=0)
                for b in range(3):
                    both = dot(h_t, join([blocks[b, k] for k in range(PROJECTED)], 0))
                    ga_ref[:, b * width : (b + 1) * width] += both[:width]
                    if b != 1:
                        sums[b // 2] += both[width : width + 8] * 0.125

        stagger(list(range(PROJECTED)), (even, spread, keep), LAG_PROJECT)
        by_piece(i, begin, gi_hbm, cs, gi_sems, out=True)
        return 0

    lax.fori_loop(0, steps // PROJECTED, project_back, 0)
    vec = jnp.sum(sums[...], axis=1)
    tail = 4 * width
    for b in range(width // 128):
        ga_ref[8 * b : 8 * b + 8, tail : tail + 128] = vec[:, 128 * b : 128 * (b + 1)]
    bias = bsum[0:1, :]
    for b in range(hidden_width // 128):
        row = 8 * (width // 128) + b
        ga_ref[row : row + 1, tail : tail + 128] = bias[:, 128 * b : 128 * (b + 1)]
    for copy in (bo_out, *grads_out):
        copy.wait()
    for i in range(final + 1):
        by_piece(i, finish, gi_hbm, cs, gi_sems, out=True)


def local_grads(inputs, frames, cotangent, proj_in, proj_out, ffn_up, ffn_down, vectors, ffn_bias):
    rows, width = inputs.shape
    hidden_width = ffn_up.shape[1]
    step = TILE * max(GROUP, PROJECTED)
    padded = -(-rows // step) * step
    wide = padded + SPAN
    pairs = width // 128
    vmem = pl.BlockSpec(memory_space=pltpu.VMEM)
    hbm = pl.BlockSpec(memory_space=pltpu.HBM)
    bias = ffn_bias.reshape(1, hidden_width)
    return pl.pallas_call(
        local_kernel,
        out_shape=(
            jax.ShapeDtypeStruct((rows, width), bf16),
            jax.ShapeDtypeStruct((rows, width), f32),
            jax.ShapeDtypeStruct((width, 4 * width + 128), f32),
            jax.ShapeDtypeStruct((width, hidden_width), f32),
            jax.ShapeDtypeStruct((hidden_width, width), f32),
        ),
        in_specs=[hbm] * 9,
        out_specs=(hbm, hbm, vmem, hbm, hbm),
        scratch_shapes=[
            pltpu.SMEM(frames.shape, jnp.int32),
            *[pltpu.VMEM(a.shape, f32) for a in (proj_in, proj_out, ffn_up, ffn_down, vectors, bias)],
            pltpu.VMEM((padded, width), bf16),
            pltpu.VMEM((padded, width), f32),
            pltpu.VMEM((padded, width), bf16),
            *[pltpu.VMEM((wide, width), bf16)] * 7,
            pltpu.VMEM((frames.size, 8, 2 * QT), f32),
            pltpu.VMEM((2, SPAN, width), f32),
            pltpu.VMEM((2, SPAN, width), f32),
            pltpu.SMEM((SPAN // QT,), jnp.int32),
            pltpu.SMEM((SPAN // QT, frames.size + 1), jnp.int32),
            pltpu.SMEM((frames.size,), jnp.int32),
            pltpu.VMEM((width, 3 * width), bf16),
            pltpu.VMEM((width, width), bf16),
            pltpu.VMEM((width, hidden_width), bf16),
            pltpu.VMEM((hidden_width, width), bf16),
            pltpu.VMEM((width, hidden_width), f32),
            pltpu.VMEM((hidden_width, width), f32),
            pltpu.VMEM((width, hidden_width), f32),
            pltpu.VMEM((8, 8, width), f32),
            pltpu.VMEM((8, hidden_width), f32),
            pltpu.SemaphoreType.DMA((11,)),
            *[pltpu.SemaphoreType.DMA((padded // (TILE * PROJECTED),))] * 2,
        ],
        compiler_params=pltpu.CompilerParams(vmem_limit_bytes=60 * 1024 * 1024),
        name="local_grads",
    )(frames, inputs, cotangent, proj_in, proj_out, ffn_up, ffn_down, vectors, bias)


def over_all(x):
    return jnp.sum(jnp.sum(x, axis=0, keepdims=True), axis=1, keepdims=True)


def momenta(first, second, grad):
    return BETA * first + (1.0 - BETA) * grad, BETA * second + (1.0 - BETA) * grad * grad


def direction(momentum, variance):
    fix = 1.0 - BETA**STEP
    return momentum / fix / (jnp.sqrt(variance / fix) + EPS_ADAM)


def places(order):
    top = len(order) - 1

    def chunk_of(pos):
        return sum((pos // (1 << (top - k))) % 2 * (1 << b) for k, b in enumerate(order))

    def place_of(chunk):
        return sum((chunk // (1 << b)) % 2 * (1 << (top - k)) for k, b in enumerate(order))

    return chunk_of, place_of


def matrix_lanes(shapes):
    return ((0, 0), (0, shapes[0][-1]), (1, 0), (2, 0))


def flat_rows(rows, blocks, b):
    return pl.ds(b, rows, stride=blocks) if blocks > 1 else pl.ds(0, rows)


def exchange_kernel(n, orders, stages, *refs):
    sources, owns, firsts, seconds = refs[:3], refs[3:7], refs[7:11], refs[11:15]
    full, shares = refs[15:18], refs[18:21]
    parcels, landed, send_sems, recv_sems = refs[21:24], refs[24:27], refs[27], refs[28]
    me = lax.axis_index("dp")

    def bit(k):
        return (me // (1 << k)) % 2

    def partner(k):
        return me + (1 - 2 * bit(k)) * (1 << k)

    barrier = pltpu.get_barrier_semaphore()
    for k in range(stages):
        pl.semaphore_signal(barrier, inc=1, device_id=(partner(k),), device_id_type=pl.DeviceIdType.MESH)
    pl.semaphore_wait(barrier, stages)

    def region(k):
        return n - (n >> k)

    def remote(p, slot, src, dst, k):
        return pltpu.make_async_remote_copy(
            src_ref=src,
            dst_ref=dst,
            send_sem=send_sems.at[p, slot],
            recv_sem=recv_sems.at[p, slot],
            device_id=(partner(k),),
            device_id_type=pl.DeviceIdType.MESH,
        )

    sent = []
    halving = {}

    def halve(p, k):
        m = n >> (k + 1)
        order = orders[p]
        if k == 0:
            away = (1 - bit(order[0])) * m

            def pack(i, _):
                parcels[p][i] = sources[p][places(order)[0](away + i)]
                return 0

            lax.fori_loop(0, m, pack, 0)
            src = parcels[p]
        else:
            src = landed[p].at[pl.ds(region(k - 1) + (1 - bit(order[k])) * m, m)]
        copy = remote(p, k, src, landed[p].at[pl.ds(region(k), m)], order[k])
        copy.start()
        halving[p, k] = copy
        sent.append(copy)

    def add(p, k):
        m = n >> (k + 1)
        order = orders[p]
        mine = bit(order[k]) * m
        halving[p, k].wait_recv()

        def one(i, _):
            if k == 0:
                kept = sources[p][places(order)[0](mine + i)]
            else:
                kept = landed[p][region(k - 1) + mine + i]
            at = region(k) + i
            landed[p][at] = landed[p][at] + kept
            return 0

        lax.fori_loop(0, m, one, 0)

    parts = range(len(orders))
    for p in parts:
        halve(p, 0)
    for k in range(1, stages):
        for p in parts:
            add(p, k - 1)
            halve(p, k)

    homes = [places(order)[1](me) for order in orders]
    matrices = matrix_lanes([own.shape for own in owns])
    gathering = {}

    def gather(p, k):
        size = 1 << (stages - 1 - k)
        at = pl.ds(homes[p] // size * size, size)
        copy = remote(p, stages + k, full[p].at[at], full[p].at[at], orders[p][k])
        copy.start()
        gathering[p, k] = copy
        sent.append(copy)

    for p in parts:
        add(p, stages - 1)
        last = region(stages - 1)
        for i, (part, lane) in enumerate(matrices):
            if part != p:
                continue
            rows = sources[p].shape[1]
            blocks = owns[i].shape[2] // 128
            for b in range(blocks):
                flat = flat_rows(rows, blocks, b)
                lanes = slice(128 * b, 128 * (b + 1))
                here = slice(lane + 128 * b, lane + 128 * (b + 1))
                momentum, variance = momenta(firsts[i][flat, :], seconds[i][flat, :], landed[p][last, :, here])
                full[p][homes[p], :, here] = direction(momentum, variance) + DECAY * owns[i][me, :, lanes]
        if p == 0:
            tail = slice(full[0].shape[2] - 128, full[0].shape[2])
            full[0][homes[0], :, tail] = landed[0][last, :, tail]
        shares[p][...] = landed[p][last]
        gather(p, stages - 1)
    for k in range(stages - 2, -1, -1):
        for p in parts:
            gathering[p, k + 1].wait_recv()
            gather(p, k)
    for p in parts:
        gathering[p, 0].wait_recv()

    for copy in sent:
        copy.wait_send()


def renew_kernel(n, orders, *refs):
    full, shares = refs[:3], refs[3:6]
    weights, firsts, seconds = refs[6:10], refs[10:14], refs[14:18]
    vec, bias, fvec, svec, fbias, sbias = refs[18:24]
    g_out, m_out, v_out = refs[24:28], refs[28:32], refs[32:36]
    w_new, w_low = refs[36:40], refs[40:44]
    gvec, gbias, mvec, vvec, wvec, mbias, vbias, wbias, norms = refs[44:53]
    rows24 = refs[53]
    for i, (part, lane) in enumerate(matrix_lanes([w.shape for w in weights])):
        _, rows, columns = weights[i].shape
        here = slice(lane, lane + columns)
        place_of = places(orders[part])[1]
        blocks = columns // 128
        for b in range(blocks):
            flat = flat_rows(rows, blocks, b)
            g = shares[part][:, lane + 128 * b : lane + 128 * (b + 1)]
            g_out[i][flat, :] = g
            m_out[i][flat, :], v_out[i][flat, :] = momenta(firsts[i][flat, :], seconds[i][flat, :], g)
        step = full[part][:, :, here]
        u_norm = jnp.sqrt(over_all(jnp.sum(step * step, axis=0)))
        old = weights[i][...]
        w_norm = jnp.sqrt(over_all(jnp.sum(old * old, axis=0)))
        norms[i : i + 1, 0:1] = w_norm
        norms[i : i + 1, 1:2] = u_norm
        ratio = RATE * (w_norm / (u_norm + EPS_ADAM))

        def renew(chunk, _, i=i, part=part, here=here, place_of=place_of, ratio=ratio):
            w_new[i][chunk] = weights[i][chunk] - ratio * full[part][place_of(chunk), :, here]
            return 0

        lax.fori_loop(0, n, renew, 0)
        if rows % 8 == 0:
            w_low[i][...] = w_new[i][...].reshape(n * rows, columns).astype(bf16)
        else:
            w_low[i][...] = jnp.zeros_like(w_low[i])

    rows = full[0].shape[1]
    tail = full[0].shape[2] - 128
    for chunk in range(rows24.shape[0] // rows):
        rows24[chunk * rows : (chunk + 1) * rows, :] = full[0][places(orders[0])[1](chunk), :, tail:]

    def plain(weight, grad, first, second):
        momentum, variance = momenta(first, second, grad)
        return momentum, variance, weight - RATE_VEC * direction(momentum, variance)

    grad = jnp.concatenate([rows24[0:8, :], rows24[8:16, :]], axis=1)
    gvec[...] = grad
    mvec[...], vvec[...], wvec[...] = plain(vec[...], grad, fvec[...], svec[...])
    grad = rows24[16:24, :]
    gbias[...] = grad
    mbias[...], vbias[...], wbias[...] = plain(bias[...], grad, fbias[...], sbias[...])


def exchange(n, grads, weights, vectors, ffn_bias, firsts, seconds, others):
    stages = n.bit_length() - 1
    far = list(range(1, stages))
    turns = [far[s:] + far[:s] for s in (len(far) * p // 3 for p in range(3))]
    orders = tuple((0, *turn) for turn in turns)
    cut = lambda a: a.reshape(n, a.shape[0] // n, a.shape[1])
    sources, blocks = list(map(cut, grads)), list(map(cut, weights))
    flat = lambda a: a.reshape(-1, 128)
    vmem = pl.BlockSpec(memory_space=pltpu.VMEM)
    like = lambda a, dtype=f32: jax.ShapeDtypeStruct(a.shape, dtype)
    firsts, seconds = list(map(flat, firsts)), list(map(flat, seconds))
    operands = [*sources, *blocks, *firsts, *seconds]
    shapes = [*map(like, sources), *[jax.ShapeDtypeStruct(s.shape[1:], f32) for s in sources]]
    reduced = pl.pallas_call(
        functools.partial(exchange_kernel, n, orders, stages),
        out_shape=shapes,
        in_specs=[vmem] * len(operands),
        out_specs=[vmem] * len(shapes),
        scratch_shapes=[
            *[pltpu.VMEM((n // 2, *s.shape[1:]), f32) for s in sources],
            *[pltpu.VMEM(s.shape, f32) for s in sources],
            pltpu.SemaphoreType.DMA((3, 2 * stages)),
            pltpu.SemaphoreType.DMA((3, 2 * stages)),
        ],
        compiler_params=pltpu.CompilerParams(
            collective_id=0, has_side_effects=True, vmem_limit_bytes=32 * 1024 * 1024
        ),
        name="exchange",
    )(*operands)
    line_bias = flat(ffn_bias)
    operands = [
        *reduced, *blocks, *firsts, *seconds, vectors, line_bias, others[0], others[1], flat(others[2]), flat(others[3]),
    ]
    moments = list(map(like, firsts))
    shapes = [
        *moments, *moments, *moments, *map(like, blocks), *[like(w, bf16) for w in weights],
        like(vectors), like(line_bias), *[like(vectors)] * 3, *[like(line_bias)] * 3, jax.ShapeDtypeStruct((4, 2), f32),
    ]
    results = pl.pallas_call(
        functools.partial(renew_kernel, n, orders),
        out_shape=shapes,
        in_specs=[vmem] * len(operands),
        out_specs=[vmem] * len(shapes),
        scratch_shapes=[pltpu.VMEM((24, 128), f32)],
        compiler_params=pltpu.CompilerParams(vmem_limit_bytes=32 * 1024 * 1024),
        name="renew",
    )(*operands)
    g, m, v = ([a.reshape(-1) for a in results[4 * i : 4 * i + 4]] for i in range(3))
    w = [new.reshape(old.shape) for new, old in zip(results[12:16], weights)]
    low = [new.astype(bf16) if block.shape[1] % 8 else own for new, own, block in zip(w, results[16:20], blocks)]
    gvec, gbias, mvec, vvec, wvec, mbias, vbias, wbias, norms = results[20:]
    line = lambda a: a.reshape(-1)
    steps = [entry for i in range(4) for entry in (m[i], v[i], w[i], low[i])]
    return (*g, gvec, line(gbias), *steps, mvec, vvec, wvec, line(mbias), line(vbias), line(wbias), norms)


def on_device(n, inputs, frames, cotangent, *rest):
    proj_in, proj_out, ffn_up, ffn_down, vectors, ffn_bias = rest[:6]
    moments, others = rest[6:14], rest[14:]
    block_out, grad_inputs, *grads = local_grads(
        inputs, frames, cotangent, proj_in, proj_out, ffn_up, ffn_down, vectors, ffn_bias
    )
    weights = (proj_in, proj_out, ffn_up, ffn_down)
    return (
        block_out,
        grad_inputs,
        *exchange(n, grads, weights, vectors, ffn_bias, moments[0::2], moments[1::2], others),
    )


def solution(mesh):
    split, rows, copied = P("dp"), P("dp", None), P()
    step = (split, split, copied, copied)
    return jax.shard_map(
        functools.partial(on_device, mesh.shape["dp"]),
        mesh=mesh,
        in_specs=(rows, rows, rows, *[copied] * 6, *[split] * 8, *[copied] * 4),
        out_specs=(rows, rows, *[split] * 4, copied, copied, *step * 4, *[copied] * 7),
        check_vma=False,
    )
```

```python
import functools
import math

import jax
import jax.numpy as jnp
from jax import lax
from jax.experimental import pallas as pl
from jax.experimental.pallas import tpu as pltpu
from jax.sharding import PartitionSpec as P

HEADS = 4
FRAME = 17
STEP = 10

EPS_NORM = 1e-05
EPS_ADAM = 1e-06
BETA = 0.5
DECAY = 0.01
RATE = 0.5
RATE_VEC = 0.2

TILE = 256
GROUP = 2
PROJECTED = 4
SLOTS = 2
LAG, LAG_BACK, LAG_FEED, LAG_PROJECT = 3, 2, 2, 1
QT = 128
SPAN = 384
LEAD = 16
REACH = 16
BIG = 1e30

f32 = jnp.float32
bf16 = jnp.bfloat16


def dot(a, b):
    return jnp.dot(a, b, preferred_element_type=f32)


def dot_nt(a, b):
    return lax.dot_general(a, b, (((1,), (1,)), ((), ())), preferred_element_type=f32)


def normalize(x):
    inv = 1.0 / x.shape[1]
    center = x - jnp.sum(x, axis=1, keepdims=True) * inv
    rstd = lax.rsqrt(jnp.sum(center * center, axis=1, keepdims=True) * inv + EPS_NORM)
    return center * rstd, rstd


def norm_back(dy, gain, n, rstd):
    inv = 1.0 / n.shape[1]
    e = dy * gain
    mean_e = jnp.sum(e, axis=1, keepdims=True) * inv
    mean_en = jnp.sum(e * n, axis=1, keepdims=True) * inv
    return rstd * (e - mean_e - n * mean_en)


def gelu_parts(x):
    t = pltpu.reciprocal(1.0 + jnp.abs(x) * (0.3275911 / math.sqrt(2.0)), approx=True)
    y = x * math.sqrt(0.5 / math.log(2.0))
    bell = jnp.exp2(-0.5 * math.log2(2.0 * math.pi) - y * y)
    unit = 0.5 * math.sqrt(2.0 * math.pi)
    poly = unit * 1.061405429
    for c in (-1.453152027, 1.421413741, -0.284496736, 0.254829592):
        poly = poly * t + unit * c
    tail = poly * t * bell
    cdf = jnp.where(x < 0.0, tail, 1.0 - tail)
    return x * cdf, cdf + x * bell


def stagger(work, stages, lag):
    held = {}
    for u in range(len(work) + lag * (len(stages) - 1)):
        for k, stage in enumerate(stages):
            at = u - k * lag
            if 0 <= at < len(work):
                held[at] = stage(work[at], held.get(at))


def fold8(x):
    return jnp.sum(x.reshape(x.shape[0] // 8, 8, x.shape[1]), axis=0)


def local_kernel(
    frames_hbm, x_hbm, cot_hbm, pin_hbm, pout_hbm, pup_hbm, pdown_hbm, vec_hbm, bias_hbm,
    bo_hbm, gi_hbm, ga_ref, gup_hbm, gdown_hbm,
    frames_ref, pin_ref, pout_ref, pup_ref, pdown_ref, vec_ref, bias_ref, xs, cs, bos, qs, ks, vs, dq, dk, dv, dms, lse, dka, dva, counts, members, starts, win, wout, wup, wdown, gup_ref, gdown_ref, gdt, sums, bsum, sems, x_sems, gi_sems,
):
    rows, width = x_hbm.shape
    padded = xs.shape[0]
    steps = padded // TILE
    pairs = width // 128
    hidden_width = pup_hbm.shape[1]
    micro, packed = frames_hbm.shape

    piece = TILE * PROJECTED
    final = padded // piece - 1

    def by_piece(i, act, hbm, local, sems_, out=False):
        def at(start, size):
            ends = hbm.at[pl.ds(start, size)], local.at[pl.ds(start, size)]
            act(pltpu.make_async_copy(*(ends[::-1] if out else ends), sems_.at[i]))

        pl.when(i < final)(lambda: at(pl.multiple_of(i * piece, piece), piece))
        pl.when(i == final)(lambda: at(final * piece, rows - final * piece))

    begin, finish = lambda copy: copy.start(), lambda copy: copy.wait()
    loads = [
        pltpu.make_async_copy(src, dst, sems.at[k])
        for k, (src, dst) in enumerate(
            (
                (vec_hbm, vec_ref),
                (pin_hbm, pin_ref),
                (frames_hbm, frames_ref),
                (bias_hbm, bias_ref),
                (pout_hbm, pout_ref),
                (pup_hbm, pup_ref),
                (pdown_hbm, pdown_ref),
                (cot_hbm, cs.at[pl.ds(0, rows)]),
            )
        )
    ]
    for copy in loads[:2]:
        copy.start()
    for i in range(final + 1):
        by_piece(i, begin, x_hbm, xs, x_sems)
    for copy in loads[2:]:
        copy.start()

    gap = padded - rows
    if gap:
        xs[pl.ds(rows, gap)] = jnp.zeros((gap, width), bf16)
        cs[pl.ds(rows, gap)] = jnp.zeros((gap, width), f32)
        dq[pl.ds(rows, gap)] = jnp.zeros((gap, width), bf16)
    for ref in (qs, ks, vs, dms):
        ref[pl.ds(padded, SPAN)] = jnp.zeros((SPAN, width), bf16)
    for ref in (ga_ref, gup_ref, gdt, sums, bsum):
        ref[...] = jnp.zeros_like(ref)
    for copy in loads[:2]:
        copy.wait()
    win[...] = pin_ref[...].astype(bf16)

    gain_one, shift_one = vec_ref[3:4, :], vec_ref[4:5, :]
    gain_two, shift_two = vec_ref[5:6, :], vec_ref[6:7, :]

    def spot(i, g, group=GROUP):
        return pl.ds(pl.multiple_of((i * group + g) * TILE, TILE), TILE)

    def project(i, _):
        by_piece(i, finish, x_hbm, xs, x_sems)

        def even(g, _):
            n, _rstd = normalize(xs[spot(i, g, PROJECTED)].astype(f32))
            return (n * gain_one + shift_one).astype(bf16)

        def spread(g, h):
            return [dot(h, win[:, b * width : (b + 1) * width]) for b in range(3)]

        def keep(g, held):
            q, k, v = held
            at = spot(i, g, PROJECTED)
            qs[at] = (q + vec_ref[0:1, :]).astype(bf16) * jnp.array(0.125, bf16)
            ks[at] = k.astype(bf16)
            vs[at] = (v + vec_ref[1:2, :]).astype(bf16)

        stagger(list(range(PROJECTED)), (even, spread, keep), LAG_PROJECT)
        return 0

    lax.fori_loop(0, steps // PROJECTED, project, 0)

    for copy in loads[2:]:
        copy.wait()
    wout[...] = pout_ref[...].astype(bf16)
    wup[...] = pup_ref[...].astype(bf16)
    wdown[...] = pdown_ref[...].astype(bf16)

    first_head = lax.broadcasted_iota(jnp.int32, (1, 128), 1) < 64
    keep0 = first_head.astype(f32).astype(bf16)
    keep1 = 1.0 - keep0

    def depth(j):
        return min(QT * (j + 1) + REACH, SPAN)

    def filled(j):
        return min(-(-depth(j) // 128) * 128, SPAN)

    def limits(j, off, stop):
        t = QT * j + (lax.broadcasted_iota(jnp.int32, (1, 2 * QT), 1) & (QT - 1))
        frame = ((t - off) * 241) >> 12
        end = jnp.minimum(off + FRAME * (frame + 1), stop)
        return end, (t >= off) & (t < stop)

    def hide(score, j, off, end):
        m = score.shape[0]
        edge = QT * j
        row = lambda lo, hi: lo + lax.broadcasted_iota(jnp.int32, (hi - lo, 2 * QT), 0)
        if j == 0:
            s = row(0, m)
            return jnp.where((s >= off) & (s < end), score, -BIG)
        return jnp.concatenate(
            [
                jnp.where(row(0, LEAD) >= off, score[:LEAD], -BIG),
                score[LEAD:edge],
                jnp.where(row(edge, m) < end, score[edge:], -BIG),
            ],
            axis=0,
        )

    def heads_apart(block):
        return jnp.concatenate([block * keep0, block * keep1], axis=0)

    def fill(block, j):
        short = filled(j) - depth(j)
        if not short:
            return block
        return jnp.concatenate([block, jnp.zeros((short, block.shape[1]), block.dtype)], axis=0)

    def heads_back(out):
        both = jnp.concatenate([out[:64, :QT], out[64:, QT:]], axis=0)
        return both.T

    def put(ref, base, lanes, block, j, off, stop):
        at = pl.ds(pl.multiple_of(base + QT * j, LEAD), QT)
        own = lax.broadcasted_iota(jnp.int32, (QT, 128), 0)
        keep = own < stop - QT * j
        if j == 0:
            keep &= own >= off
        ref[at, lanes] = jnp.where(keep, block, ref[at, lanes].astype(f32)).astype(bf16)

    classes = SPAN // QT
    for c in range(classes):
        counts[c] = 0

    def sort(i, start):
        length = frames_ref[i // packed, i % packed] * FRAME
        tiles = ((start & (LEAD - 1)) + length + QT - 1) // QT - 1
        seat = counts[tiles]
        members[tiles, seat] = i
        counts[tiles] = seat + 1
        starts[i] = start
        return start + length

    lax.fori_loop(0, micro * packed, sort, 0)
    for c in range(classes - 1):
        odd = counts[c] & 1

        @pl.when(odd == 1)
        def _(c=c):
            members[c + 1, counts[c + 1]] = members[c, counts[c] - 1]
            counts[c + 1] = counts[c + 1] + 1

    def window(n, tiles):
        i = members[tiles - 1, n]
        start = starts[i]
        off = start & (LEAD - 1)
        stop = off + frames_ref[i // packed, i % packed] * FRAME
        return i, pl.multiple_of(start - off, LEAD), off, stop

    def units(tiles, n):
        windows = [window(SLOTS * n + slot, tiles) for slot in range(SLOTS)]
        for j in reversed(range(tiles)):
            for p in range(pairs):
                for slot in range(SLOTS):
                    yield slot, p, slice(128 * p, 128 * (p + 1)), j, windows[slot]

    def attend(tiles, n, _):
        todo, v_t = [], {}

        def compare(unit, _):
            _slot, _p, lanes, j, (_i, base, _off, _stop) = unit
            query = heads_apart(qs[pl.ds(pl.multiple_of(base + QT * j, LEAD), QT), lanes])
            return dot_nt(ks[pl.ds(base, depth(j)), lanes], query)

        def soften(unit, raw):
            slot, p, lanes, j, (i, base, off, stop) = unit
            end, valid = limits(j, off, stop)
            score = hide(raw, j, off, end)
            peak = jnp.max(score, axis=0, keepdims=True)
            weight = jnp.exp(score - peak)
            total = jnp.sum(weight, axis=0, keepdims=True)
            row = pairs * j + p
            lse[i, row : row + 1, :] = jnp.where(valid, peak + jnp.log(total), BIG)
            prob = (weight * jnp.where(valid, 1.0 / total, 0.0)).astype(bf16)
            if (slot, p) not in v_t:
                v_t[slot, p] = vs[pl.ds(base, filled(tiles - 1)), lanes].T
            return dot(v_t[slot, p][:, : filled(j)], fill(prob, j))

        def turn(unit, out):
            _slot, _p, lanes, j, (_i, base, off, stop) = unit
            todo.append((dq, base, lanes, heads_back(out), j, off, stop))

        stagger(list(units(tiles, n)), (compare, soften, turn), LAG)
        for entry in todo:
            put(*entry)
        return 0

    for tiles in range(1, classes + 1):
        lax.fori_loop(0, counts[tiles - 1] // SLOTS, functools.partial(attend, tiles), 0)

    ones = jnp.ones((16, TILE * GROUP), bf16)

    def join(blocks, axis):
        return jnp.concatenate(blocks, axis=axis)

    def feed_forward(i, _):
        state = []
        for g in range(GROUP):
            at = spot(i, g)
            mixed = dq[at]
            resid = xs[at].astype(f32) + dot(mixed, wout[...]) + vec_ref[2:3, :]
            n, rstd = normalize(resid)
            h = (n * gain_two + shift_two).astype(bf16)
            state.append((at, mixed, resid, n, rstd, h, cs[at].astype(bf16)))
        h_t = jnp.concatenate([join([e[5].T for e in state], 1), ones], axis=0)
        low_t = join([e[6].T for e in state], 1)
        feeds, d_hs, acts, d_pres = [None] * GROUP, [None] * GROUP, {}, {}

        def expand(unit, _):
            c, g = unit
            cols = slice(c, c + 256)
            return dot(state[g][5], wup[:, cols]), dot_nt(state[g][6], wdown[cols, :])

        def bend(unit, held):
            c, g = unit
            pre, d_act = held
            act, slope = gelu_parts(pre + bias_ref[:, c : c + 256])
            act = act.astype(bf16)
            d_pre = (d_act * slope).astype(bf16)
            acts[c, g], d_pres[c, g] = act, d_pre
            return act, d_pre

        def shrink(unit, held):
            c, g = unit
            act, d_pre = held
            cols = slice(c, c + 256)
            feed, d_h = dot(act, wdown[cols, :]), dot_nt(d_pre, wup[:, cols])
            feeds[g] = feed if feeds[g] is None else feeds[g] + feed
            d_hs[g] = d_h if d_hs[g] is None else d_hs[g] + d_h
            if g == GROUP - 1:
                act = join([acts.get((c, k)) for k in range(GROUP)], 0)
                d_pre = join([d_pres.get((c, k)) for k in range(GROUP)], 0)
                gdt[:, cols] += dot(low_t, act)
                both = dot(h_t, d_pre)
                gup_ref[:, cols] += both[:width]
                bsum[:, cols] += both[width : width + 8]

        stagger([(c, g) for c in range(0, hidden_width, 256) for g in range(GROUP)], (expand, bend, shrink), LAG_FEED)
        branches = []
        for g in range(GROUP):
            at, _mixed, resid, n, rstd, _h, _low = state[g]
            feed, d_h = feeds[g], d_hs[g]
            bos[at] = (resid + feed + vec_ref[7:8, :]).astype(bf16)
            d_resid = cs[at] + norm_back(d_h, gain_two, n, rstd)
            cs[at] = d_resid
            branch = d_resid.astype(bf16)
            branches.append(branch)
            sums[5] += fold8(d_h * n)
            sums[6] += fold8(d_h)
            dms[at] = dot_nt(branch, wout[...]).astype(bf16)
        mixed_t = jnp.concatenate([join([e[1].T for e in state], 1), ones], axis=0)
        both = dot(mixed_t, join(branches, 0))
        ga_ref[:, 3 * width : 4 * width] += both[:width]
        sums[2] += both[width : width + 8] * 0.125
        sums[7] += dot(ones, join([e[6] for e in state], 0))[:8] * 0.125
        return 0

    lax.fori_loop(0, steps // GROUP, feed_forward, 0)
    bo_out = pltpu.make_async_copy(bos.at[pl.ds(0, rows)], bo_hbm, sems.at[8])
    bo_out.start()
    for c in range(0, hidden_width, 256):
        gdown_ref[c : c + 256, :] = gdt[:, c : c + 256].T
    grads_out = [
        pltpu.make_async_copy(gup_ref, gup_hbm, sems.at[9]),
        pltpu.make_async_copy(gdown_ref, gdown_hbm, sems.at[10]),
    ]
    for copy in grads_out:
        copy.start()

    def attend_back(tiles, n, _):
        todo, k_t = [], {}

        def compare(unit, _):
            _slot, _p, lanes, j, (_i, base, _off, _stop) = unit
            here = pl.ds(pl.multiple_of(base + QT * j, LEAD), QT)
            query, d_out = heads_apart(qs[here, lanes]), heads_apart(dms[here, lanes])
            m = depth(j)
            return query, d_out, dot_nt(ks[pl.ds(base, m), lanes], query), dot_nt(vs[pl.ds(base, m), lanes], d_out)

        def soften(unit, held):
            slot, p, lanes, j, (i, base, off, stop) = unit
            query, d_out, raw, d_prob = held
            end, _valid = limits(j, off, stop)
            row = pairs * j + p
            prob = jnp.exp(hide(raw, j, off, end) - lse[i, row : row + 1, :])
            delta = jnp.sum(prob * d_prob, axis=0, keepdims=True)
            d_score = (prob * (d_prob - delta)).astype(bf16)
            if (slot, p) not in k_t:
                k_t[slot, p] = ks[pl.ds(base, filled(tiles - 1)), lanes].T
            out = dot(k_t[slot, p][:, : filled(j)], fill(d_score, j))
            return dot(prob.astype(bf16), d_out), dot(d_score, query), out

        def collect(unit, held):
            slot, _p, lanes, j, (_i, base, off, stop) = unit
            d_val, d_key, out = held
            m = depth(j)
            first = j == tiles - 1
            dva[slot, :m, lanes] = d_val if first else dva[slot, :m, lanes] + d_val
            dka[slot, :m, lanes] = d_key if first else dka[slot, :m, lanes] + d_key
            todo.append((dq, base, lanes, heads_back(out) * 0.125, j, off, stop))

        stagger(list(units(tiles, n)), (compare, soften, collect), LAG_BACK)
        for entry in todo:
            put(*entry)
        for slot, p, lanes, j, (i, base, off, stop) in units(tiles, n):
            at = slice(QT * j, QT * (j + 1))
            put(dv, base, lanes, dva[slot, at, lanes], j, off, stop)
            put(dk, base, lanes, dka[slot, at, lanes], j, off, stop)
        return 0

    for tiles in range(1, classes + 1):
        lax.fori_loop(0, counts[tiles - 1] // SLOTS, functools.partial(attend_back, tiles), 0)
    if gap:
        for ref in (dq, dk, dv):
            ref[pl.ds(rows, gap)] = jnp.zeros((gap, width), bf16)

    def project_back(i, _):
        turned, blocks = {}, {}

        def even(g, _):
            n, rstd = normalize(xs[spot(i, g, PROJECTED)].astype(f32))
            turned[g] = (n * gain_one + shift_one).astype(bf16).T
            return n, rstd

        def spread(g, held):
            d_h = None
            for b, ref in enumerate((dq, dk, dv)):
                block = ref[spot(i, g, PROJECTED)]
                blocks[b, g] = block
                part = dot_nt(block, win[:, b * width : (b + 1) * width])
                d_h = part if d_h is None else d_h + part
            return *held, d_h

        def keep(g, held):
            n, rstd, d_h = held
            sums[3] += fold8(d_h * n)
            sums[4] += fold8(d_h)
            at = spot(i, g, PROJECTED)
            cs[at] = cs[at] + norm_back(d_h, gain_one, n, rstd)
            if g == PROJECTED - 1:
                h_t = jnp.concatenate([join([turned[k] for k in range(PROJECTED)], 1), jnp.ones((16, TILE * PROJECTED), bf16)], axis=0)
                for b in range(3):
                    both = dot(h_t, join([blocks[b, k] for k in range(PROJECTED)], 0))
                    ga_ref[:, b * width : (b + 1) * width] += both[:width]
                    if b != 1:
                        sums[b // 2] += both[width : width + 8] * 0.125

        stagger(list(range(PROJECTED)), (even, spread, keep), LAG_PROJECT)
        by_piece(i, begin, gi_hbm, cs, gi_sems, out=True)
        return 0

    lax.fori_loop(0, steps // PROJECTED, project_back, 0)
    vec = jnp.sum(sums[...], axis=1)
    tail = 4 * width
    for b in range(width // 128):
        ga_ref[8 * b : 8 * b + 8, tail : tail + 128] = vec[:, 128 * b : 128 * (b + 1)]
    bias = bsum[0:1, :]
    for b in range(hidden_width // 128):
        row = 8 * (width // 128) + b
        ga_ref[row : row + 1, tail : tail + 128] = bias[:, 128 * b : 128 * (b + 1)]
    for copy in (bo_out, *grads_out):
        copy.wait()
    for i in range(final + 1):
        by_piece(i, finish, gi_hbm, cs, gi_sems, out=True)


def local_grads(inputs, frames, cotangent, proj_in, proj_out, ffn_up, ffn_down, vectors, ffn_bias):
    rows, width = inputs.shape
    hidden_width = ffn_up.shape[1]
    step = TILE * max(GROUP, PROJECTED)
    padded = -(-rows // step) * step
    wide = padded + SPAN
    pairs = width // 128
    vmem = pl.BlockSpec(memory_space=pltpu.VMEM)
    hbm = pl.BlockSpec(memory_space=pltpu.HBM)
    bias = ffn_bias.reshape(1, hidden_width)
    return pl.pallas_call(
        local_kernel,
        out_shape=(
            jax.ShapeDtypeStruct((rows, width), bf16),
            jax.ShapeDtypeStruct((rows, width), f32),
            jax.ShapeDtypeStruct((width, 4 * width + 128), f32),
            jax.ShapeDtypeStruct((width, hidden_width), f32),
            jax.ShapeDtypeStruct((hidden_width, width), f32),
        ),
        in_specs=[hbm] * 9,
        out_specs=(hbm, hbm, vmem, hbm, hbm),
        scratch_shapes=[
            pltpu.SMEM(frames.shape, jnp.int32),
            *[pltpu.VMEM(a.shape, f32) for a in (proj_in, proj_out, ffn_up, ffn_down, vectors, bias)],
            pltpu.VMEM((padded, width), bf16),
            pltpu.VMEM((padded, width), f32),
            pltpu.VMEM((padded, width), bf16),
            *[pltpu.VMEM((wide, width), bf16)] * 7,
            pltpu.VMEM((frames.size, 8, 2 * QT), f32),
            pltpu.VMEM((2, SPAN, width), f32),
            pltpu.VMEM((2, SPAN, width), f32),
            pltpu.SMEM((SPAN // QT,), jnp.int32),
            pltpu.SMEM((SPAN // QT, frames.size + 1), jnp.int32),
            pltpu.SMEM((frames.size,), jnp.int32),
            pltpu.VMEM((width, 3 * width), bf16),
            pltpu.VMEM((width, width), bf16),
            pltpu.VMEM((width, hidden_width), bf16),
            pltpu.VMEM((hidden_width, width), bf16),
            pltpu.VMEM((width, hidden_width), f32),
            pltpu.VMEM((hidden_width, width), f32),
            pltpu.VMEM((width, hidden_width), f32),
            pltpu.VMEM((8, 8, width), f32),
            pltpu.VMEM((8, hidden_width), f32),
            pltpu.SemaphoreType.DMA((11,)),
            *[pltpu.SemaphoreType.DMA((padded // (TILE * PROJECTED),))] * 2,
        ],
        compiler_params=pltpu.CompilerParams(vmem_limit_bytes=60 * 1024 * 1024),
        name="local_grads",
    )(frames, inputs, cotangent, proj_in, proj_out, ffn_up, ffn_down, vectors, bias)


def over_all(x):
    return jnp.sum(jnp.sum(x, axis=0, keepdims=True), axis=1, keepdims=True)


def momenta(first, second, grad):
    return BETA * first + (1.0 - BETA) * grad, BETA * second + (1.0 - BETA) * grad * grad


def direction(momentum, variance):
    fix = 1.0 - BETA**STEP
    return momentum / fix / (jnp.sqrt(variance / fix) + EPS_ADAM)


def places(order):
    top = len(order) - 1

    def chunk_of(pos):
        return sum((pos // (1 << (top - k))) % 2 * (1 << b) for k, b in enumerate(order))

    def place_of(chunk):
        return sum((chunk // (1 << b)) % 2 * (1 << (top - k)) for k, b in enumerate(order))

    return chunk_of, place_of


def each(count, body, block=32):
    block = min(count, block)
    if count == block:
        for i in range(count):
            body(i)
        return

    def some(outer, _):
        for i in range(block):
            body(outer * block + i)
        return 0

    lax.fori_loop(0, count // block, some, 0)


def cut_pieces(shapes):
    wide, tall = shapes[1][2] // 2, shapes[2][1] // 2
    return (
        (0, slice(0, shapes[0][1]), slice(0, 640)),
        (0, slice(0, shapes[0][1]), slice(640, shapes[0][2])),
        (1, slice(0, shapes[1][1]), slice(0, wide)),
        (1, slice(0, shapes[1][1]), slice(wide, 2 * wide)),
        (2, slice(0, tall), slice(0, shapes[2][2])),
        (2, slice(tall, 2 * tall), slice(0, shapes[2][2])),
    )


def cut_matrices(shapes):
    (_, r_in, w_in), (_, _, w_out), (_, r_up, w_up), (_, r_down, w_down) = shapes
    rest = w_in - 640
    return (
        (0, 0, r_in, 0, 640, 0, 0),
        (0, 0, r_in, 640, rest, 1, 0),
        (1, 0, r_in, 0, w_out, 1, rest),
        (2, 0, r_up, 0, w_up // 2, 2, 0),
        (2, 0, r_up, w_up // 2, w_up // 2, 3, 0),
        (3, 0, r_down // 2, 0, w_down, 4, 0),
        (3, r_down // 2, r_down // 2, 0, w_down, 5, 0),
    )


def flat_rows(first, rows, blocks, b):
    return pl.ds(first * blocks + b, rows, stride=blocks)


def exchange_kernel(n, walks, *refs):
    count, stages = len(walks), len(walks[0])
    sources, owns, firsts, seconds = refs[:3], refs[3:7], refs[7:11], refs[11:15]
    full, shares = refs[15 : 15 + count], refs[15 + count : 15 + 2 * count]
    parcels, landed = refs[15 + 2 * count : 15 + 3 * count], refs[15 + 3 * count : 15 + 4 * count]
    send_sems, recv_sems = refs[15 + 4 * count :]
    pieces = cut_pieces([s.shape for s in sources])
    orders = [[b for bits in walk for b in bits] for walk in walks]
    me = lax.axis_index("dp")

    def bit(k):
        return (me // (1 << k)) % 2

    def flips(bits):
        return [[b for j, b in enumerate(bits) if t >> j & 1] for t in range(1, 1 << len(bits))]

    def other(flip):
        return me + sum((1 - 2 * bit(b)) * (1 << b) for b in flip)

    def digit(bits, flip=()):
        top = len(bits) - 1
        return sum((1 - bit(b) if b in flip else bit(b)) * (1 << (top - j)) for j, b in enumerate(bits))

    def left(p, k):
        return n >> sum(len(bits) for bits in walks[p][: k + 1])

    def slot(p, k):
        return n - left(p, k - 1) if k else 0

    barrier = pltpu.get_barrier_semaphore()
    met = sorted({tuple(sorted(flip)) for walk in walks for bits in walk for flip in flips(bits)})
    for flip in met:
        pl.semaphore_signal(barrier, inc=1, device_id=(other(flip),), device_id_type=pl.DeviceIdType.MESH)
    pl.semaphore_wait(barrier, len(met))

    sent, used = {}, [0] * count

    def remote(p, src, dst, flip, key):
        copy = pltpu.make_async_remote_copy(
            src_ref=src,
            dst_ref=dst,
            send_sem=send_sems.at[p, used[p]],
            recv_sem=recv_sems.at[p, used[p]],
            device_id=(other(flip),),
            device_id_type=pl.DeviceIdType.MESH,
        )
        used[p] += 1
        copy.start()
        sent.setdefault(key, []).append(copy)
        return copy

    def leave(key):
        for copy in sent.pop(key, ()):
            copy.wait_send()

    def chunk_of(p, i, first):
        return places(orders[p][1:])[0](i) + first * (1 << orders[p][0])

    arriving = {}

    def split(p, k):
        m, bits = left(p, k), walks[p][k]
        copies = []
        for t, flip in enumerate(flips(bits)):
            if k == 0:
                source, rows, lanes = pieces[p]

                def pack(i):
                    parcels[p][i] = sources[source][chunk_of(p, i, 1 - bit(bits[0])), rows, lanes]

                each(m, pack)
                src = parcels[p]
            else:
                src = landed[p].at[pl.ds(slot(p, k - 1) + digit(bits, flip) * m, m)]
            copies.append(remote(p, src, landed[p].at[pl.ds(slot(p, k) + t * m, m)], flip, ("split", p, k)))
        arriving[p, k] = copies

    def add(p, k):
        m, bits = left(p, k), walks[p][k]
        for copy in arriving[p, k]:
            copy.wait_recv()
        new = pl.ds(slot(p, k), m)
        if k:
            total = landed[p][pl.ds(slot(p, k - 1) + digit(bits) * m, m)]
            for t in range(len(arriving[p, k])):
                total = total + landed[p][pl.ds(slot(p, k) + t * m, m)]
            landed[p][new] = total
            return
        source, rows, lanes = pieces[p]

        def one(i):
            landed[p][i] = landed[p][i] + sources[source][chunk_of(p, i, bit(bits[0])), rows, lanes]

        each(m, one)

    parts = range(count)
    half = count // 2
    for p in parts:
        split(p, 0)
    for k in range(1, stages):
        for p in parts:
            add(p, k - 1)
            if p >= half:
                leave(("split", p - half, k))
            split(p, k)

    homes = [places(order)[1](me) for order in orders]
    matrices = cut_matrices([own.shape for own in owns])

    def gather(p, k):
        m = left(p, k)
        at = pl.ds(homes[p] // m * m, m)
        arriving[p, stages + k] = [
            remote(p, full[p].at[at], full[p].at[at], flip, ("gather", p, k)) for flip in flips(walks[p][k])
        ]

    last = stages - 1
    for p in parts:
        add(p, last)
        share = slot(p, last)
        for i, row, rows, lane, lanes, piece, start in matrices:
            if piece != p:
                continue
            blocks = owns[i].shape[2] // 128
            for b in range(lanes // 128):
                flat = flat_rows(row, rows, blocks, lane // 128 + b)
                here = slice(start + 128 * b, start + 128 * (b + 1))
                own = owns[i][me, row : row + rows, lane + 128 * b : lane + 128 * (b + 1)]
                momentum, variance = momenta(firsts[i][flat, :], seconds[i][flat, :], landed[p][share, :, here])
                full[p][homes[p], :, here] = direction(momentum, variance) + DECAY * own
        if p == 1:
            tail = slice(full[1].shape[2] - 128, full[1].shape[2])
            full[1][homes[1], :, tail] = landed[1][share, :, tail]
        shares[p][...] = landed[p][share]
        gather(p, last)
    for k in range(last - 1, -1, -1):
        for p in parts:
            for copy in arriving[p, stages + k + 1]:
                copy.wait_recv()
            if p >= half and k:
                leave(("gather", p - half, k))
            gather(p, k)
    for p in parts:
        for copy in arriving[p, stages]:
            copy.wait_recv()
    for key in list(sent):
        leave(key)


def renew_kernel(n, orders, *refs):
    count = len(orders)
    full, shares, refs = refs[:count], refs[count : 2 * count], refs[2 * count :]
    weights, firsts, seconds = refs[:4], refs[4:8], refs[8:12]
    vec, bias, fvec, svec, fbias, sbias = refs[12:18]
    g_out, m_out, v_out = refs[18:22], refs[22:26], refs[26:30]
    w_out, low_out = refs[30:34], refs[34:38]
    gvec, gbias, mvec, vvec, wvec, mbias, vbias, wbias, norms = refs[38:47]
    rows24, w_new, w_low, sems = refs[47], refs[48:52], refs[52:56], refs[56]
    matrices = cut_matrices([w.shape for w in weights])
    for i, row, rows, lane, lanes, piece, start in matrices:
        blocks = weights[i].shape[2] // 128
        for b in range(lanes // 128):
            flat = flat_rows(row, rows, blocks, lane // 128 + b)
            g = shares[piece][:, start + 128 * b : start + 128 * (b + 1)]
            g_out[i][flat, :] = g
            m_out[i][flat, :], v_out[i][flat, :] = momenta(firsts[i][flat, :], seconds[i][flat, :], g)
    leaving = []
    for i in (2, 3, 0, 1):
        _, rows, columns = weights[i].shape
        own = [entry for entry in matrices if entry[0] == i]
        total = 0.0
        for _i, _row, _rows, _lane, lanes, piece, start in own:
            step = full[piece][:, :, start : start + lanes]
            total = total + over_all(jnp.sum(step * step, axis=0))
        u_norm = jnp.sqrt(total)
        old = weights[i][...]
        w_norm = jnp.sqrt(over_all(jnp.sum(old * old, axis=0)))
        norms[i : i + 1, 0:1] = w_norm
        norms[i : i + 1, 1:2] = u_norm
        ratio = RATE * (w_norm / (u_norm + EPS_ADAM))

        def renew(chunk, own=own, ratio=ratio, i=i):
            for _i, row, rows, lane, lanes, piece, start in own:
                at, to = slice(row, row + rows), slice(lane, lane + lanes)
                step = full[piece][places(orders[piece])[1](chunk), :, start : start + lanes]
                w_new[i][chunk, at, to] = weights[i][chunk, at, to] - ratio * step

        each(n, renew)
        if rows % 8 == 0:
            w_low[i][...] = w_new[i][...].reshape(n * rows, columns).astype(bf16)
        else:
            w_low[i][...] = jnp.zeros_like(w_low[i])
        for k, (src, dst) in enumerate(((w_new[i], w_out[i]), (w_low[i], low_out[i]))):
            leaving.append(pltpu.make_async_copy(src, dst, sems.at[2 * i + k]))
            leaving[-1].start()

    rows = full[1].shape[1]
    tail = full[1].shape[2] - 128
    for chunk in range(rows24.shape[0] // rows):
        rows24[chunk * rows : (chunk + 1) * rows, :] = full[1][places(orders[1])[1](chunk), :, tail:]

    def plain(weight, grad, first, second):
        momentum, variance = momenta(first, second, grad)
        return momentum, variance, weight - RATE_VEC * direction(momentum, variance)

    grad = jnp.concatenate([rows24[0:8, :], rows24[8:16, :]], axis=1)
    gvec[...] = grad
    mvec[...], vvec[...], wvec[...] = plain(vec[...], grad, fvec[...], svec[...])
    grad = rows24[16:24, :]
    gbias[...] = grad
    mbias[...], vbias[...], wbias[...] = plain(bias[...], grad, fbias[...], sbias[...])
    for copy in leaving:
        copy.wait()


def exchange(n, grads, weights, vectors, ffn_bias, firsts, seconds, others):
    far = list(range(1, n.bit_length() - 1))
    axes = [far[len(far) * p // 3 : len(far) * (p + 1) // 3] for p in range(3)]
    x, y, z = ([(b,) for b in axis] for axis in axes)
    walks = tuple(
        ((0,), *a, *b, *c) for a, b, c in ((x, y, z), (y, z, x), (z, x, y), (x, z, y), (y, x, z), (z, y, x))
    )
    orders = tuple(tuple(b for bits in walk for b in bits) for walk in walks)
    copies = 2 * sum((1 << len(bits)) - 1 for bits in walks[0])
    cut = lambda a: a.reshape(n, a.shape[0] // n, a.shape[1])
    sources, blocks = list(map(cut, grads)), list(map(cut, weights))
    flat = lambda a: a.reshape(-1, 128)
    vmem = pl.BlockSpec(memory_space=pltpu.VMEM)
    like = lambda a, dtype=f32: jax.ShapeDtypeStruct(a.shape, dtype)
    firsts, seconds = list(map(flat, firsts)), list(map(flat, seconds))
    operands = [*sources, *blocks, *firsts, *seconds]
    sizes = [
        (rows.stop - rows.start, lanes.stop - lanes.start) for _, rows, lanes in cut_pieces([s.shape for s in sources])
    ]
    shapes = [jax.ShapeDtypeStruct((n, *s), f32) for s in sizes] + [jax.ShapeDtypeStruct(s, f32) for s in sizes]
    reduced = pl.pallas_call(
        functools.partial(exchange_kernel, n, walks),
        out_shape=shapes,
        in_specs=[vmem] * len(operands),
        out_specs=[vmem] * len(shapes),
        scratch_shapes=[
            *[pltpu.VMEM((n // 2, *s), f32) for s in sizes],
            *[pltpu.VMEM((n, *s), f32) for s in sizes],
            pltpu.SemaphoreType.DMA((len(sizes), copies)),
            pltpu.SemaphoreType.DMA((len(sizes), copies)),
        ],
        compiler_params=pltpu.CompilerParams(
            collective_id=0, has_side_effects=True, vmem_limit_bytes=32 * 1024 * 1024
        ),
        name="exchange",
    )(*operands)
    line_bias = flat(ffn_bias)
    operands = [
        *reduced, *blocks, *firsts, *seconds, vectors, line_bias, others[0], others[1], flat(others[2]), flat(others[3]),
    ]
    moments = list(map(like, firsts))
    shapes = [
        *moments, *moments, *moments, *map(like, blocks), *[like(w, bf16) for w in weights],
        like(vectors), like(line_bias), *[like(vectors)] * 3, *[like(line_bias)] * 3, jax.ShapeDtypeStruct((4, 2), f32),
    ]
    results = pl.pallas_call(
        functools.partial(renew_kernel, n, orders),
        out_shape=shapes,
        in_specs=[vmem] * len(operands),
        out_specs=[vmem] * 12 + [pl.BlockSpec(memory_space=pl.ANY)] * 8 + [vmem] * 9,
        scratch_shapes=[
            pltpu.VMEM((24, 128), f32),
            *[pltpu.VMEM(b.shape, f32) for b in blocks],
            *[pltpu.VMEM(w.shape, bf16) for w in weights],
            pltpu.SemaphoreType.DMA((8,)),
        ],
        compiler_params=pltpu.CompilerParams(vmem_limit_bytes=32 * 1024 * 1024),
        name="renew",
    )(*operands)
    g, m, v = ([a.reshape(-1) for a in results[4 * i : 4 * i + 4]] for i in range(3))
    w = [new.reshape(old.shape) for new, old in zip(results[12:16], weights)]
    low = [new.astype(bf16) if block.shape[1] % 8 else own for new, own, block in zip(w, results[16:20], blocks)]
    gvec, gbias, mvec, vvec, wvec, mbias, vbias, wbias, norms = results[20:]
    line = lambda a: a.reshape(-1)
    steps = [entry for i in range(4) for entry in (m[i], v[i], w[i], low[i])]
    return (*g, gvec, line(gbias), *steps, mvec, vvec, wvec, line(mbias), line(vbias), line(wbias), norms)


def on_device(n, inputs, frames, cotangent, *rest):
    proj_in, proj_out, ffn_up, ffn_down, vectors, ffn_bias = rest[:6]
    moments, others = rest[6:14], rest[14:]
    block_out, grad_inputs, *grads = local_grads(
        inputs, frames, cotangent, proj_in, proj_out, ffn_up, ffn_down, vectors, ffn_bias
    )
    weights = (proj_in, proj_out, ffn_up, ffn_down)
    return (
        block_out,
        grad_inputs,
        *exchange(n, grads, weights, vectors, ffn_bias, moments[0::2], moments[1::2], others),
    )


def solution(mesh):
    split, rows, copied = P("dp"), P("dp", None), P()
    step = (split, split, copied, copied)
    return jax.shard_map(
        functools.partial(on_device, mesh.shape["dp"]),
        mesh=mesh,
        in_specs=(rows, rows, rows, *[copied] * 6, *[split] * 8, *[copied] * 4),
        out_specs=(rows, rows, *[split] * 4, copied, copied, *step * 4, *[copied] * 7),
        check_vma=False,
    )
```

```python
import functools
import math

import jax
import jax.numpy as jnp
from jax import lax
from jax.experimental import pallas as pl
from jax.experimental.pallas import tpu as pltpu
from jax.sharding import PartitionSpec as P

HEADS = 4
FRAME = 17
STEP = 10

EPS_NORM = 1e-05
EPS_ADAM = 1e-06
BETA = 0.5
DECAY = 0.01
RATE = 0.5
RATE_VEC = 0.2

TILE = 256
GROUP = 2
PROJECTED = 4
SLOTS = 2
LAG, LAG_BACK, LAG_FEED, LAG_PROJECT = 3, 2, 2, 1
QT = 128
SPAN = 384
LEAD = 16
REACH = 16
BIG = 1e30

f32 = jnp.float32
bf16 = jnp.bfloat16


def dot(a, b):
    return jnp.dot(a, b, preferred_element_type=f32)


def dot_nt(a, b):
    return lax.dot_general(a, b, (((1,), (1,)), ((), ())), preferred_element_type=f32)


def normalize(x):
    inv = 1.0 / x.shape[1]
    center = x - jnp.sum(x, axis=1, keepdims=True) * inv
    rstd = lax.rsqrt(jnp.sum(center * center, axis=1, keepdims=True) * inv + EPS_NORM)
    return center * rstd, rstd


def norm_back(dy, gain, n, rstd):
    inv = 1.0 / n.shape[1]
    e = dy * gain
    mean_e = jnp.sum(e, axis=1, keepdims=True) * inv
    mean_en = jnp.sum(e * n, axis=1, keepdims=True) * inv
    return rstd * (e - mean_e - n * mean_en)


def gelu_parts(x):
    t = pltpu.reciprocal(1.0 + jnp.abs(x) * (0.3275911 / math.sqrt(2.0)), approx=True)
    y = x * math.sqrt(0.5 / math.log(2.0))
    bell = jnp.exp2(-0.5 * math.log2(2.0 * math.pi) - y * y)
    unit = 0.5 * math.sqrt(2.0 * math.pi)
    poly = unit * 1.061405429
    for c in (-1.453152027, 1.421413741, -0.284496736, 0.254829592):
        poly = poly * t + unit * c
    tail = poly * t * bell
    cdf = jnp.where(x < 0.0, tail, 1.0 - tail)
    return x * cdf, cdf + x * bell


def stagger(work, stages, lag):
    held = {}
    for u in range(len(work) + lag * (len(stages) - 1)):
        for k, stage in enumerate(stages):
            at = u - k * lag
            if 0 <= at < len(work):
                held[at] = stage(work[at], held.get(at))


def fold8(x):
    return jnp.sum(x.reshape(x.shape[0] // 8, 8, x.shape[1]), axis=0)


def local_kernel(
    frames_hbm, x_hbm, cot_hbm, pin_hbm, pout_hbm, pup_hbm, pdown_hbm, vec_hbm, bias_hbm,
    bo_hbm, gi_hbm, ga_hbm, gup_hbm, gdown_hbm,
    frames_ref, pin_ref, pout_ref, pup_ref, pdown_ref, vec_ref, bias_ref, xs, cs, bos, qs, ks, vs, dq, dk, dv, dms, lse, dka, dva, counts, members, starts, win, wout, wup, wdown, ga_ref, gup_ref, gdown_ref, gdt, sums, bsum, sems, x_sems, gi_sems,
):
    rows, width = x_hbm.shape
    padded = xs.shape[0]
    steps = padded // TILE
    pairs = width // 128
    hidden_width = pup_hbm.shape[1]
    micro, packed = frames_hbm.shape

    piece = TILE * PROJECTED
    final = padded // piece - 1

    def by_piece(i, act, hbm, local, sems_, out=False):
        def at(start, size):
            ends = hbm.at[pl.ds(start, size)], local.at[pl.ds(start, size)]
            act(pltpu.make_async_copy(*(ends[::-1] if out else ends), sems_.at[i]))

        pl.when(i < final)(lambda: at(pl.multiple_of(i * piece, piece), piece))
        pl.when(i == final)(lambda: at(final * piece, rows - final * piece))

    begin, finish = lambda copy: copy.start(), lambda copy: copy.wait()
    loads = [
        pltpu.make_async_copy(src, dst, sems.at[k])
        for k, (src, dst) in enumerate(
            (
                (vec_hbm, vec_ref),
                (pin_hbm, pin_ref),
                (frames_hbm, frames_ref),
                (bias_hbm, bias_ref),
                (pout_hbm, pout_ref),
                (pup_hbm, pup_ref),
                (pdown_hbm, pdown_ref),
                (cot_hbm, cs.at[pl.ds(0, rows)]),
            )
        )
    ]
    for copy in loads[:2]:
        copy.start()
    for i in range(final + 1):
        by_piece(i, begin, x_hbm, xs, x_sems)
    for copy in loads[2:]:
        copy.start()

    gap = padded - rows
    if gap:
        xs[pl.ds(rows, gap)] = jnp.zeros((gap, width), bf16)
        cs[pl.ds(rows, gap)] = jnp.zeros((gap, width), f32)
        dq[pl.ds(rows, gap)] = jnp.zeros((gap, width), bf16)
    for ref in (qs, ks, vs, dms):
        ref[pl.ds(padded, SPAN)] = jnp.zeros((SPAN, width), bf16)
    for ref in (ga_ref, gup_ref, gdt, sums, bsum):
        ref[...] = jnp.zeros_like(ref)
    for copy in loads[:2]:
        copy.wait()
    win[...] = pin_ref[...].astype(bf16)

    gain_one, shift_one = vec_ref[3:4, :], vec_ref[4:5, :]
    gain_two, shift_two = vec_ref[5:6, :], vec_ref[6:7, :]

    def spot(i, g, group=GROUP):
        return pl.ds(pl.multiple_of((i * group + g) * TILE, TILE), TILE)

    def project(i, _):
        by_piece(i, finish, x_hbm, xs, x_sems)

        def even(g, _):
            n, _rstd = normalize(xs[spot(i, g, PROJECTED)].astype(f32))
            return (n * gain_one + shift_one).astype(bf16)

        def spread(g, h):
            return [dot(h, win[:, b * width : (b + 1) * width]) for b in range(3)]

        def keep(g, held):
            q, k, v = held
            at = spot(i, g, PROJECTED)
            qs[at] = (q + vec_ref[0:1, :]).astype(bf16) * jnp.array(0.125, bf16)
            ks[at] = k.astype(bf16)
            vs[at] = (v + vec_ref[1:2, :]).astype(bf16)

        stagger(list(range(PROJECTED)), (even, spread, keep), LAG_PROJECT)
        return 0

    lax.fori_loop(0, steps // PROJECTED, project, 0)

    for copy in loads[2:]:
        copy.wait()
    wout[...] = pout_ref[...].astype(bf16)
    wup[...] = pup_ref[...].astype(bf16)
    wdown[...] = pdown_ref[...].astype(bf16)

    first_head = lax.broadcasted_iota(jnp.int32, (1, 128), 1) < 64
    keep0 = first_head.astype(f32).astype(bf16)
    keep1 = 1.0 - keep0

    def depth(j):
        return min(QT * (j + 1) + REACH, SPAN)

    def filled(j):
        return min(-(-depth(j) // 128) * 128, SPAN)

    def limits(j, off, stop):
        t = QT * j + (lax.broadcasted_iota(jnp.int32, (1, 2 * QT), 1) & (QT - 1))
        frame = ((t - off) * 241) >> 12
        end = jnp.minimum(off + FRAME * (frame + 1), stop)
        return end, (t >= off) & (t < stop)

    def hide(score, j, off, end):
        m = score.shape[0]
        edge = QT * j
        row = lambda lo, hi: lo + lax.broadcasted_iota(jnp.int32, (hi - lo, 2 * QT), 0)
        if j == 0:
            s = row(0, m)
            return jnp.where((s >= off) & (s < end), score, -BIG)
        return jnp.concatenate(
            [
                jnp.where(row(0, LEAD) >= off, score[:LEAD], -BIG),
                score[LEAD:edge],
                jnp.where(row(edge, m) < end, score[edge:], -BIG),
            ],
            axis=0,
        )

    def heads_apart(block):
        return jnp.concatenate([block * keep0, block * keep1], axis=0)

    def fill(block, j):
        short = filled(j) - depth(j)
        if not short:
            return block
        return jnp.concatenate([block, jnp.zeros((short, block.shape[1]), block.dtype)], axis=0)

    def heads_back(out):
        both = jnp.concatenate([out[:64, :QT], out[64:, QT:]], axis=0)
        return both.T

    def put(ref, base, lanes, block, j, off, stop):
        at = pl.ds(pl.multiple_of(base + QT * j, LEAD), QT)
        own = lax.broadcasted_iota(jnp.int32, (QT, 128), 0)
        keep = own < stop - QT * j
        if j == 0:
            keep &= own >= off
        ref[at, lanes] = jnp.where(keep, block, ref[at, lanes].astype(f32)).astype(bf16)

    classes = SPAN // QT
    for c in range(classes):
        counts[c] = 0

    def sort(i, start):
        length = frames_ref[i // packed, i % packed] * FRAME
        tiles = ((start & (LEAD - 1)) + length + QT - 1) // QT - 1
        seat = counts[tiles]
        members[tiles, seat] = i
        counts[tiles] = seat + 1
        starts[i] = start
        return start + length

    lax.fori_loop(0, micro * packed, sort, 0)
    for c in range(classes - 1):
        odd = counts[c] & 1

        @pl.when(odd == 1)
        def _(c=c):
            members[c + 1, counts[c + 1]] = members[c, counts[c] - 1]
            counts[c + 1] = counts[c + 1] + 1

    def window(n, tiles):
        i = members[tiles - 1, n]
        start = starts[i]
        off = start & (LEAD - 1)
        stop = off + frames_ref[i // packed, i % packed] * FRAME
        return i, pl.multiple_of(start - off, LEAD), off, stop

    def units(tiles, n):
        windows = [window(SLOTS * n + slot, tiles) for slot in range(SLOTS)]
        for j in reversed(range(tiles)):
            for p in range(pairs):
                for slot in range(SLOTS):
                    yield slot, p, slice(128 * p, 128 * (p + 1)), j, windows[slot]

    def attend(tiles, n, _):
        todo, v_t = [], {}

        def compare(unit, _):
            _slot, _p, lanes, j, (_i, base, _off, _stop) = unit
            query = heads_apart(qs[pl.ds(pl.multiple_of(base + QT * j, LEAD), QT), lanes])
            return dot_nt(ks[pl.ds(base, depth(j)), lanes], query)

        def soften(unit, raw):
            slot, p, lanes, j, (i, base, off, stop) = unit
            end, valid = limits(j, off, stop)
            score = hide(raw, j, off, end)
            peak = jnp.max(score, axis=0, keepdims=True)
            weight = jnp.exp(score - peak)
            total = jnp.sum(weight, axis=0, keepdims=True)
            row = pairs * j + p
            lse[i, row : row + 1, :] = jnp.where(valid, peak + jnp.log(total), BIG)
            prob = (weight * jnp.where(valid, 1.0 / total, 0.0)).astype(bf16)
            if (slot, p) not in v_t:
                v_t[slot, p] = vs[pl.ds(base, filled(tiles - 1)), lanes].T
            return dot(v_t[slot, p][:, : filled(j)], fill(prob, j))

        def turn(unit, out):
            _slot, _p, lanes, j, (_i, base, off, stop) = unit
            todo.append((dq, base, lanes, heads_back(out), j, off, stop))

        stagger(list(units(tiles, n)), (compare, soften, turn), LAG)
        for entry in todo:
            put(*entry)
        return 0

    for tiles in range(1, classes + 1):
        lax.fori_loop(0, counts[tiles - 1] // SLOTS, functools.partial(attend, tiles), 0)

    ones = jnp.ones((16, TILE * GROUP), bf16)

    def join(blocks, axis):
        return jnp.concatenate(blocks, axis=axis)

    def feed_forward(i, _):
        state = []
        for g in range(GROUP):
            at = spot(i, g)
            mixed = dq[at]
            resid = xs[at].astype(f32) + dot(mixed, wout[...]) + vec_ref[2:3, :]
            n, rstd = normalize(resid)
            h = (n * gain_two + shift_two).astype(bf16)
            state.append((at, mixed, resid, n, rstd, h, cs[at].astype(bf16)))
        h_t = jnp.concatenate([join([e[5].T for e in state], 1), ones], axis=0)
        low_t = join([e[6].T for e in state], 1)
        feeds, d_hs, acts, d_pres = [None] * GROUP, [None] * GROUP, {}, {}

        def expand(unit, _):
            c, g = unit
            cols = slice(c, c + 256)
            return dot(state[g][5], wup[:, cols]), dot_nt(state[g][6], wdown[cols, :])

        def bend(unit, held):
            c, g = unit
            pre, d_act = held
            act, slope = gelu_parts(pre + bias_ref[:, c : c + 256])
            act = act.astype(bf16)
            d_pre = (d_act * slope).astype(bf16)
            acts[c, g], d_pres[c, g] = act, d_pre
            return act, d_pre

        def shrink(unit, held):
            c, g = unit
            act, d_pre = held
            cols = slice(c, c + 256)
            feed, d_h = dot(act, wdown[cols, :]), dot_nt(d_pre, wup[:, cols])
            feeds[g] = feed if feeds[g] is None else feeds[g] + feed
            d_hs[g] = d_h if d_hs[g] is None else d_hs[g] + d_h
            if g == GROUP - 1:
                act = join([acts.get((c, k)) for k in range(GROUP)], 0)
                d_pre = join([d_pres.get((c, k)) for k in range(GROUP)], 0)
                gdt[:, cols] += dot(low_t, act)
                both = dot(h_t, d_pre)
                gup_ref[:, cols] += both[:width]
                bsum[:, cols] += both[width : width + 8]

        stagger([(c, g) for c in range(0, hidden_width, 256) for g in range(GROUP)], (expand, bend, shrink), LAG_FEED)
        branches = []
        for g in range(GROUP):
            at, _mixed, resid, n, rstd, _h, _low = state[g]
            feed, d_h = feeds[g], d_hs[g]
            bos[at] = (resid + feed + vec_ref[7:8, :]).astype(bf16)
            d_resid = cs[at] + norm_back(d_h, gain_two, n, rstd)
            cs[at] = d_resid
            branch = d_resid.astype(bf16)
            branches.append(branch)
            sums[5] += fold8(d_h * n)
            sums[6] += fold8(d_h)
            dms[at] = dot_nt(branch, wout[...]).astype(bf16)
        mixed_t = jnp.concatenate([join([e[1].T for e in state], 1), ones], axis=0)
        both = dot(mixed_t, join(branches, 0))
        ga_ref[:, 3 * width : 4 * width] += both[:width]
        sums[2] += both[width : width + 8] * 0.125
        sums[7] += dot(ones, join([e[6] for e in state], 0))[:8] * 0.125
        return 0

    lax.fori_loop(0, steps // GROUP, feed_forward, 0)
    bo_out = pltpu.make_async_copy(bos.at[pl.ds(0, rows)], bo_hbm, sems.at[8])
    bo_out.start()
    for c in range(0, hidden_width, 256):
        gdown_ref[c : c + 256, :] = gdt[:, c : c + 256].T
    grads_out = [
        pltpu.make_async_copy(gup_ref, gup_hbm.at[pl.ds(0, width)], sems.at[9]),
        pltpu.make_async_copy(gdown_ref, gdown_hbm.at[pl.ds(0, hidden_width)], sems.at[10]),
    ]
    for copy in grads_out:
        copy.start()

    def attend_back(tiles, n, _):
        todo, k_t = [], {}

        def compare(unit, _):
            _slot, _p, lanes, j, (_i, base, _off, _stop) = unit
            here = pl.ds(pl.multiple_of(base + QT * j, LEAD), QT)
            query, d_out = heads_apart(qs[here, lanes]), heads_apart(dms[here, lanes])
            m = depth(j)
            return query, d_out, dot_nt(ks[pl.ds(base, m), lanes], query), dot_nt(vs[pl.ds(base, m), lanes], d_out)

        def soften(unit, held):
            slot, p, lanes, j, (i, base, off, stop) = unit
            query, d_out, raw, d_prob = held
            end, _valid = limits(j, off, stop)
            row = pairs * j + p
            prob = jnp.exp(hide(raw, j, off, end) - lse[i, row : row + 1, :])
            delta = jnp.sum(prob * d_prob, axis=0, keepdims=True)
            d_score = (prob * (d_prob - delta)).astype(bf16)
            if (slot, p) not in k_t:
                k_t[slot, p] = ks[pl.ds(base, filled(tiles - 1)), lanes].T
            out = dot(k_t[slot, p][:, : filled(j)], fill(d_score, j))
            return dot(prob.astype(bf16), d_out), dot(d_score, query), out

        def collect(unit, held):
            slot, _p, lanes, j, (_i, base, off, stop) = unit
            d_val, d_key, out = held
            m = depth(j)
            first = j == tiles - 1
            dva[slot, :m, lanes] = d_val if first else dva[slot, :m, lanes] + d_val
            dka[slot, :m, lanes] = d_key if first else dka[slot, :m, lanes] + d_key
            todo.append((dq, base, lanes, heads_back(out) * 0.125, j, off, stop))

        stagger(list(units(tiles, n)), (compare, soften, collect), LAG_BACK)
        for entry in todo:
            put(*entry)
        for slot, p, lanes, j, (i, base, off, stop) in units(tiles, n):
            at = slice(QT * j, QT * (j + 1))
            put(dv, base, lanes, dva[slot, at, lanes], j, off, stop)
            put(dk, base, lanes, dka[slot, at, lanes], j, off, stop)
        return 0

    for tiles in range(1, classes + 1):
        lax.fori_loop(0, counts[tiles - 1] // SLOTS, functools.partial(attend_back, tiles), 0)
    if gap:
        for ref in (dq, dk, dv):
            ref[pl.ds(rows, gap)] = jnp.zeros((gap, width), bf16)

    def project_back(i, _):
        turned, blocks = {}, {}

        def even(g, _):
            n, rstd = normalize(xs[spot(i, g, PROJECTED)].astype(f32))
            turned[g] = (n * gain_one + shift_one).astype(bf16).T
            return n, rstd

        def spread(g, held):
            d_h = None
            for b, ref in enumerate((dq, dk, dv)):
                block = ref[spot(i, g, PROJECTED)]
                blocks[b, g] = block
                part = dot_nt(block, win[:, b * width : (b + 1) * width])
                d_h = part if d_h is None else d_h + part
            return *held, d_h

        def keep(g, held):
            n, rstd, d_h = held
            sums[3] += fold8(d_h * n)
            sums[4] += fold8(d_h)
            at = spot(i, g, PROJECTED)
            cs[at] = cs[at] + norm_back(d_h, gain_one, n, rstd)
            if g == PROJECTED - 1:
                h_t = jnp.concatenate([join([turned[k] for k in range(PROJECTED)], 1), jnp.ones((16, TILE * PROJECTED), bf16)], axis=0)
                for b in range(3):
                    both = dot(h_t, join([blocks[b, k] for k in range(PROJECTED)], 0))
                    ga_ref[:, b * width : (b + 1) * width] += both[:width]
                    if b != 1:
                        sums[b // 2] += both[width : width + 8] * 0.125

        stagger(list(range(PROJECTED)), (even, spread, keep), LAG_PROJECT)
        by_piece(i, begin, gi_hbm, cs, gi_sems, out=True)
        return 0

    lax.fori_loop(0, steps // PROJECTED, project_back, 0)
    vec = jnp.sum(sums[...], axis=1)
    tail = 4 * width
    for b in range(width // 128):
        ga_ref[8 * b : 8 * b + 8, tail : tail + 128] = vec[:, 128 * b : 128 * (b + 1)]
    bias = bsum[0:1, :]
    for b in range(hidden_width // 128):
        row = 8 * (width // 128) + b
        ga_ref[row : row + 1, tail : tail + 128] = bias[:, 128 * b : 128 * (b + 1)]
    grads_out.append(pltpu.make_async_copy(ga_ref, ga_hbm.at[pl.ds(0, width)], sems.at[11]))
    grads_out[-1].start()
    for copy in (bo_out, *grads_out):
        copy.wait()
    for i in range(final + 1):
        by_piece(i, finish, gi_hbm, cs, gi_sems, out=True)


def local_grads(spare, inputs, frames, cotangent, proj_in, proj_out, ffn_up, ffn_down, vectors, ffn_bias):
    rows, width = inputs.shape
    hidden_width = ffn_up.shape[1]
    step = TILE * max(GROUP, PROJECTED)
    padded = -(-rows // step) * step
    wide = padded + SPAN
    pairs = width // 128
    hbm = pl.BlockSpec(memory_space=pltpu.HBM)
    bias = ffn_bias.reshape(1, hidden_width)
    return pl.pallas_call(
        local_kernel,
        out_shape=(
            jax.ShapeDtypeStruct((rows, width), bf16),
            jax.ShapeDtypeStruct((rows, width), f32),
            jax.ShapeDtypeStruct((spare * width, 4 * width + 128), f32),
            jax.ShapeDtypeStruct((spare * width, hidden_width), f32),
            jax.ShapeDtypeStruct((spare * hidden_width, width), f32),
        ),
        in_specs=[hbm] * 9,
        out_specs=(hbm,) * 5,
        scratch_shapes=[
            pltpu.SMEM(frames.shape, jnp.int32),
            *[pltpu.VMEM(a.shape, f32) for a in (proj_in, proj_out, ffn_up, ffn_down, vectors, bias)],
            pltpu.VMEM((padded, width), bf16),
            pltpu.VMEM((padded, width), f32),
            pltpu.VMEM((padded, width), bf16),
            *[pltpu.VMEM((wide, width), bf16)] * 7,
            pltpu.VMEM((frames.size, 8, 2 * QT), f32),
            pltpu.VMEM((2, SPAN, width), f32),
            pltpu.VMEM((2, SPAN, width), f32),
            pltpu.SMEM((SPAN // QT,), jnp.int32),
            pltpu.SMEM((SPAN // QT, frames.size + 1), jnp.int32),
            pltpu.SMEM((frames.size,), jnp.int32),
            pltpu.VMEM((width, 3 * width), bf16),
            pltpu.VMEM((width, width), bf16),
            pltpu.VMEM((width, hidden_width), bf16),
            pltpu.VMEM((hidden_width, width), bf16),
            pltpu.VMEM((width, 4 * width + 128), f32),
            pltpu.VMEM((width, hidden_width), f32),
            pltpu.VMEM((hidden_width, width), f32),
            pltpu.VMEM((width, hidden_width), f32),
            pltpu.VMEM((8, 8, width), f32),
            pltpu.VMEM((8, hidden_width), f32),
            pltpu.SemaphoreType.DMA((12,)),
            *[pltpu.SemaphoreType.DMA((padded // (TILE * PROJECTED),))] * 2,
        ],
        compiler_params=pltpu.CompilerParams(vmem_limit_bytes=60 * 1024 * 1024),
        name="local_grads",
    )(frames, inputs, cotangent, proj_in, proj_out, ffn_up, ffn_down, vectors, bias)


def over_all(x):
    return jnp.sum(jnp.sum(x, axis=0, keepdims=True), axis=1, keepdims=True)


def momenta(first, second, grad):
    return BETA * first + (1.0 - BETA) * grad, BETA * second + (1.0 - BETA) * grad * grad


def direction(momentum, variance):
    fix = 1.0 - BETA**STEP
    return momentum / fix / (jnp.sqrt(variance / fix) + EPS_ADAM)


def places(order):
    top = len(order) - 1

    def chunk_of(pos):
        return sum((pos // (1 << (top - k))) % 2 * (1 << b) for k, b in enumerate(order))

    def place_of(chunk):
        return sum((chunk // (1 << b)) % 2 * (1 << (top - k)) for k, b in enumerate(order))

    return chunk_of, place_of


def each(count, body, block=32):
    block = min(count, block)
    if count == block:
        for i in range(count):
            body(i)
        return

    def some(outer, _):
        for i in range(block):
            body(outer * block + i)
        return 0

    lax.fori_loop(0, count // block, some, 0)


def cut_pieces(shapes):
    wide, tall = shapes[1][2] // 2, shapes[2][1] // 2
    return (
        (0, slice(0, shapes[0][1]), slice(0, 640)),
        (0, slice(0, shapes[0][1]), slice(640, shapes[0][2])),
        (1, slice(0, shapes[1][1]), slice(0, wide)),
        (1, slice(0, shapes[1][1]), slice(wide, 2 * wide)),
        (2, slice(0, tall), slice(0, shapes[2][2])),
        (2, slice(tall, 2 * tall), slice(0, shapes[2][2])),
    )


def cut_matrices(shapes):
    (_, r_in, w_in), (_, _, w_out), (_, r_up, w_up), (_, r_down, w_down) = shapes
    rest = w_in - 640
    return (
        (0, 0, r_in, 0, 640, 0, 0),
        (0, 0, r_in, 640, rest, 1, 0),
        (1, 0, r_in, 0, w_out, 1, rest),
        (2, 0, r_up, 0, w_up // 2, 2, 0),
        (2, 0, r_up, w_up // 2, w_up // 2, 3, 0),
        (3, 0, r_down // 2, 0, w_down, 4, 0),
        (3, r_down // 2, r_down // 2, 0, w_down, 5, 0),
    )


def flat_rows(first, rows, blocks, b):
    return pl.ds(first * blocks + b, rows, stride=blocks)


def exchange_kernel(n, walks, *refs):
    count, stages = len(walks), len(walks[0])
    grads, owns, firsts, seconds = refs[:3], refs[3:7], refs[7:11], refs[11:15]
    full, shares = refs[15 : 15 + count], refs[15 + count : 15 + 2 * count]
    parcels, landed = refs[15 + 2 * count : 15 + 3 * count], refs[15 + 3 * count : 15 + 4 * count]
    sources, (send_sems, recv_sems, load_sems) = refs[15 + 4 * count : 18 + 4 * count], refs[18 + 4 * count :]
    pieces = cut_pieces([s.shape for s in sources])
    orders = [[b for bits in walk for b in bits] for walk in walks]
    me = lax.axis_index("dp")

    def bit(k):
        return (me // (1 << k)) % 2

    def flips(bits):
        return [[b for j, b in enumerate(bits) if t >> j & 1] for t in range(1, 1 << len(bits))]

    def other(flip):
        return me + sum((1 - 2 * bit(b)) * (1 << b) for b in flip)

    def digit(bits, flip=()):
        top = len(bits) - 1
        return sum((1 - bit(b) if b in flip else bit(b)) * (1 << (top - j)) for j, b in enumerate(bits))

    def left(p, k):
        return n >> sum(len(bits) for bits in walks[p][: k + 1])

    def slot(p, k):
        return n - left(p, k - 1) if k else 0

    loads = [
        pltpu.make_async_copy(grad.at[pl.ds(0, n)], source, load_sems.at[k])
        for k, (grad, source) in enumerate(zip(grads, sources))
    ]
    for copy in loads:
        copy.start()
    barrier = pltpu.get_barrier_semaphore()
    met = sorted({tuple(sorted(flip)) for walk in walks for bits in walk for flip in flips(bits)})
    for flip in met:
        pl.semaphore_signal(barrier, inc=1, device_id=(other(flip),), device_id_type=pl.DeviceIdType.MESH)
    pl.semaphore_wait(barrier, len(met))

    sent, used = [], [0] * count

    def remote(p, src, dst, flip):
        copy = pltpu.make_async_remote_copy(
            src_ref=src,
            dst_ref=dst,
            send_sem=send_sems.at[p, used[p]],
            recv_sem=recv_sems.at[p, used[p]],
            device_id=(other(flip),),
            device_id_type=pl.DeviceIdType.MESH,
        )
        used[p] += 1
        copy.start()
        sent.append(copy)
        return copy

    def chunk_of(p, i, first):
        return places(orders[p][1:])[0](i) + first * (1 << orders[p][0])

    arriving = {}

    def split(p, k):
        m, bits = left(p, k), walks[p][k]
        copies = []
        for t, flip in enumerate(flips(bits)):
            if k == 0:
                source, rows, lanes = pieces[p]

                def pack(i):
                    parcels[p][i] = sources[source][chunk_of(p, i, 1 - bit(bits[0])), rows, lanes]

                each(m, pack)
                src = parcels[p]
            else:
                src = landed[p].at[pl.ds(slot(p, k - 1) + digit(bits, flip) * m, m)]
            copies.append(remote(p, src, landed[p].at[pl.ds(slot(p, k) + t * m, m)], flip))
        arriving[p, k] = copies

    def add(p, k):
        m, bits = left(p, k), walks[p][k]
        for copy in arriving[p, k]:
            copy.wait_recv()
        new = pl.ds(slot(p, k), m)
        if k:
            total = landed[p][pl.ds(slot(p, k - 1) + digit(bits) * m, m)]
            for t in range(len(arriving[p, k])):
                total = total + landed[p][pl.ds(slot(p, k) + t * m, m)]
            landed[p][new] = total
            return
        source, rows, lanes = pieces[p]

        def one(i):
            landed[p][i] = landed[p][i] + sources[source][chunk_of(p, i, bit(bits[0])), rows, lanes]

        each(m, one)

    parts = range(count)
    for p in parts:
        if pieces[p][0] not in [source for source, _, _ in pieces[:p]]:
            loads[pieces[p][0]].wait()
        split(p, 0)
    for k in range(1, stages):
        for p in parts:
            add(p, k - 1)
            split(p, k)

    homes = [places(order)[1](me) for order in orders]
    matrices = cut_matrices([own.shape for own in owns])

    def gather(p, k):
        m = left(p, k)
        at = pl.ds(homes[p] // m * m, m)
        arriving[p, stages + k] = [
            remote(p, full[p].at[at], full[p].at[at], flip) for flip in flips(walks[p][k])
        ]

    last = stages - 1
    for p in parts:
        add(p, last)
        share = slot(p, last)
        for i, row, rows, lane, lanes, piece, start in matrices:
            if piece != p:
                continue
            blocks = owns[i].shape[2] // 128
            for b in range(lanes // 128):
                flat = flat_rows(row, rows, blocks, lane // 128 + b)
                here = slice(start + 128 * b, start + 128 * (b + 1))
                own = owns[i][me, row : row + rows, lane + 128 * b : lane + 128 * (b + 1)]
                momentum, variance = momenta(firsts[i][flat, :], seconds[i][flat, :], landed[p][share, :, here])
                full[p][homes[p], :, here] = direction(momentum, variance) + DECAY * own
        if p == 1:
            tail = slice(full[1].shape[2] - 128, full[1].shape[2])
            full[1][homes[1], :, tail] = landed[1][share, :, tail]
        shares[p][...] = landed[p][share]
        gather(p, last)
    for k in range(last - 1, -1, -1):
        for p in parts:
            for copy in arriving[p, stages + k + 1]:
                copy.wait_recv()
            gather(p, k)
    for p in parts:
        for copy in arriving[p, stages]:
            copy.wait_recv()
    for copy in sent:
        copy.wait_send()


def renew_kernel(n, orders, *refs):
    count = len(orders)
    full, shares, refs = refs[:count], refs[count : 2 * count], refs[2 * count :]
    weights, firsts, seconds = refs[:4], refs[4:8], refs[8:12]
    vec, bias, fvec, svec, fbias, sbias = refs[12:18]
    g_out, m_out, v_out = refs[18:22], refs[22:26], refs[26:30]
    w_out, low_out = refs[30:34], refs[34:38]
    gvec, gbias, mvec, vvec, wvec, mbias, vbias, wbias, norms = refs[38:47]
    rows24, w_new, w_low, sems = refs[47], refs[48:52], refs[52:56], refs[56]
    matrices = cut_matrices([w.shape for w in weights])
    for i, row, rows, lane, lanes, piece, start in matrices:
        blocks = weights[i].shape[2] // 128
        for b in range(lanes // 128):
            flat = flat_rows(row, rows, blocks, lane // 128 + b)
            g = shares[piece][:, start + 128 * b : start + 128 * (b + 1)]
            g_out[i][flat, :] = g
            m_out[i][flat, :], v_out[i][flat, :] = momenta(firsts[i][flat, :], seconds[i][flat, :], g)
    leaving = []
    for i in (2, 3, 0, 1):
        _, rows, columns = weights[i].shape
        own = [entry for entry in matrices if entry[0] == i]
        total = 0.0
        for _i, _row, _rows, _lane, lanes, piece, start in own:
            step = full[piece][:, :, start : start + lanes]
            total = total + over_all(jnp.sum(step * step, axis=0))
        u_norm = jnp.sqrt(total)
        old = weights[i][...]
        w_norm = jnp.sqrt(over_all(jnp.sum(old * old, axis=0)))
        norms[0:1, i : i + 1] = w_norm
        norms[1:2, i : i + 1] = u_norm
        ratio = RATE * (w_norm / (u_norm + EPS_ADAM))

        def renew(chunk, own=own, ratio=ratio, i=i):
            for _i, row, rows, lane, lanes, piece, start in own:
                at, to = slice(row, row + rows), slice(lane, lane + lanes)
                step = full[piece][places(orders[piece])[1](chunk), :, start : start + lanes]
                w_new[i][chunk, at, to] = weights[i][chunk, at, to] - ratio * step

        each(n, renew)
        if rows % 8 == 0:
            w_low[i][...] = w_new[i][...].reshape(n * rows, columns).astype(bf16)
        else:
            w_low[i][...] = jnp.zeros_like(w_low[i])
        for k, (src, dst) in enumerate(((w_new[i], w_out[i]), (w_low[i], low_out[i]))):
            leaving.append(pltpu.make_async_copy(src, dst, sems.at[2 * i + k]))
            leaving[-1].start()

    rows = full[1].shape[1]
    tail = full[1].shape[2] - 128
    for chunk in range(rows24.shape[0] // rows):
        rows24[chunk * rows : (chunk + 1) * rows, :] = full[1][places(orders[1])[1](chunk), :, tail:]

    def plain(weight, grad, first, second):
        momentum, variance = momenta(first, second, grad)
        return momentum, variance, weight - RATE_VEC * direction(momentum, variance)

    grad = jnp.concatenate([rows24[0:8, :], rows24[8:16, :]], axis=1)
    gvec[...] = grad
    mvec[...], vvec[...], wvec[...] = plain(vec[...], grad, fvec[...], svec[...])
    grad = rows24[16:24, :]
    gbias[...] = grad
    mbias[...], vbias[...], wbias[...] = plain(bias[...], grad, fbias[...], sbias[...])
    for copy in leaving:
        copy.wait()


def exchange(n, spare, grads, weights, vectors, ffn_bias, firsts, seconds, others):
    far = list(range(1, n.bit_length() - 1))
    axes = [far[len(far) * p // 3 : len(far) * (p + 1) // 3] for p in range(3)]
    x, y, z = ([(b,) for b in axis] for axis in axes)
    walks = tuple(
        ((0,), *a, *b, *c) for a, b, c in ((x, y, z), (y, z, x), (z, x, y), (x, z, y), (y, x, z), (z, y, x))
    )
    if len(far) == 4:
        sets = ("xyab", "yxba", "ayxb", "xayb", "ybxa", "bxya")
        walks = tuple(((0,), *((far["xyab".index(c)],) for c in order)) for order in sets)
    orders = tuple(tuple(b for bits in walk for b in bits) for walk in walks)
    copies = 2 * sum((1 << len(bits)) - 1 for bits in walks[0])
    cut = lambda a: a.reshape(n, a.shape[0] // n, a.shape[1])
    blocks = list(map(cut, weights))
    chunks = [(g.shape[0] // (n * spare), g.shape[1]) for g in grads]
    sources = [g.reshape(n * spare, *chunk) for g, chunk in zip(grads, chunks)]
    held = [(n, *chunk) for chunk in chunks]
    flat = lambda a: a.reshape(-1, 128)
    vmem = pl.BlockSpec(memory_space=pltpu.VMEM)
    like = lambda a, dtype=f32: jax.ShapeDtypeStruct(a.shape, dtype)
    firsts, seconds = list(map(flat, firsts)), list(map(flat, seconds))
    operands = [*sources, *blocks, *firsts, *seconds]
    sizes = [
        (rows.stop - rows.start, lanes.stop - lanes.start) for _, rows, lanes in cut_pieces(held)
    ]
    shapes = [jax.ShapeDtypeStruct((n, *s), f32) for s in sizes] + [jax.ShapeDtypeStruct(s, f32) for s in sizes]
    reduced = pl.pallas_call(
        functools.partial(exchange_kernel, n, walks),
        out_shape=shapes,
        in_specs=[pl.BlockSpec(memory_space=pl.ANY)] * 3 + [vmem] * 12,
        out_specs=[vmem] * len(shapes),
        scratch_shapes=[
            *[pltpu.VMEM((n // 2, *s), f32) for s in sizes],
            *[pltpu.VMEM((n, *s), f32) for s in sizes],
            *[pltpu.VMEM(shape, f32) for shape in held],
            pltpu.SemaphoreType.DMA((len(sizes), copies)),
            pltpu.SemaphoreType.DMA((len(sizes), copies)),
            pltpu.SemaphoreType.DMA((3,)),
        ],
        compiler_params=pltpu.CompilerParams(
            collective_id=0, has_side_effects=True, vmem_limit_bytes=44 * 1024 * 1024
        ),
        name="exchange",
    )(*operands)
    line_bias = flat(ffn_bias)
    operands = [
        *reduced, *blocks, *firsts, *seconds, vectors, line_bias, others[0], others[1], flat(others[2]), flat(others[3]),
    ]
    moments = list(map(like, firsts))
    shapes = [
        *moments, *moments, *moments, *map(like, blocks), *[like(w, bf16) for w in weights],
        like(vectors), like(line_bias), *[like(vectors)] * 3, *[like(line_bias)] * 3, jax.ShapeDtypeStruct((2, 4), f32),
    ]
    results = pl.pallas_call(
        functools.partial(renew_kernel, n, orders),
        out_shape=shapes,
        in_specs=[vmem] * len(operands),
        out_specs=[vmem] * 12 + [pl.BlockSpec(memory_space=pl.ANY)] * 8 + [vmem] * 9,
        scratch_shapes=[
            pltpu.VMEM((24, 128), f32),
            *[pltpu.VMEM(b.shape, f32) for b in blocks],
            *[pltpu.VMEM(w.shape, bf16) for w in weights],
            pltpu.SemaphoreType.DMA((8,)),
        ],
        compiler_params=pltpu.CompilerParams(vmem_limit_bytes=32 * 1024 * 1024),
        name="renew",
    )(*operands)
    g, m, v = ([a.reshape(-1) for a in results[4 * i : 4 * i + 4]] for i in range(3))
    w = [new.reshape(old.shape) for new, old in zip(results[12:16], weights)]
    low = [new.astype(bf16) if block.shape[1] % 8 else own for new, own, block in zip(w, results[16:20], blocks)]
    gvec, gbias, mvec, vvec, wvec, mbias, vbias, wbias, norms = results[20:]
    line = lambda a: a.reshape(-1)
    steps = [entry for i in range(4) for entry in (m[i], v[i], w[i], low[i])]
    return (*g, gvec, line(gbias), *steps, mvec, vvec, wvec, line(mbias), line(vbias), line(wbias), norms.T)


def on_device(n, inputs, frames, cotangent, *rest):
    proj_in, proj_out, ffn_up, ffn_down, vectors, ffn_bias = rest[:6]
    moments, others = rest[6:14], rest[14:]
    spare = 24 if proj_in.shape[0] % (8 * n) == 0 else 1
    block_out, grad_inputs, *grads = local_grads(
        spare, inputs, frames, cotangent, proj_in, proj_out, ffn_up, ffn_down, vectors, ffn_bias
    )
    weights = (proj_in, proj_out, ffn_up, ffn_down)
    return (
        block_out,
        grad_inputs,
        *exchange(n, spare, grads, weights, vectors, ffn_bias, moments[0::2], moments[1::2], others),
    )


def solution(mesh):
    split, rows, copied = P("dp"), P("dp", None), P()
    step = (split, split, copied, copied)
    return jax.shard_map(
        functools.partial(on_device, mesh.shape["dp"]),
        mesh=mesh,
        in_specs=(rows, rows, rows, *[copied] * 6, *[split] * 8, *[copied] * 4),
        out_specs=(rows, rows, *[split] * 4, copied, copied, *step * 4, *[copied] * 7),
        check_vma=False,
    )
```

```python
import functools
import math

import jax
import jax.numpy as jnp
from jax import lax
from jax.experimental import pallas as pl
from jax.experimental.pallas import tpu as pltpu
from jax.sharding import PartitionSpec as P

HEADS = 4
FRAME = 17
STEP = 10

EPS_NORM = 1e-05
EPS_ADAM = 1e-06
BETA = 0.5
DECAY = 0.01
RATE = 0.5
RATE_VEC = 0.2

TILE = 256
GROUP = 2
PROJECTED = 4
SLOTS = 2
LAG, LAG_BACK, LAG_FEED, LAG_PROJECT = 3, 2, 2, 1
QT = 128
SPAN = 384
LEAD = 16
REACH = 16
BIG = 1e30

f32 = jnp.float32
bf16 = jnp.bfloat16


def dot(a, b):
    return jnp.dot(a, b, preferred_element_type=f32)


def dot_nt(a, b):
    return lax.dot_general(a, b, (((1,), (1,)), ((), ())), preferred_element_type=f32)


def normalize(x):
    inv = 1.0 / x.shape[1]
    center = x - jnp.sum(x, axis=1, keepdims=True) * inv
    rstd = lax.rsqrt(jnp.sum(center * center, axis=1, keepdims=True) * inv + EPS_NORM)
    return center * rstd, rstd


def norm_back(dy, gain, n, rstd):
    inv = 1.0 / n.shape[1]
    e = dy * gain
    mean_e = jnp.sum(e, axis=1, keepdims=True) * inv
    mean_en = jnp.sum(e * n, axis=1, keepdims=True) * inv
    return rstd * (e - mean_e - n * mean_en)


def gelu_parts(x):
    t = pltpu.reciprocal(1.0 + jnp.abs(x) * (0.3275911 / math.sqrt(2.0)), approx=True)
    y = x * math.sqrt(0.5 / math.log(2.0))
    bell = jnp.exp2(-0.5 * math.log2(2.0 * math.pi) - y * y)
    unit = 0.5 * math.sqrt(2.0 * math.pi)
    poly = unit * 1.061405429
    for c in (-1.453152027, 1.421413741, -0.284496736, 0.254829592):
        poly = poly * t + unit * c
    tail = poly * t * bell
    cdf = jnp.where(x < 0.0, tail, 1.0 - tail)
    return x * cdf, cdf + x * bell


def stagger(work, stages, lag):
    held = {}
    for u in range(len(work) + lag * (len(stages) - 1)):
        for k, stage in enumerate(stages):
            at = u - k * lag
            if 0 <= at < len(work):
                held[at] = stage(work[at], held.get(at))


def fold8(x):
    return jnp.sum(x.reshape(x.shape[0] // 8, 8, x.shape[1]), axis=0)


def local_kernel(
    frames_hbm, x_hbm, cot_hbm, pin_hbm, pout_hbm, pup_hbm, pdown_hbm, vec_hbm, bias_hbm,
    bo_hbm, gi_hbm, ga_hbm, gup_hbm, gdown_hbm,
    frames_ref, pin_ref, pout_ref, pup_ref, pdown_ref, vec_ref, bias_ref, xs, cs, bos, qs, ks, vs, dq, dk, dv, dms, lse, dka, dva, counts, members, starts, win, wout, wup, wdown, ga_ref, gup_ref, gdown_ref, gdt, sums, bsum, sems, x_sems, gi_sems,
):
    rows, width = x_hbm.shape
    padded = xs.shape[0]
    steps = padded // TILE
    pairs = width // 128
    hidden_width = pup_hbm.shape[1]
    micro, packed = frames_hbm.shape

    piece = TILE * PROJECTED
    final = padded // piece - 1

    def by_piece(i, act, hbm, local, sems_, out=False):
        def at(start, size):
            ends = hbm.at[pl.ds(start, size)], local.at[pl.ds(start, size)]
            act(pltpu.make_async_copy(*(ends[::-1] if out else ends), sems_.at[i]))

        pl.when(i < final)(lambda: at(pl.multiple_of(i * piece, piece), piece))
        pl.when(i == final)(lambda: at(final * piece, rows - final * piece))

    begin, finish = lambda copy: copy.start(), lambda copy: copy.wait()
    loads = [
        pltpu.make_async_copy(src, dst, sems.at[k])
        for k, (src, dst) in enumerate(
            (
                (vec_hbm, vec_ref),
                (pin_hbm, pin_ref),
                (frames_hbm, frames_ref),
                (bias_hbm, bias_ref),
                (pout_hbm, pout_ref),
                (pup_hbm, pup_ref),
                (pdown_hbm, pdown_ref),
                (cot_hbm, cs.at[pl.ds(0, rows)]),
            )
        )
    ]
    for copy in loads[:2]:
        copy.start()
    for i in range(final + 1):
        by_piece(i, begin, x_hbm, xs, x_sems)
    for copy in loads[2:]:
        copy.start()

    gap = padded - rows
    if gap:
        xs[pl.ds(rows, gap)] = jnp.zeros((gap, width), bf16)
        cs[pl.ds(rows, gap)] = jnp.zeros((gap, width), f32)
        dq[pl.ds(rows, gap)] = jnp.zeros((gap, width), bf16)
    for ref in (qs, ks, vs, dms):
        ref[pl.ds(padded, SPAN)] = jnp.zeros((SPAN, width), bf16)
    for ref in (ga_ref, gup_ref, gdt, sums, bsum):
        ref[...] = jnp.zeros_like(ref)
    for copy in loads[:2]:
        copy.wait()
    win[...] = pin_ref[...].astype(bf16)

    gain_one, shift_one = vec_ref[3:4, :], vec_ref[4:5, :]
    gain_two, shift_two = vec_ref[5:6, :], vec_ref[6:7, :]

    def spot(i, g, group=GROUP):
        return pl.ds(pl.multiple_of((i * group + g) * TILE, TILE), TILE)

    def project(i, _):
        by_piece(i, finish, x_hbm, xs, x_sems)

        def even(g, _):
            n, _rstd = normalize(xs[spot(i, g, PROJECTED)].astype(f32))
            return (n * gain_one + shift_one).astype(bf16)

        def spread(g, h):
            return [dot(h, win[:, b * width : (b + 1) * width]) for b in range(3)]

        def keep(g, held):
            q, k, v = held
            at = spot(i, g, PROJECTED)
            qs[at] = (q + vec_ref[0:1, :]).astype(bf16) * jnp.array(0.125, bf16)
            ks[at] = k.astype(bf16)
            vs[at] = (v + vec_ref[1:2, :]).astype(bf16)

        stagger(list(range(PROJECTED)), (even, spread, keep), LAG_PROJECT)
        return 0

    lax.fori_loop(0, steps // PROJECTED, project, 0)

    for copy in loads[2:]:
        copy.wait()
    wout[...] = pout_ref[...].astype(bf16)
    wup[...] = pup_ref[...].astype(bf16)
    wdown[...] = pdown_ref[...].astype(bf16)

    first_head = lax.broadcasted_iota(jnp.int32, (1, 128), 1) < 64
    keep0 = first_head.astype(f32).astype(bf16)
    keep1 = 1.0 - keep0

    def depth(j):
        return min(QT * (j + 1) + REACH, SPAN)

    def filled(j):
        return min(-(-depth(j) // 128) * 128, SPAN)

    def limits(j, off, stop):
        t = QT * j + (lax.broadcasted_iota(jnp.int32, (1, 2 * QT), 1) & (QT - 1))
        frame = ((t - off) * 241) >> 12
        end = jnp.minimum(off + FRAME * (frame + 1), stop)
        return end, (t >= off) & (t < stop)

    def hide(score, j, off, end):
        m = score.shape[0]
        edge = QT * j
        row = lambda lo, hi: lo + lax.broadcasted_iota(jnp.int32, (hi - lo, 2 * QT), 0)
        if j == 0:
            s = row(0, m)
            return jnp.where((s >= off) & (s < end), score, -BIG)
        return jnp.concatenate(
            [
                jnp.where(row(0, LEAD) >= off, score[:LEAD], -BIG),
                score[LEAD:edge],
                jnp.where(row(edge, m) < end, score[edge:], -BIG),
            ],
            axis=0,
        )

    def heads_apart(block):
        return jnp.concatenate([block * keep0, block * keep1], axis=0)

    def fill(block, j):
        short = filled(j) - depth(j)
        if not short:
            return block
        return jnp.concatenate([block, jnp.zeros((short, block.shape[1]), block.dtype)], axis=0)

    def heads_back(out):
        both = jnp.concatenate([out[:64, :QT], out[64:, QT:]], axis=0)
        return both.T

    def put(ref, base, lanes, block, j, off, stop):
        at = pl.ds(pl.multiple_of(base + QT * j, LEAD), QT)
        own = lax.broadcasted_iota(jnp.int32, (QT, 128), 0)
        keep = own < stop - QT * j
        if j == 0:
            keep &= own >= off
        ref[at, lanes] = jnp.where(keep, block, ref[at, lanes].astype(f32)).astype(bf16)

    classes = SPAN // QT
    for c in range(classes):
        counts[c] = 0

    def sort(i, start):
        length = frames_ref[i // packed, i % packed] * FRAME
        tiles = ((start & (LEAD - 1)) + length + QT - 1) // QT - 1
        seat = counts[tiles]
        members[tiles, seat] = i
        counts[tiles] = seat + 1
        starts[i] = start
        return start + length

    lax.fori_loop(0, micro * packed, sort, 0)
    for c in range(classes - 1):
        odd = counts[c] & 1

        @pl.when(odd == 1)
        def _(c=c):
            members[c + 1, counts[c + 1]] = members[c, counts[c] - 1]
            counts[c + 1] = counts[c + 1] + 1

    def window(n, tiles):
        i = members[tiles - 1, n]
        start = starts[i]
        off = start & (LEAD - 1)
        stop = off + frames_ref[i // packed, i % packed] * FRAME
        return i, pl.multiple_of(start - off, LEAD), off, stop

    def units(tiles, n):
        windows = [window(SLOTS * n + slot, tiles) for slot in range(SLOTS)]
        for j in reversed(range(tiles)):
            for p in range(pairs):
                for slot in range(SLOTS):
                    yield slot, p, slice(128 * p, 128 * (p + 1)), j, windows[slot]

    def attend(tiles, n, _):
        todo, v_t = [], {}

        def compare(unit, _):
            _slot, _p, lanes, j, (_i, base, _off, _stop) = unit
            query = heads_apart(qs[pl.ds(pl.multiple_of(base + QT * j, LEAD), QT), lanes])
            return dot_nt(ks[pl.ds(base, depth(j)), lanes], query)

        def soften(unit, raw):
            slot, p, lanes, j, (i, base, off, stop) = unit
            end, valid = limits(j, off, stop)
            score = hide(raw, j, off, end)
            peak = jnp.max(score, axis=0, keepdims=True)
            weight = jnp.exp(score - peak)
            total = jnp.sum(weight, axis=0, keepdims=True)
            row = pairs * j + p
            lse[i, row : row + 1, :] = jnp.where(valid, peak + jnp.log(total), BIG)
            prob = (weight * jnp.where(valid, 1.0 / total, 0.0)).astype(bf16)
            if (slot, p) not in v_t:
                v_t[slot, p] = vs[pl.ds(base, filled(tiles - 1)), lanes].T
            return dot(v_t[slot, p][:, : filled(j)], fill(prob, j))

        def turn(unit, out):
            _slot, _p, lanes, j, (_i, base, off, stop) = unit
            todo.append((dq, base, lanes, heads_back(out), j, off, stop))

        stagger(list(units(tiles, n)), (compare, soften, turn), LAG)
        for entry in todo:
            put(*entry)
        return 0

    for tiles in range(1, classes + 1):
        lax.fori_loop(0, counts[tiles - 1] // SLOTS, functools.partial(attend, tiles), 0)

    ones = jnp.ones((16, TILE * GROUP), bf16)

    def join(blocks, axis):
        return jnp.concatenate(blocks, axis=axis)

    def feed_forward(i, _):
        state = []
        for g in range(GROUP):
            at = spot(i, g)
            mixed = dq[at]
            resid = xs[at].astype(f32) + dot(mixed, wout[...]) + vec_ref[2:3, :]
            n, rstd = normalize(resid)
            h = (n * gain_two + shift_two).astype(bf16)
            state.append((at, mixed, resid, n, rstd, h, cs[at].astype(bf16)))
        h_t = jnp.concatenate([join([e[5].T for e in state], 1), ones], axis=0)
        low_t = join([e[6].T for e in state], 1)
        feeds, d_hs, acts, d_pres = [None] * GROUP, [None] * GROUP, {}, {}

        def expand(unit, _):
            c, g = unit
            cols = slice(c, c + 256)
            return dot(state[g][5], wup[:, cols]), dot_nt(state[g][6], wdown[cols, :])

        def bend(unit, held):
            c, g = unit
            pre, d_act = held
            act, slope = gelu_parts(pre + bias_ref[:, c : c + 256])
            act = act.astype(bf16)
            d_pre = (d_act * slope).astype(bf16)
            acts[c, g], d_pres[c, g] = act, d_pre
            return act, d_pre

        def shrink(unit, held):
            c, g = unit
            act, d_pre = held
            cols = slice(c, c + 256)
            feed, d_h = dot(act, wdown[cols, :]), dot_nt(d_pre, wup[:, cols])
            feeds[g] = feed if feeds[g] is None else feeds[g] + feed
            d_hs[g] = d_h if d_hs[g] is None else d_hs[g] + d_h
            if g == GROUP - 1:
                act = join([acts.get((c, k)) for k in range(GROUP)], 0)
                d_pre = join([d_pres.get((c, k)) for k in range(GROUP)], 0)
                gdt[:, cols] += dot(low_t, act)
                both = dot(h_t, d_pre)
                gup_ref[:, cols] += both[:width]
                bsum[:, cols] += both[width : width + 8]

        stagger([(c, g) for c in range(0, hidden_width, 256) for g in range(GROUP)], (expand, bend, shrink), LAG_FEED)
        branches = []
        for g in range(GROUP):
            at, _mixed, resid, n, rstd, _h, _low = state[g]
            feed, d_h = feeds[g], d_hs[g]
            bos[at] = (resid + feed + vec_ref[7:8, :]).astype(bf16)
            d_resid = cs[at] + norm_back(d_h, gain_two, n, rstd)
            cs[at] = d_resid
            branch = d_resid.astype(bf16)
            branches.append(branch)
            sums[5] += fold8(d_h * n)
            sums[6] += fold8(d_h)
            dms[at] = dot_nt(branch, wout[...]).astype(bf16)
        mixed_t = jnp.concatenate([join([e[1].T for e in state], 1), ones], axis=0)
        both = dot(mixed_t, join(branches, 0))
        ga_ref[:, 3 * width : 4 * width] += both[:width]
        sums[2] += both[width : width + 8] * 0.125
        sums[7] += dot(ones, join([e[6] for e in state], 0))[:8] * 0.125
        return 0

    lax.fori_loop(0, steps // GROUP, feed_forward, 0)
    bo_out = pltpu.make_async_copy(bos.at[pl.ds(0, rows)], bo_hbm, sems.at[8])
    bo_out.start()
    for c in range(0, hidden_width, 256):
        gdown_ref[c : c + 256, :] = gdt[:, c : c + 256].T
    grads_out = [
        pltpu.make_async_copy(gup_ref, gup_hbm.at[pl.ds(0, width)], sems.at[9]),
        pltpu.make_async_copy(gdown_ref, gdown_hbm.at[pl.ds(0, hidden_width)], sems.at[10]),
    ]
    for copy in grads_out:
        copy.start()

    def attend_back(tiles, n, _):
        todo, k_t = [], {}

        def compare(unit, _):
            _slot, _p, lanes, j, (_i, base, _off, _stop) = unit
            here = pl.ds(pl.multiple_of(base + QT * j, LEAD), QT)
            query, d_out = heads_apart(qs[here, lanes]), heads_apart(dms[here, lanes])
            m = depth(j)
            return query, d_out, dot_nt(ks[pl.ds(base, m), lanes], query), dot_nt(vs[pl.ds(base, m), lanes], d_out)

        def soften(unit, held):
            slot, p, lanes, j, (i, base, off, stop) = unit
            query, d_out, raw, d_prob = held
            end, _valid = limits(j, off, stop)
            row = pairs * j + p
            prob = jnp.exp(hide(raw, j, off, end) - lse[i, row : row + 1, :])
            delta = jnp.sum(prob * d_prob, axis=0, keepdims=True)
            d_score = (prob * (d_prob - delta)).astype(bf16)
            if (slot, p) not in k_t:
                k_t[slot, p] = ks[pl.ds(base, filled(tiles - 1)), lanes].T
            out = dot(k_t[slot, p][:, : filled(j)], fill(d_score, j))
            return dot(prob.astype(bf16), d_out), dot(d_score, query), out

        def collect(unit, held):
            slot, _p, lanes, j, (_i, base, off, stop) = unit
            d_val, d_key, out = held
            m = depth(j)
            first = j == tiles - 1
            dva[slot, :m, lanes] = d_val if first else dva[slot, :m, lanes] + d_val
            dka[slot, :m, lanes] = d_key if first else dka[slot, :m, lanes] + d_key
            todo.append((dq, base, lanes, heads_back(out) * 0.125, j, off, stop))

        stagger(list(units(tiles, n)), (compare, soften, collect), LAG_BACK)
        for entry in todo:
            put(*entry)
        for slot, p, lanes, j, (i, base, off, stop) in units(tiles, n):
            at = slice(QT * j, QT * (j + 1))
            put(dv, base, lanes, dva[slot, at, lanes], j, off, stop)
            put(dk, base, lanes, dka[slot, at, lanes], j, off, stop)
        return 0

    for tiles in range(1, classes + 1):
        lax.fori_loop(0, counts[tiles - 1] // SLOTS, functools.partial(attend_back, tiles), 0)
    if gap:
        for ref in (dq, dk, dv):
            ref[pl.ds(rows, gap)] = jnp.zeros((gap, width), bf16)

    def project_back(i, _):
        turned, blocks = {}, {}

        def even(g, _):
            n, rstd = normalize(xs[spot(i, g, PROJECTED)].astype(f32))
            turned[g] = (n * gain_one + shift_one).astype(bf16).T
            return n, rstd

        def spread(g, held):
            d_h = None
            for b, ref in enumerate((dq, dk, dv)):
                block = ref[spot(i, g, PROJECTED)]
                blocks[b, g] = block
                part = dot_nt(block, win[:, b * width : (b + 1) * width])
                d_h = part if d_h is None else d_h + part
            return *held, d_h

        def keep(g, held):
            n, rstd, d_h = held
            sums[3] += fold8(d_h * n)
            sums[4] += fold8(d_h)
            at = spot(i, g, PROJECTED)
            cs[at] = cs[at] + norm_back(d_h, gain_one, n, rstd)
            if g == PROJECTED - 1:
                h_t = jnp.concatenate([join([turned[k] for k in range(PROJECTED)], 1), jnp.ones((16, TILE * PROJECTED), bf16)], axis=0)
                for b in range(3):
                    both = dot(h_t, join([blocks[b, k] for k in range(PROJECTED)], 0))
                    ga_ref[:, b * width : (b + 1) * width] += both[:width]
                    if b != 1:
                        sums[b // 2] += both[width : width + 8] * 0.125

        stagger(list(range(PROJECTED)), (even, spread, keep), LAG_PROJECT)
        by_piece(i, begin, gi_hbm, cs, gi_sems, out=True)
        return 0

    lax.fori_loop(0, steps // PROJECTED, project_back, 0)
    vec = jnp.sum(sums[...], axis=1)
    tail = 4 * width
    for b in range(width // 128):
        ga_ref[8 * b : 8 * b + 8, tail : tail + 128] = vec[:, 128 * b : 128 * (b + 1)]
    bias = bsum[0:1, :]
    for b in range(hidden_width // 128):
        row = 8 * (width // 128) + b
        ga_ref[row : row + 1, tail : tail + 128] = bias[:, 128 * b : 128 * (b + 1)]
    grads_out.append(pltpu.make_async_copy(ga_ref, ga_hbm.at[pl.ds(0, width)], sems.at[11]))
    grads_out[-1].start()
    for copy in (bo_out, *grads_out):
        copy.wait()
    for i in range(final + 1):
        by_piece(i, finish, gi_hbm, cs, gi_sems, out=True)


def local_grads(spare, inputs, frames, cotangent, proj_in, proj_out, ffn_up, ffn_down, vectors, ffn_bias):
    rows, width = inputs.shape
    hidden_width = ffn_up.shape[1]
    step = TILE * max(GROUP, PROJECTED)
    padded = -(-rows // step) * step
    wide = padded + SPAN
    pairs = width // 128
    hbm = pl.BlockSpec(memory_space=pltpu.HBM)
    bias = ffn_bias.reshape(1, hidden_width)
    return pl.pallas_call(
        local_kernel,
        out_shape=(
            jax.ShapeDtypeStruct((rows, width), bf16),
            jax.ShapeDtypeStruct((rows, width), f32),
            jax.ShapeDtypeStruct((spare * width, 4 * width + 128), f32),
            jax.ShapeDtypeStruct((spare * width, hidden_width), f32),
            jax.ShapeDtypeStruct((spare * hidden_width, width), f32),
        ),
        in_specs=[hbm] * 9,
        out_specs=(hbm,) * 5,
        scratch_shapes=[
            pltpu.SMEM(frames.shape, jnp.int32),
            *[pltpu.VMEM(a.shape, f32) for a in (proj_in, proj_out, ffn_up, ffn_down, vectors, bias)],
            pltpu.VMEM((padded, width), bf16),
            pltpu.VMEM((padded, width), f32),
            pltpu.VMEM((padded, width), bf16),
            *[pltpu.VMEM((wide, width), bf16)] * 7,
            pltpu.VMEM((frames.size, 8, 2 * QT), f32),
            pltpu.VMEM((2, SPAN, width), f32),
            pltpu.VMEM((2, SPAN, width), f32),
            pltpu.SMEM((SPAN // QT,), jnp.int32),
            pltpu.SMEM((SPAN // QT, frames.size + 1), jnp.int32),
            pltpu.SMEM((frames.size,), jnp.int32),
            pltpu.VMEM((width, 3 * width), bf16),
            pltpu.VMEM((width, width), bf16),
            pltpu.VMEM((width, hidden_width), bf16),
            pltpu.VMEM((hidden_width, width), bf16),
            pltpu.VMEM((width, 4 * width + 128), f32),
            pltpu.VMEM((width, hidden_width), f32),
            pltpu.VMEM((hidden_width, width), f32),
            pltpu.VMEM((width, hidden_width), f32),
            pltpu.VMEM((8, 8, width), f32),
            pltpu.VMEM((8, hidden_width), f32),
            pltpu.SemaphoreType.DMA((12,)),
            *[pltpu.SemaphoreType.DMA((padded // (TILE * PROJECTED),))] * 2,
        ],
        compiler_params=pltpu.CompilerParams(vmem_limit_bytes=60 * 1024 * 1024),
        name="local_grads",
    )(frames, inputs, cotangent, proj_in, proj_out, ffn_up, ffn_down, vectors, bias)


def over_all(x):
    return jnp.sum(jnp.sum(x, axis=0, keepdims=True), axis=1, keepdims=True)


def momenta(first, second, grad):
    return BETA * first + (1.0 - BETA) * grad, BETA * second + (1.0 - BETA) * grad * grad


def direction(momentum, variance):
    fix = 1.0 - BETA**STEP
    return momentum / fix / (jnp.sqrt(variance / fix) + EPS_ADAM)


def places(order):
    top = len(order) - 1

    def chunk_of(pos):
        return sum((pos // (1 << (top - k))) % 2 * (1 << b) for k, b in enumerate(order))

    def place_of(chunk):
        return sum((chunk // (1 << b)) % 2 * (1 << (top - k)) for k, b in enumerate(order))

    return chunk_of, place_of


def each(count, body, block=32):
    block = min(count, block)
    if count == block:
        for i in range(count):
            body(i)
        return

    def some(outer, _):
        for i in range(block):
            body(outer * block + i)
        return 0

    lax.fori_loop(0, count // block, some, 0)


def cut_pieces(shapes):
    wide, tall = shapes[1][2] // 2, shapes[2][1] // 2
    return (
        (0, slice(0, shapes[0][1]), slice(0, 640)),
        (0, slice(0, shapes[0][1]), slice(640, shapes[0][2])),
        (1, slice(0, shapes[1][1]), slice(0, wide)),
        (1, slice(0, shapes[1][1]), slice(wide, 2 * wide)),
        (2, slice(0, tall), slice(0, shapes[2][2])),
        (2, slice(tall, 2 * tall), slice(0, shapes[2][2])),
    )


def cut_matrices(shapes):
    (_, r_in, w_in), (_, _, w_out), (_, r_up, w_up), (_, r_down, w_down) = shapes
    rest = w_in - 640
    return (
        (0, 0, r_in, 0, 640, 0, 0),
        (0, 0, r_in, 640, rest, 1, 0),
        (1, 0, r_in, 0, w_out, 1, rest),
        (2, 0, r_up, 0, w_up // 2, 2, 0),
        (2, 0, r_up, w_up // 2, w_up // 2, 3, 0),
        (3, 0, r_down // 2, 0, w_down, 4, 0),
        (3, r_down // 2, r_down // 2, 0, w_down, 5, 0),
    )


def flat_rows(first, rows, blocks, b):
    return pl.ds(first * blocks + b, rows, stride=blocks)


def exchange_kernel(n, walks, *refs):
    count, stages = len(walks), len(walks[0])
    grads, owns, firsts, seconds = refs[:3], refs[3:7], refs[7:11], refs[11:15]
    full, shares = refs[15 : 15 + count], refs[15 + count : 15 + 2 * count]
    parcels, landed = refs[15 + 2 * count : 15 + 3 * count], refs[15 + 3 * count : 15 + 4 * count]
    sources, (send_sems, recv_sems, load_sems) = refs[15 + 4 * count : 18 + 4 * count], refs[18 + 4 * count :]
    pieces = cut_pieces([s.shape for s in sources])
    orders = [[b for bits in walk for b in bits] for walk in walks]
    me = lax.axis_index("dp")

    def bit(k):
        return (me // (1 << k)) % 2

    def flips(bits):
        return [[b for j, b in enumerate(bits) if t >> j & 1] for t in range(1, 1 << len(bits))]

    def other(flip):
        return me + sum((1 - 2 * bit(b)) * (1 << b) for b in flip)

    def digit(bits, flip=()):
        top = len(bits) - 1
        return sum((1 - bit(b) if b in flip else bit(b)) * (1 << (top - j)) for j, b in enumerate(bits))

    def left(p, k):
        return n >> sum(len(bits) for bits in walks[p][: k + 1])

    def slot(p, k):
        return n - left(p, k - 1) if k else 0

    quarters = [pl.ds(q * n // 4, n // 4) for q in range(4)]
    loads = [
        [pltpu.make_async_copy(grad.at[at], source.at[at], load_sems.at[k, q]) for q, at in enumerate(quarters)]
        for k, (grad, source) in enumerate(zip(grads, sources))
    ]
    for copy in (copy for group in loads for copy in group):
        copy.start()
    barrier = pltpu.get_barrier_semaphore()
    met = sorted({tuple(sorted(flip)) for walk in walks for bits in walk for flip in flips(bits)})
    for flip in met:
        pl.semaphore_signal(barrier, inc=1, device_id=(other(flip),), device_id_type=pl.DeviceIdType.MESH)
    pl.semaphore_wait(barrier, len(met))

    sent, used = [], [0] * count

    def remote(p, src, dst, flip):
        copy = pltpu.make_async_remote_copy(
            src_ref=src,
            dst_ref=dst,
            send_sem=send_sems.at[p, used[p]],
            recv_sem=recv_sems.at[p, used[p]],
            device_id=(other(flip),),
            device_id_type=pl.DeviceIdType.MESH,
        )
        used[p] += 1
        copy.start()
        sent.append(copy)
        return copy

    def chunk_of(p, i, first):
        return places(orders[p][1:])[0](i) + first * (1 << orders[p][0])

    arriving = {}

    def split(p, k):
        m, bits = left(p, k), walks[p][k]
        copies = []
        for t, flip in enumerate(flips(bits)):
            if k == 0:
                source, rows, lanes = pieces[p]

                def pack(i):
                    parcels[p][i] = sources[source][chunk_of(p, i, 1 - bit(bits[0])), rows, lanes]

                each(m, pack)
                src = parcels[p]
            else:
                src = landed[p].at[pl.ds(slot(p, k - 1) + digit(bits, flip) * m, m)]
            copies.append(remote(p, src, landed[p].at[pl.ds(slot(p, k) + t * m, m)], flip))
        arriving[p, k] = copies

    def add(p, k):
        m, bits = left(p, k), walks[p][k]
        for copy in arriving[p, k]:
            copy.wait_recv()
        new = pl.ds(slot(p, k), m)
        if k:
            total = landed[p][pl.ds(slot(p, k - 1) + digit(bits) * m, m)]
            for t in range(len(arriving[p, k])):
                total = total + landed[p][pl.ds(slot(p, k) + t * m, m)]
            landed[p][new] = total
            return
        source, rows, lanes = pieces[p]

        def one(i):
            landed[p][i] = landed[p][i] + sources[source][chunk_of(p, i, bit(bits[0])), rows, lanes]

        each(m, one)

    parts = range(count)
    for p in parts:
        if pieces[p][0] not in [source for source, _, _ in pieces[:p]]:
            for copy in loads[pieces[p][0]]:
                copy.wait()
        split(p, 0)
    for k in range(1, stages):
        for p in parts:
            add(p, k - 1)
            split(p, k)

    homes = [places(order)[1](me) for order in orders]
    matrices = cut_matrices([own.shape for own in owns])

    def gather(p, k):
        m = left(p, k)
        at = pl.ds(homes[p] // m * m, m)
        arriving[p, stages + k] = [
            remote(p, full[p].at[at], full[p].at[at], flip) for flip in flips(walks[p][k])
        ]

    last = stages - 1
    for p in parts:
        add(p, last)
        share = slot(p, last)
        for i, row, rows, lane, lanes, piece, start in matrices:
            if piece != p:
                continue
            blocks = owns[i].shape[2] // 128
            for b in range(lanes // 128):
                flat = flat_rows(row, rows, blocks, lane // 128 + b)
                here = slice(start + 128 * b, start + 128 * (b + 1))
                own = owns[i][me, row : row + rows, lane + 128 * b : lane + 128 * (b + 1)]
                momentum, variance = momenta(firsts[i][flat, :], seconds[i][flat, :], landed[p][share, :, here])
                full[p][homes[p], :, here] = direction(momentum, variance) + DECAY * own
        if p == 1:
            tail = slice(full[1].shape[2] - 128, full[1].shape[2])
            full[1][homes[1], :, tail] = landed[1][share, :, tail]
        shares[p][...] = landed[p][share]
        gather(p, last)
    for k in range(last - 1, -1, -1):
        for p in parts:
            for copy in arriving[p, stages + k + 1]:
                copy.wait_recv()
            gather(p, k)
    for p in parts:
        for copy in arriving[p, stages]:
            copy.wait_recv()
    for copy in sent:
        copy.wait_send()


def renew_kernel(n, orders, *refs):
    count = len(orders)
    full, shares, refs = refs[:count], refs[count : 2 * count], refs[2 * count :]
    weights, firsts, seconds = refs[:4], refs[4:8], refs[8:12]
    vec, bias, fvec, svec, fbias, sbias = refs[12:18]
    g_out, m_out, v_out = refs[18:22], refs[22:26], refs[26:30]
    w_out, low_out = refs[30:34], refs[34:38]
    gvec, gbias, mvec, vvec, wvec, mbias, vbias, wbias, norms = refs[38:47]
    rows24, w_new, w_low, sems = refs[47], refs[48:52], refs[52:56], refs[56]
    matrices = cut_matrices([w.shape for w in weights])
    for i, row, rows, lane, lanes, piece, start in matrices:
        blocks = weights[i].shape[2] // 128
        for b in range(lanes // 128):
            flat = flat_rows(row, rows, blocks, lane // 128 + b)
            g = shares[piece][:, start + 128 * b : start + 128 * (b + 1)]
            g_out[i][flat, :] = g
            m_out[i][flat, :], v_out[i][flat, :] = momenta(firsts[i][flat, :], seconds[i][flat, :], g)
    leaving = []
    for i in (2, 3, 0, 1):
        _, rows, columns = weights[i].shape
        own = [entry for entry in matrices if entry[0] == i]
        total = 0.0
        for _i, _row, _rows, _lane, lanes, piece, start in own:
            step = full[piece][:, :, start : start + lanes]
            total = total + over_all(jnp.sum(step * step, axis=0))
        u_norm = jnp.sqrt(total)
        old = weights[i][...]
        w_norm = jnp.sqrt(over_all(jnp.sum(old * old, axis=0)))
        norms[0:1, i : i + 1] = w_norm
        norms[1:2, i : i + 1] = u_norm
        ratio = RATE * (w_norm / (u_norm + EPS_ADAM))

        def renew(chunk, own=own, ratio=ratio, i=i):
            for _i, row, rows, lane, lanes, piece, start in own:
                at, to = slice(row, row + rows), slice(lane, lane + lanes)
                step = full[piece][places(orders[piece])[1](chunk), :, start : start + lanes]
                w_new[i][chunk, at, to] = weights[i][chunk, at, to] - ratio * step

        each(n, renew)
        if rows % 8 == 0:
            w_low[i][...] = w_new[i][...].reshape(n * rows, columns).astype(bf16)
        else:
            w_low[i][...] = jnp.zeros_like(w_low[i])
        for k, (src, dst) in enumerate(((w_new[i], w_out[i]), (w_low[i], low_out[i]))):
            leaving.append(pltpu.make_async_copy(src, dst, sems.at[2 * i + k]))
            leaving[-1].start()

    rows = full[1].shape[1]
    tail = full[1].shape[2] - 128
    for chunk in range(rows24.shape[0] // rows):
        rows24[chunk * rows : (chunk + 1) * rows, :] = full[1][places(orders[1])[1](chunk), :, tail:]

    def plain(weight, grad, first, second):
        momentum, variance = momenta(first, second, grad)
        return momentum, variance, weight - RATE_VEC * direction(momentum, variance)

    grad = jnp.concatenate([rows24[0:8, :], rows24[8:16, :]], axis=1)
    gvec[...] = grad
    mvec[...], vvec[...], wvec[...] = plain(vec[...], grad, fvec[...], svec[...])
    grad = rows24[16:24, :]
    gbias[...] = grad
    mbias[...], vbias[...], wbias[...] = plain(bias[...], grad, fbias[...], sbias[...])
    for copy in leaving:
        copy.wait()


def exchange(n, spare, grads, weights, vectors, ffn_bias, firsts, seconds, others):
    far = list(range(1, n.bit_length() - 1))
    axes = [far[len(far) * p // 3 : len(far) * (p + 1) // 3] for p in range(3)]
    x, y, z = ([(b,) for b in axis] for axis in axes)
    walks = tuple(
        ((0,), *a, *b, *c) for a, b, c in ((x, y, z), (y, z, x), (z, x, y), (x, z, y), (y, x, z), (z, y, x))
    )
    if len(far) == 4:
        sets = ("xyab", "yxba", "ayxb", "xayb", "ybxa", "bxya")
        walks = tuple(((0,), *((far["xyab".index(c)],) for c in order)) for order in sets)
    orders = tuple(tuple(b for bits in walk for b in bits) for walk in walks)
    copies = 2 * sum((1 << len(bits)) - 1 for bits in walks[0])
    cut = lambda a: a.reshape(n, a.shape[0] // n, a.shape[1])
    blocks = list(map(cut, weights))
    chunks = [(g.shape[0] // (n * spare), g.shape[1]) for g in grads]
    sources = [g.reshape(n * spare, *chunk) for g, chunk in zip(grads, chunks)]
    held = [(n, *chunk) for chunk in chunks]
    flat = lambda a: a.reshape(-1, 128)
    vmem = pl.BlockSpec(memory_space=pltpu.VMEM)
    like = lambda a, dtype=f32: jax.ShapeDtypeStruct(a.shape, dtype)
    firsts, seconds = list(map(flat, firsts)), list(map(flat, seconds))
    operands = [*sources, *blocks, *firsts, *seconds]
    sizes = [
        (rows.stop - rows.start, lanes.stop - lanes.start) for _, rows, lanes in cut_pieces(held)
    ]
    shapes = [jax.ShapeDtypeStruct((n, *s), f32) for s in sizes] + [jax.ShapeDtypeStruct(s, f32) for s in sizes]
    reduced = pl.pallas_call(
        functools.partial(exchange_kernel, n, walks),
        out_shape=shapes,
        in_specs=[pl.BlockSpec(memory_space=pl.ANY)] * 3 + [vmem] * 12,
        out_specs=[vmem] * len(shapes),
        scratch_shapes=[
            *[pltpu.VMEM((n // 2, *s), f32) for s in sizes],
            *[pltpu.VMEM((n, *s), f32) for s in sizes],
            *[pltpu.VMEM(shape, f32) for shape in held],
            pltpu.SemaphoreType.DMA((len(sizes), copies)),
            pltpu.SemaphoreType.DMA((len(sizes), copies)),
            pltpu.SemaphoreType.DMA((3, 4)),
        ],
        compiler_params=pltpu.CompilerParams(
            collective_id=0, has_side_effects=True, vmem_limit_bytes=44 * 1024 * 1024
        ),
        name="exchange",
    )(*operands)
    line_bias = flat(ffn_bias)
    operands = [
        *reduced, *blocks, *firsts, *seconds, vectors, line_bias, others[0], others[1], flat(others[2]), flat(others[3]),
    ]
    moments = list(map(like, firsts))
    shapes = [
        *moments, *moments, *moments, *map(like, blocks), *[like(w, bf16) for w in weights],
        like(vectors), like(line_bias), *[like(vectors)] * 3, *[like(line_bias)] * 3, jax.ShapeDtypeStruct((2, 4), f32),
    ]
    results = pl.pallas_call(
        functools.partial(renew_kernel, n, orders),
        out_shape=shapes,
        in_specs=[vmem] * len(operands),
        out_specs=[vmem] * 12 + [pl.BlockSpec(memory_space=pl.ANY)] * 8 + [vmem] * 9,
        scratch_shapes=[
            pltpu.VMEM((24, 128), f32),
            *[pltpu.VMEM(b.shape, f32) for b in blocks],
            *[pltpu.VMEM(w.shape, bf16) for w in weights],
            pltpu.SemaphoreType.DMA((8,)),
        ],
        compiler_params=pltpu.CompilerParams(vmem_limit_bytes=32 * 1024 * 1024),
        name="renew",
    )(*operands)
    g, m, v = ([a.reshape(-1) for a in results[4 * i : 4 * i + 4]] for i in range(3))
    w = [new.reshape(old.shape) for new, old in zip(results[12:16], weights)]
    low = [new.astype(bf16) if block.shape[1] % 8 else own for new, own, block in zip(w, results[16:20], blocks)]
    gvec, gbias, mvec, vvec, wvec, mbias, vbias, wbias, norms = results[20:]
    line = lambda a: a.reshape(-1)
    steps = [entry for i in range(4) for entry in (m[i], v[i], w[i], low[i])]
    return (*g, gvec, line(gbias), *steps, mvec, vvec, wvec, line(mbias), line(vbias), line(wbias), norms.T)


def on_device(n, inputs, frames, cotangent, *rest):
    proj_in, proj_out, ffn_up, ffn_down, vectors, ffn_bias = rest[:6]
    moments, others = rest[6:14], rest[14:]
    spare = 24 if proj_in.shape[0] % (8 * n) == 0 else 1
    block_out, grad_inputs, *grads = local_grads(
        spare, inputs, frames, cotangent, proj_in, proj_out, ffn_up, ffn_down, vectors, ffn_bias
    )
    weights = (proj_in, proj_out, ffn_up, ffn_down)
    return (
        block_out,
        grad_inputs,
        *exchange(n, spare, grads, weights, vectors, ffn_bias, moments[0::2], moments[1::2], others),
    )


def solution(mesh):
    split, rows, copied = P("dp"), P("dp", None), P()
    step = (split, split, copied, copied)
    return jax.shard_map(
        functools.partial(on_device, mesh.shape["dp"]),
        mesh=mesh,
        in_specs=(rows, rows, rows, *[copied] * 6, *[split] * 8, *[copied] * 4),
        out_specs=(rows, rows, *[split] * 4, copied, copied, *step * 4, *[copied] * 7),
        check_vma=False,
    )
```

```python
import functools
import math

import jax
import jax.numpy as jnp
from jax import lax
from jax.experimental import pallas as pl
from jax.experimental.pallas import tpu as pltpu
from jax.sharding import PartitionSpec as P

HEADS = 4
FRAME = 17
STEP = 10

EPS_NORM = 1e-05
EPS_ADAM = 1e-06
BETA = 0.5
DECAY = 0.01
RATE = 0.5
RATE_VEC = 0.2

TILE = 256
GROUP = 2
PROJECTED = 4
SLOTS = 2
LAG, LAG_BACK, LAG_FEED, LAG_PROJECT = 3, 2, 2, 1
QT = 128
SPAN = 384
LEAD = 16
REACH = 16
BIG = 1e30

f32 = jnp.float32
bf16 = jnp.bfloat16


def dot(a, b):
    return jnp.dot(a, b, preferred_element_type=f32)


def dot_nt(a, b):
    return lax.dot_general(a, b, (((1,), (1,)), ((), ())), preferred_element_type=f32)


def normalize(x):
    inv = 1.0 / x.shape[1]
    center = x - jnp.sum(x, axis=1, keepdims=True) * inv
    rstd = lax.rsqrt(jnp.sum(center * center, axis=1, keepdims=True) * inv + EPS_NORM)
    return center * rstd, rstd


def norm_back(dy, gain, n, rstd):
    inv = 1.0 / n.shape[1]
    e = dy * gain
    mean_e = jnp.sum(e, axis=1, keepdims=True) * inv
    mean_en = jnp.sum(e * n, axis=1, keepdims=True) * inv
    return rstd * (e - mean_e - n * mean_en)


def gelu_parts(x):
    t = pltpu.reciprocal(1.0 + jnp.abs(x) * (0.3275911 / math.sqrt(2.0)), approx=True)
    y = x * math.sqrt(0.5 / math.log(2.0))
    bell = jnp.exp2(-0.5 * math.log2(2.0 * math.pi) - y * y)
    unit = 0.5 * math.sqrt(2.0 * math.pi)
    poly = unit * 1.061405429
    for c in (-1.453152027, 1.421413741, -0.284496736, 0.254829592):
        poly = poly * t + unit * c
    tail = poly * t * bell
    cdf = jnp.where(x < 0.0, tail, 1.0 - tail)
    return x * cdf, cdf + x * bell


def stagger(work, stages, lag):
    held = {}
    for u in range(len(work) + lag * (len(stages) - 1)):
        for k, stage in enumerate(stages):
            at = u - k * lag
            if 0 <= at < len(work):
                held[at] = stage(work[at], held.get(at))


def fold8(x):
    return jnp.sum(x.reshape(x.shape[0] // 8, 8, x.shape[1]), axis=0)


def local_kernel(
    frames_hbm, x_hbm, cot_hbm, pin_hbm, pout_hbm, pup_hbm, pdown_hbm, vec_hbm, bias_hbm,
    bo_hbm, gi_hbm, ga_hbm, gup_hbm, gdown_hbm,
    frames_ref, pin_ref, pout_ref, pup_ref, pdown_ref, vec_ref, bias_ref, xs, cs, bos, qs, ks, vs, dq, dk, dv, dms, lse, dka, dva, counts, members, starts, win, wout, wup, wdown, ga_ref, gup_ref, gdown_ref, gdt, sums, bsum, sems, x_sems, gi_sems,
):
    rows, width = x_hbm.shape
    padded = xs.shape[0]
    steps = padded // TILE
    pairs = width // 128
    hidden_width = pup_hbm.shape[1]
    micro, packed = frames_hbm.shape

    piece = TILE * PROJECTED
    final = padded // piece - 1

    def by_piece(i, act, hbm, local, sems_, out=False):
        def at(start, size):
            ends = hbm.at[pl.ds(start, size)], local.at[pl.ds(start, size)]
            act(pltpu.make_async_copy(*(ends[::-1] if out else ends), sems_.at[i]))

        pl.when(i < final)(lambda: at(pl.multiple_of(i * piece, piece), piece))
        pl.when(i == final)(lambda: at(final * piece, rows - final * piece))

    begin, finish = lambda copy: copy.start(), lambda copy: copy.wait()
    loads = [
        pltpu.make_async_copy(src, dst, sems.at[k])
        for k, (src, dst) in enumerate(
            (
                (vec_hbm, vec_ref),
                (pin_hbm, pin_ref),
                (frames_hbm, frames_ref),
                (bias_hbm, bias_ref),
                (pout_hbm, pout_ref),
                (pup_hbm, pup_ref),
                (pdown_hbm, pdown_ref),
                (cot_hbm, cs.at[pl.ds(0, rows)]),
            )
        )
    ]
    for copy in loads[:2]:
        copy.start()
    for i in range(final + 1):
        by_piece(i, begin, x_hbm, xs, x_sems)
    for copy in loads[2:]:
        copy.start()

    gap = padded - rows
    if gap:
        xs[pl.ds(rows, gap)] = jnp.zeros((gap, width), bf16)
        cs[pl.ds(rows, gap)] = jnp.zeros((gap, width), f32)
        dq[pl.ds(rows, gap)] = jnp.zeros((gap, width), bf16)
    for ref in (qs, ks, vs, dms):
        ref[pl.ds(padded, SPAN)] = jnp.zeros((SPAN, width), bf16)
    for ref in (ga_ref, gup_ref, gdt, sums, bsum):
        ref[...] = jnp.zeros_like(ref)
    for copy in loads[:2]:
        copy.wait()
    win[...] = pin_ref[...].astype(bf16)

    gain_one, shift_one = vec_ref[3:4, :], vec_ref[4:5, :]
    gain_two, shift_two = vec_ref[5:6, :], vec_ref[6:7, :]

    def spot(i, g, group=GROUP):
        return pl.ds(pl.multiple_of((i * group + g) * TILE, TILE), TILE)

    def project(i, _):
        by_piece(i, finish, x_hbm, xs, x_sems)

        def even(g, _):
            n, _rstd = normalize(xs[spot(i, g, PROJECTED)].astype(f32))
            return (n * gain_one + shift_one).astype(bf16)

        def spread(g, h):
            return [dot(h, win[:, b * width : (b + 1) * width]) for b in range(3)]

        def keep(g, held):
            q, k, v = held
            at = spot(i, g, PROJECTED)
            qs[at] = (q + vec_ref[0:1, :]).astype(bf16) * jnp.array(0.125, bf16)
            ks[at] = k.astype(bf16)
            vs[at] = (v + vec_ref[1:2, :]).astype(bf16)

        stagger(list(range(PROJECTED)), (even, spread, keep), LAG_PROJECT)
        return 0

    lax.fori_loop(0, steps // PROJECTED, project, 0)

    for copy in loads[2:]:
        copy.wait()
    wout[...] = pout_ref[...].astype(bf16)
    wup[...] = pup_ref[...].astype(bf16)
    wdown[...] = pdown_ref[...].astype(bf16)

    first_head = lax.broadcasted_iota(jnp.int32, (1, 128), 1) < 64
    keep0 = first_head.astype(f32).astype(bf16)
    keep1 = 1.0 - keep0

    def depth(j):
        return min(QT * (j + 1) + REACH, SPAN)

    def filled(j):
        return min(-(-depth(j) // 128) * 128, SPAN)

    def limits(j, off, stop):
        t = QT * j + (lax.broadcasted_iota(jnp.int32, (1, 2 * QT), 1) & (QT - 1))
        frame = ((t - off) * 241) >> 12
        end = jnp.minimum(off + FRAME * (frame + 1), stop)
        return end, (t >= off) & (t < stop)

    def hide(score, j, off, end):
        m = score.shape[0]
        edge = QT * j
        row = lambda lo, hi: lo + lax.broadcasted_iota(jnp.int32, (hi - lo, 2 * QT), 0)
        if j == 0:
            s = row(0, m)
            return jnp.where((s >= off) & (s < end), score, -BIG)
        return jnp.concatenate(
            [
                jnp.where(row(0, LEAD) >= off, score[:LEAD], -BIG),
                score[LEAD:edge],
                jnp.where(row(edge, m) < end, score[edge:], -BIG),
            ],
            axis=0,
        )

    def heads_apart(block):
        return jnp.concatenate([block * keep0, block * keep1], axis=0)

    def fill(block, j):
        short = filled(j) - depth(j)
        if not short:
            return block
        return jnp.concatenate([block, jnp.zeros((short, block.shape[1]), block.dtype)], axis=0)

    def heads_back(out):
        both = jnp.concatenate([out[:64, :QT], out[64:, QT:]], axis=0)
        return both.T

    def put(ref, base, lanes, block, j, off, stop):
        at = pl.ds(pl.multiple_of(base + QT * j, LEAD), QT)
        own = lax.broadcasted_iota(jnp.int32, (QT, 128), 0)
        keep = own < stop - QT * j
        if j == 0:
            keep &= own >= off
        ref[at, lanes] = jnp.where(keep, block, ref[at, lanes].astype(f32)).astype(bf16)

    classes = SPAN // QT
    for c in range(classes):
        counts[c] = 0

    def sort(i, start):
        length = frames_ref[i // packed, i % packed] * FRAME
        tiles = ((start & (LEAD - 1)) + length + QT - 1) // QT - 1
        seat = counts[tiles]
        members[tiles, seat] = i
        counts[tiles] = seat + 1
        starts[i] = start
        return start + length

    lax.fori_loop(0, micro * packed, sort, 0)
    for c in range(classes - 1):
        odd = counts[c] & 1

        @pl.when(odd == 1)
        def _(c=c):
            members[c + 1, counts[c + 1]] = members[c, counts[c] - 1]
            counts[c + 1] = counts[c + 1] + 1

    def window(n, tiles):
        i = members[tiles - 1, n]
        start = starts[i]
        off = start & (LEAD - 1)
        stop = off + frames_ref[i // packed, i % packed] * FRAME
        return i, pl.multiple_of(start - off, LEAD), off, stop

    def units(tiles, n):
        windows = [window(SLOTS * n + slot, tiles) for slot in range(SLOTS)]
        for j in reversed(range(tiles)):
            for p in range(pairs):
                for slot in range(SLOTS):
                    yield slot, p, slice(128 * p, 128 * (p + 1)), j, windows[slot]

    def attend(tiles, n, _):
        todo, v_t = [], {}

        def compare(unit, _):
            _slot, _p, lanes, j, (_i, base, _off, _stop) = unit
            query = heads_apart(qs[pl.ds(pl.multiple_of(base + QT * j, LEAD), QT), lanes])
            return dot_nt(ks[pl.ds(base, depth(j)), lanes], query)

        def soften(unit, raw):
            slot, p, lanes, j, (i, base, off, stop) = unit
            end, valid = limits(j, off, stop)
            score = hide(raw, j, off, end)
            peak = jnp.max(score, axis=0, keepdims=True)
            weight = jnp.exp(score - peak)
            total = jnp.sum(weight, axis=0, keepdims=True)
            row = pairs * j + p
            lse[i, row : row + 1, :] = jnp.where(valid, peak + jnp.log(total), BIG)
            prob = (weight * jnp.where(valid, 1.0 / total, 0.0)).astype(bf16)
            if (slot, p) not in v_t:
                v_t[slot, p] = vs[pl.ds(base, filled(tiles - 1)), lanes].T
            return dot(v_t[slot, p][:, : filled(j)], fill(prob, j))

        def turn(unit, out):
            _slot, _p, lanes, j, (_i, base, off, stop) = unit
            todo.append((dq, base, lanes, heads_back(out), j, off, stop))

        stagger(list(units(tiles, n)), (compare, soften, turn), LAG)
        for entry in todo:
            put(*entry)
        return 0

    for tiles in range(1, classes + 1):
        lax.fori_loop(0, counts[tiles - 1] // SLOTS, functools.partial(attend, tiles), 0)

    ones = jnp.ones((16, TILE * GROUP), bf16)

    def join(blocks, axis):
        return jnp.concatenate(blocks, axis=axis)

    def feed_forward(i, _):
        state = []
        for g in range(GROUP):
            at = spot(i, g)
            mixed = dq[at]
            resid = xs[at].astype(f32) + dot(mixed, wout[...]) + vec_ref[2:3, :]
            n, rstd = normalize(resid)
            h = (n * gain_two + shift_two).astype(bf16)
            state.append((at, mixed, resid, n, rstd, h, cs[at].astype(bf16)))
        h_t = jnp.concatenate([join([e[5].T for e in state], 1), ones], axis=0)
        low_t = join([e[6].T for e in state], 1)
        feeds, d_hs, acts, d_pres = [None] * GROUP, [None] * GROUP, {}, {}

        def expand(unit, _):
            c, g = unit
            cols = slice(c, c + 256)
            return dot(state[g][5], wup[:, cols]), dot_nt(state[g][6], wdown[cols, :])

        def bend(unit, held):
            c, g = unit
            pre, d_act = held
            act, slope = gelu_parts(pre + bias_ref[:, c : c + 256])
            act = act.astype(bf16)
            d_pre = (d_act * slope).astype(bf16)
            acts[c, g], d_pres[c, g] = act, d_pre
            return act, d_pre

        def shrink(unit, held):
            c, g = unit
            act, d_pre = held
            cols = slice(c, c + 256)
            feed, d_h = dot(act, wdown[cols, :]), dot_nt(d_pre, wup[:, cols])
            feeds[g] = feed if feeds[g] is None else feeds[g] + feed
            d_hs[g] = d_h if d_hs[g] is None else d_hs[g] + d_h
            if g == GROUP - 1:
                act = join([acts.get((c, k)) for k in range(GROUP)], 0)
                d_pre = join([d_pres.get((c, k)) for k in range(GROUP)], 0)
                gdt[:, cols] += dot(low_t, act)
                both = dot(h_t, d_pre)
                gup_ref[:, cols] += both[:width]
                bsum[:, cols] += both[width : width + 8]

        stagger([(c, g) for c in range(0, hidden_width, 256) for g in range(GROUP)], (expand, bend, shrink), LAG_FEED)
        branches = []
        for g in range(GROUP):
            at, _mixed, resid, n, rstd, _h, _low = state[g]
            feed, d_h = feeds[g], d_hs[g]
            bos[at] = (resid + feed + vec_ref[7:8, :]).astype(bf16)
            d_resid = cs[at] + norm_back(d_h, gain_two, n, rstd)
            cs[at] = d_resid
            branch = d_resid.astype(bf16)
            branches.append(branch)
            sums[5] += fold8(d_h * n)
            sums[6] += fold8(d_h)
            dms[at] = dot_nt(branch, wout[...]).astype(bf16)
        mixed_t = jnp.concatenate([join([e[1].T for e in state], 1), ones], axis=0)
        both = dot(mixed_t, join(branches, 0))
        ga_ref[:, 3 * width : 4 * width] += both[:width]
        sums[2] += both[width : width + 8] * 0.125
        sums[7] += dot(ones, join([e[6] for e in state], 0))[:8] * 0.125
        return 0

    lax.fori_loop(0, steps // GROUP, feed_forward, 0)
    bo_out = pltpu.make_async_copy(bos.at[pl.ds(0, rows)], bo_hbm, sems.at[8])
    bo_out.start()
    for c in range(0, hidden_width, 256):
        gdown_ref[c : c + 256, :] = gdt[:, c : c + 256].T
    grads_out = [
        pltpu.make_async_copy(gup_ref, gup_hbm.at[pl.ds(0, width)], sems.at[9]),
        pltpu.make_async_copy(gdown_ref, gdown_hbm.at[pl.ds(0, hidden_width)], sems.at[10]),
    ]
    for copy in grads_out:
        copy.start()

    def attend_back(tiles, n, _):
        todo, k_t = [], {}

        def compare(unit, _):
            _slot, _p, lanes, j, (_i, base, _off, _stop) = unit
            here = pl.ds(pl.multiple_of(base + QT * j, LEAD), QT)
            query, d_out = heads_apart(qs[here, lanes]), heads_apart(dms[here, lanes])
            m = depth(j)
            return query, d_out, dot_nt(ks[pl.ds(base, m), lanes], query), dot_nt(vs[pl.ds(base, m), lanes], d_out)

        def soften(unit, held):
            slot, p, lanes, j, (i, base, off, stop) = unit
            query, d_out, raw, d_prob = held
            end, _valid = limits(j, off, stop)
            row = pairs * j + p
            prob = jnp.exp(hide(raw, j, off, end) - lse[i, row : row + 1, :])
            delta = jnp.sum(prob * d_prob, axis=0, keepdims=True)
            d_score = (prob * (d_prob - delta)).astype(bf16)
            if (slot, p) not in k_t:
                k_t[slot, p] = ks[pl.ds(base, filled(tiles - 1)), lanes].T
            out = dot(k_t[slot, p][:, : filled(j)], fill(d_score, j))
            return dot(prob.astype(bf16), d_out), dot(d_score, query), out

        def collect(unit, held):
            slot, _p, lanes, j, (_i, base, off, stop) = unit
            d_val, d_key, out = held
            m = depth(j)
            first = j == tiles - 1
            dva[slot, :m, lanes] = d_val if first else dva[slot, :m, lanes] + d_val
            dka[slot, :m, lanes] = d_key if first else dka[slot, :m, lanes] + d_key
            todo.append((dq, base, lanes, heads_back(out) * 0.125, j, off, stop))

        stagger(list(units(tiles, n)), (compare, soften, collect), LAG_BACK)
        for entry in todo:
            put(*entry)
        for slot, p, lanes, j, (i, base, off, stop) in units(tiles, n):
            at = slice(QT * j, QT * (j + 1))
            put(dv, base, lanes, dva[slot, at, lanes], j, off, stop)
            put(dk, base, lanes, dka[slot, at, lanes], j, off, stop)
        return 0

    for tiles in range(1, classes + 1):
        lax.fori_loop(0, counts[tiles - 1] // SLOTS, functools.partial(attend_back, tiles), 0)
    if gap:
        for ref in (dq, dk, dv):
            ref[pl.ds(rows, gap)] = jnp.zeros((gap, width), bf16)

    def project_back(i, _):
        turned, blocks = {}, {}

        def even(g, _):
            n, rstd = normalize(xs[spot(i, g, PROJECTED)].astype(f32))
            turned[g] = (n * gain_one + shift_one).astype(bf16).T
            return n, rstd

        def spread(g, held):
            d_h = None
            for b, ref in enumerate((dq, dk, dv)):
                block = ref[spot(i, g, PROJECTED)]
                blocks[b, g] = block
                part = dot_nt(block, win[:, b * width : (b + 1) * width])
                d_h = part if d_h is None else d_h + part
            return *held, d_h

        def keep(g, held):
            n, rstd, d_h = held
            sums[3] += fold8(d_h * n)
            sums[4] += fold8(d_h)
            at = spot(i, g, PROJECTED)
            cs[at] = cs[at] + norm_back(d_h, gain_one, n, rstd)
            if g == PROJECTED - 1:
                h_t = jnp.concatenate([join([turned[k] for k in range(PROJECTED)], 1), jnp.ones((16, TILE * PROJECTED), bf16)], axis=0)
                for b in range(3):
                    both = dot(h_t, join([blocks[b, k] for k in range(PROJECTED)], 0))
                    ga_ref[:, b * width : (b + 1) * width] += both[:width]
                    if b != 1:
                        sums[b // 2] += both[width : width + 8] * 0.125

        stagger(list(range(PROJECTED)), (even, spread, keep), LAG_PROJECT)
        by_piece(i, begin, gi_hbm, cs, gi_sems, out=True)
        return 0

    lax.fori_loop(0, steps // PROJECTED, project_back, 0)
    vec = jnp.sum(sums[...], axis=1)
    tail = 4 * width
    for b in range(width // 128):
        ga_ref[8 * b : 8 * b + 8, tail : tail + 128] = vec[:, 128 * b : 128 * (b + 1)]
    bias = bsum[0:1, :]
    for b in range(hidden_width // 128):
        row = 8 * (width // 128) + b
        ga_ref[row : row + 1, tail : tail + 128] = bias[:, 128 * b : 128 * (b + 1)]
    grads_out.append(pltpu.make_async_copy(ga_ref, ga_hbm.at[pl.ds(0, width)], sems.at[11]))
    grads_out[-1].start()
    for copy in (bo_out, *grads_out):
        copy.wait()
    for i in range(final + 1):
        by_piece(i, finish, gi_hbm, cs, gi_sems, out=True)


def local_grads(spare, inputs, frames, cotangent, proj_in, proj_out, ffn_up, ffn_down, vectors, ffn_bias):
    rows, width = inputs.shape
    hidden_width = ffn_up.shape[1]
    step = TILE * max(GROUP, PROJECTED)
    padded = -(-rows // step) * step
    wide = padded + SPAN
    pairs = width // 128
    hbm = pl.BlockSpec(memory_space=pltpu.HBM)
    bias = ffn_bias.reshape(1, hidden_width)
    return pl.pallas_call(
        local_kernel,
        out_shape=(
            jax.ShapeDtypeStruct((rows, width), bf16),
            jax.ShapeDtypeStruct((rows, width), f32),
            jax.ShapeDtypeStruct((spare * width, 4 * width + 128), f32),
            jax.ShapeDtypeStruct((spare * width, hidden_width), f32),
            jax.ShapeDtypeStruct((spare * hidden_width, width), f32),
        ),
        in_specs=[hbm] * 9,
        out_specs=(hbm,) * 5,
        scratch_shapes=[
            pltpu.SMEM(frames.shape, jnp.int32),
            *[pltpu.VMEM(a.shape, f32) for a in (proj_in, proj_out, ffn_up, ffn_down, vectors, bias)],
            pltpu.VMEM((padded, width), bf16),
            pltpu.VMEM((padded, width), f32),
            pltpu.VMEM((padded, width), bf16),
            *[pltpu.VMEM((wide, width), bf16)] * 7,
            pltpu.VMEM((frames.size, 8, 2 * QT), f32),
            pltpu.VMEM((2, SPAN, width), f32),
            pltpu.VMEM((2, SPAN, width), f32),
            pltpu.SMEM((SPAN // QT,), jnp.int32),
            pltpu.SMEM((SPAN // QT, frames.size + 1), jnp.int32),
            pltpu.SMEM((frames.size,), jnp.int32),
            pltpu.VMEM((width, 3 * width), bf16),
            pltpu.VMEM((width, width), bf16),
            pltpu.VMEM((width, hidden_width), bf16),
            pltpu.VMEM((hidden_width, width), bf16),
            pltpu.VMEM((width, 4 * width + 128), f32),
            pltpu.VMEM((width, hidden_width), f32),
            pltpu.VMEM((hidden_width, width), f32),
            pltpu.VMEM((width, hidden_width), f32),
            pltpu.VMEM((8, 8, width), f32),
            pltpu.VMEM((8, hidden_width), f32),
            pltpu.SemaphoreType.DMA((12,)),
            *[pltpu.SemaphoreType.DMA((padded // (TILE * PROJECTED),))] * 2,
        ],
        compiler_params=pltpu.CompilerParams(vmem_limit_bytes=60 * 1024 * 1024),
        name="local_grads",
    )(frames, inputs, cotangent, proj_in, proj_out, ffn_up, ffn_down, vectors, bias)


def over_all(x):
    return jnp.sum(jnp.sum(x, axis=0, keepdims=True), axis=1, keepdims=True)


def momenta(first, second, grad):
    return BETA * first + (1.0 - BETA) * grad, BETA * second + (1.0 - BETA) * grad * grad


def direction(momentum, variance):
    fix = 1.0 - BETA**STEP
    return momentum / fix / (jnp.sqrt(variance / fix) + EPS_ADAM)


def places(order):
    top = len(order) - 1

    def chunk_of(pos):
        return sum((pos // (1 << (top - k))) % 2 * (1 << b) for k, b in enumerate(order))

    def place_of(chunk):
        return sum((chunk // (1 << b)) % 2 * (1 << (top - k)) for k, b in enumerate(order))

    return chunk_of, place_of


def each(count, body, block=32):
    block = min(count, block)
    if count == block:
        for i in range(count):
            body(i)
        return

    def some(outer, _):
        for i in range(block):
            body(outer * block + i)
        return 0

    lax.fori_loop(0, count // block, some, 0)


def cut_pieces(shapes):
    wide, tall = shapes[1][2] // 2, shapes[2][1] // 2
    return (
        (0, slice(0, shapes[0][1]), slice(0, 640)),
        (0, slice(0, shapes[0][1]), slice(640, shapes[0][2])),
        (1, slice(0, shapes[1][1]), slice(0, wide)),
        (1, slice(0, shapes[1][1]), slice(wide, 2 * wide)),
        (2, slice(0, tall), slice(0, shapes[2][2])),
        (2, slice(tall, 2 * tall), slice(0, shapes[2][2])),
    )


def cut_matrices(shapes):
    (_, r_in, w_in), (_, _, w_out), (_, r_up, w_up), (_, r_down, w_down) = shapes
    rest = w_in - 640
    return (
        (0, 0, r_in, 0, 640, 0, 0),
        (0, 0, r_in, 640, rest, 1, 0),
        (1, 0, r_in, 0, w_out, 1, rest),
        (2, 0, r_up, 0, w_up // 2, 2, 0),
        (2, 0, r_up, w_up // 2, w_up // 2, 3, 0),
        (3, 0, r_down // 2, 0, w_down, 4, 0),
        (3, r_down // 2, r_down // 2, 0, w_down, 5, 0),
    )


def flat_rows(first, rows, blocks, b):
    return pl.ds(first * blocks + b, rows, stride=blocks)


def exchange_kernel(n, walks, *refs):
    count, stages = len(walks), len(walks[0])
    grads, owns, firsts, seconds = refs[:3], refs[3:7], refs[7:11], refs[11:15]
    full, shares = refs[15 : 15 + count], refs[15 + count : 15 + 2 * count]
    parcels, landed = refs[15 + 2 * count : 15 + 3 * count], refs[15 + 3 * count : 15 + 4 * count]
    sources, (send_sems, recv_sems, load_sems) = refs[15 + 4 * count : 18 + 4 * count], refs[18 + 4 * count :]
    pieces = cut_pieces([s.shape for s in sources])
    orders = [[b for bits in walk for b in bits] for walk in walks]
    me = lax.axis_index("dp")

    def bit(k):
        return (me // (1 << k)) % 2

    def flips(bits):
        return [[b for j, b in enumerate(bits) if t >> j & 1] for t in range(1, 1 << len(bits))]

    def other(flip):
        return me + sum((1 - 2 * bit(b)) * (1 << b) for b in flip)

    def digit(bits, flip=()):
        top = len(bits) - 1
        return sum((1 - bit(b) if b in flip else bit(b)) * (1 << (top - j)) for j, b in enumerate(bits))

    def left(p, k):
        return n >> sum(len(bits) for bits in walks[p][: k + 1])

    def slot(p, k):
        return n - left(p, k - 1) if k else 0

    quarters = [pl.ds(q * n // 4, n // 4) for q in range(4)]
    loads = [
        [pltpu.make_async_copy(grad.at[at], source.at[at], load_sems.at[k, q]) for q, at in enumerate(quarters)]
        for k, (grad, source) in enumerate(zip(grads, sources))
    ]
    for copy in (copy for group in loads for copy in group):
        copy.start()
    barrier = pltpu.get_barrier_semaphore()
    met = sorted({tuple(sorted(flip)) for walk in walks for bits in walk for flip in flips(bits)})
    for flip in met:
        pl.semaphore_signal(barrier, inc=1, device_id=(other(flip),), device_id_type=pl.DeviceIdType.MESH)
    pl.semaphore_wait(barrier, len(met))

    sent, used = [], [0] * count

    def remote(p, src, dst, flip):
        copy = pltpu.make_async_remote_copy(
            src_ref=src,
            dst_ref=dst,
            send_sem=send_sems.at[p, used[p]],
            recv_sem=recv_sems.at[p, used[p]],
            device_id=(other(flip),),
            device_id_type=pl.DeviceIdType.MESH,
        )
        used[p] += 1
        copy.start()
        sent.append(copy)
        return copy

    def chunk_of(p, i, first):
        return places(orders[p][1:])[0](i) + first * (1 << orders[p][0])

    arriving = {}

    def split(p, k):
        m, bits = left(p, k), walks[p][k]
        copies = []
        for t, flip in enumerate(flips(bits)):
            if k == 0:
                source, rows, lanes = pieces[p]

                def pack(i):
                    parcels[p][i] = sources[source][chunk_of(p, i, 1 - bit(bits[0])), rows, lanes]

                each(m, pack)
                src = parcels[p]
            else:
                src = landed[p].at[pl.ds(slot(p, k - 1) + digit(bits, flip) * m, m)]
            copies.append(remote(p, src, landed[p].at[pl.ds(slot(p, k) + t * m, m)], flip))
        arriving[p, k] = copies

    def add(p, k):
        m, bits = left(p, k), walks[p][k]
        for copy in arriving[p, k]:
            copy.wait_recv()
        new = pl.ds(slot(p, k), m)
        if k:
            total = landed[p][pl.ds(slot(p, k - 1) + digit(bits) * m, m)]
            for t in range(len(arriving[p, k])):
                total = total + landed[p][pl.ds(slot(p, k) + t * m, m)]
            landed[p][new] = total
            return
        source, rows, lanes = pieces[p]

        def one(i):
            landed[p][i] = landed[p][i] + sources[source][chunk_of(p, i, bit(bits[0])), rows, lanes]

        each(m, one)

    parts = range(count)
    for p in parts:
        if pieces[p][0] not in [source for source, _, _ in pieces[:p]]:
            for copy in loads[pieces[p][0]]:
                copy.wait()
        split(p, 0)
    for k in range(1, stages):
        for p in parts:
            add(p, k - 1)
            split(p, k)

    homes = [places(order)[1](me) for order in orders]
    matrices = cut_matrices([own.shape for own in owns])

    def gather(p, k):
        m = left(p, k)
        at = pl.ds(homes[p] // m * m, m)
        arriving[p, stages + k] = [
            remote(p, full[p].at[at], full[p].at[at], flip) for flip in flips(walks[p][k])
        ]

    last = stages - 1
    for p in parts:
        add(p, last)
        share = slot(p, last)
        for i, row, rows, lane, lanes, piece, start in matrices:
            if piece != p:
                continue
            blocks = owns[i].shape[2] // 128
            for b in range(lanes // 128):
                flat = flat_rows(row, rows, blocks, lane // 128 + b)
                here = slice(start + 128 * b, start + 128 * (b + 1))
                own = owns[i][me, row : row + rows, lane + 128 * b : lane + 128 * (b + 1)]
                momentum, variance = momenta(firsts[i][flat, :], seconds[i][flat, :], landed[p][share, :, here])
                full[p][homes[p], :, here] = direction(momentum, variance) + DECAY * own
        if p == 1:
            tail = slice(full[1].shape[2] - 128, full[1].shape[2])
            full[1][homes[1], :, tail] = landed[1][share, :, tail]
        shares[p][...] = landed[p][share]
        gather(p, last)
    for k in range(last - 1, -1, -1):
        for p in parts:
            for copy in arriving[p, stages + k + 1]:
                copy.wait_recv()
            gather(p, k)
    for p in parts:
        for copy in arriving[p, stages]:
            copy.wait_recv()
    for copy in sent:
        copy.wait_send()


def renew_kernel(n, orders, *refs):
    count = len(orders)
    full, shares, refs = refs[:count], refs[count : 2 * count], refs[2 * count :]
    weights, firsts, seconds = refs[:4], refs[4:8], refs[8:12]
    vec, bias, fvec, svec, fbias, sbias = refs[12:18]
    g_out, m_out, v_out = refs[18:22], refs[22:26], refs[26:30]
    w_out, low_out = refs[30:34], refs[34:38]
    gvec, gbias, mvec, vvec, wvec, mbias, vbias, wbias, norms = refs[38:47]
    rows24, w_new, w_low, sems = refs[47], refs[48:52], refs[52:56], refs[56]
    matrices = cut_matrices([w.shape for w in weights])
    for i, row, rows, lane, lanes, piece, start in matrices:
        blocks = weights[i].shape[2] // 128
        for b in range(lanes // 128):
            flat = flat_rows(row, rows, blocks, lane // 128 + b)
            g = shares[piece][:, start + 128 * b : start + 128 * (b + 1)]
            g_out[i][flat, :] = g
            m_out[i][flat, :], v_out[i][flat, :] = momenta(firsts[i][flat, :], seconds[i][flat, :], g)
    leaving = []
    for i in (2, 3, 0, 1):
        _, rows, columns = weights[i].shape
        own = [entry for entry in matrices if entry[0] == i]
        total = 0.0
        for _i, _row, _rows, _lane, lanes, piece, start in own:
            step = full[piece][:, :, start : start + lanes]
            total = total + over_all(jnp.sum(step * step, axis=0))
        u_norm = jnp.sqrt(total)
        old = weights[i][...]
        w_norm = jnp.sqrt(over_all(jnp.sum(old * old, axis=0)))
        norms[0:1, i : i + 1] = w_norm
        norms[1:2, i : i + 1] = u_norm
        ratio = RATE * (w_norm / (u_norm + EPS_ADAM))

        def renew(chunk, own=own, ratio=ratio, i=i):
            for _i, row, rows, lane, lanes, piece, start in own:
                at, to = slice(row, row + rows), slice(lane, lane + lanes)
                step = full[piece][places(orders[piece])[1](chunk), :, start : start + lanes]
                w_new[i][chunk, at, to] = weights[i][chunk, at, to] - ratio * step

        each(n, renew)
        if rows % 8 == 0:
            w_low[i][...] = w_new[i][...].reshape(n * rows, columns).astype(bf16)
        else:
            w_low[i][...] = jnp.zeros_like(w_low[i])
        for k, (src, dst) in enumerate(((w_new[i], w_out[i]), (w_low[i], low_out[i]))):
            part = src.shape[0] // 4
            for q in range(4):
                at = pl.ds(q * part, part)
                leaving.append(pltpu.make_async_copy(src.at[at], dst.at[at], sems.at[2 * i + k, q]))
                leaving[-1].start()

    rows = full[1].shape[1]
    tail = full[1].shape[2] - 128
    for chunk in range(rows24.shape[0] // rows):
        rows24[chunk * rows : (chunk + 1) * rows, :] = full[1][places(orders[1])[1](chunk), :, tail:]

    def plain(weight, grad, first, second):
        momentum, variance = momenta(first, second, grad)
        return momentum, variance, weight - RATE_VEC * direction(momentum, variance)

    grad = jnp.concatenate([rows24[0:8, :], rows24[8:16, :]], axis=1)
    gvec[...] = grad
    mvec[...], vvec[...], wvec[...] = plain(vec[...], grad, fvec[...], svec[...])
    grad = rows24[16:24, :]
    gbias[...] = grad
    mbias[...], vbias[...], wbias[...] = plain(bias[...], grad, fbias[...], sbias[...])
    for copy in leaving:
        copy.wait()


def exchange(n, spare, grads, weights, vectors, ffn_bias, firsts, seconds, others):
    far = list(range(1, n.bit_length() - 1))
    axes = [far[len(far) * p // 3 : len(far) * (p + 1) // 3] for p in range(3)]
    x, y, z = ([(b,) for b in axis] for axis in axes)
    walks = tuple(
        ((0,), *a, *b, *c) for a, b, c in ((x, y, z), (y, z, x), (z, x, y), (x, z, y), (y, x, z), (z, y, x))
    )
    if len(far) == 4:
        sets = ("xyab", "yxba", "ayxb", "xayb", "ybxa", "bxya")
        walks = tuple(((0,), *((far["xyab".index(c)],) for c in order)) for order in sets)
    orders = tuple(tuple(b for bits in walk for b in bits) for walk in walks)
    copies = 2 * sum((1 << len(bits)) - 1 for bits in walks[0])
    cut = lambda a: a.reshape(n, a.shape[0] // n, a.shape[1])
    blocks = list(map(cut, weights))
    chunks = [(g.shape[0] // (n * spare), g.shape[1]) for g in grads]
    sources = [g.reshape(n * spare, *chunk) for g, chunk in zip(grads, chunks)]
    held = [(n, *chunk) for chunk in chunks]
    flat = lambda a: a.reshape(-1, 128)
    vmem = pl.BlockSpec(memory_space=pltpu.VMEM)
    like = lambda a, dtype=f32: jax.ShapeDtypeStruct(a.shape, dtype)
    firsts, seconds = list(map(flat, firsts)), list(map(flat, seconds))
    operands = [*sources, *blocks, *firsts, *seconds]
    sizes = [
        (rows.stop - rows.start, lanes.stop - lanes.start) for _, rows, lanes in cut_pieces(held)
    ]
    shapes = [jax.ShapeDtypeStruct((n, *s), f32) for s in sizes] + [jax.ShapeDtypeStruct(s, f32) for s in sizes]
    reduced = pl.pallas_call(
        functools.partial(exchange_kernel, n, walks),
        out_shape=shapes,
        in_specs=[pl.BlockSpec(memory_space=pl.ANY)] * 3 + [vmem] * 12,
        out_specs=[vmem] * len(shapes),
        scratch_shapes=[
            *[pltpu.VMEM((n // 2, *s), f32) for s in sizes],
            *[pltpu.VMEM((n, *s), f32) for s in sizes],
            *[pltpu.VMEM(shape, f32) for shape in held],
            pltpu.SemaphoreType.DMA((len(sizes), copies)),
            pltpu.SemaphoreType.DMA((len(sizes), copies)),
            pltpu.SemaphoreType.DMA((3, 4)),
        ],
        compiler_params=pltpu.CompilerParams(
            collective_id=0, has_side_effects=True, vmem_limit_bytes=44 * 1024 * 1024
        ),
        name="exchange",
    )(*operands)
    line_bias = flat(ffn_bias)
    operands = [
        *reduced, *blocks, *firsts, *seconds, vectors, line_bias, others[0], others[1], flat(others[2]), flat(others[3]),
    ]
    moments = list(map(like, firsts))
    shapes = [
        *moments, *moments, *moments, *map(like, blocks), *[like(w, bf16) for w in weights],
        like(vectors), like(line_bias), *[like(vectors)] * 3, *[like(line_bias)] * 3, jax.ShapeDtypeStruct((2, 4), f32),
    ]
    results = pl.pallas_call(
        functools.partial(renew_kernel, n, orders),
        out_shape=shapes,
        in_specs=[vmem] * len(operands),
        out_specs=[vmem] * 12 + [pl.BlockSpec(memory_space=pl.ANY)] * 8 + [vmem] * 9,
        scratch_shapes=[
            pltpu.VMEM((24, 128), f32),
            *[pltpu.VMEM(b.shape, f32) for b in blocks],
            *[pltpu.VMEM(w.shape, bf16) for w in weights],
            pltpu.SemaphoreType.DMA((8, 4)),
        ],
        compiler_params=pltpu.CompilerParams(vmem_limit_bytes=32 * 1024 * 1024),
        name="renew",
    )(*operands)
    g, m, v = ([a.reshape(-1) for a in results[4 * i : 4 * i + 4]] for i in range(3))
    w = [new.reshape(old.shape) for new, old in zip(results[12:16], weights)]
    low = [new.astype(bf16) if block.shape[1] % 8 else own for new, own, block in zip(w, results[16:20], blocks)]
    gvec, gbias, mvec, vvec, wvec, mbias, vbias, wbias, norms = results[20:]
    line = lambda a: a.reshape(-1)
    steps = [entry for i in range(4) for entry in (m[i], v[i], w[i], low[i])]
    return (*g, gvec, line(gbias), *steps, mvec, vvec, wvec, line(mbias), line(vbias), line(wbias), norms.T)


def on_device(n, inputs, frames, cotangent, *rest):
    proj_in, proj_out, ffn_up, ffn_down, vectors, ffn_bias = rest[:6]
    moments, others = rest[6:14], rest[14:]
    spare = 24 if proj_in.shape[0] % (8 * n) == 0 else 1
    block_out, grad_inputs, *grads = local_grads(
        spare, inputs, frames, cotangent, proj_in, proj_out, ffn_up, ffn_down, vectors, ffn_bias
    )
    weights = (proj_in, proj_out, ffn_up, ffn_down)
    return (
        block_out,
        grad_inputs,
        *exchange(n, spare, grads, weights, vectors, ffn_bias, moments[0::2], moments[1::2], others),
    )


def solution(mesh):
    split, rows, copied = P("dp"), P("dp", None), P()
    step = (split, split, copied, copied)
    return jax.shard_map(
        functools.partial(on_device, mesh.shape["dp"]),
        mesh=mesh,
        in_specs=(rows, rows, rows, *[copied] * 6, *[split] * 8, *[copied] * 4),
        out_specs=(rows, rows, *[split] * 4, copied, copied, *step * 4, *[copied] * 7),
        check_vma=False,
    )
```
